32 devices in a mesh: fsdp: 16 (over z, y, core), tp: 2 (over x).
Axes of the slice: x: 2, y: 2, z: 4, core: 2. Of those that a mesh axis runs over, the one named last changes fastest.
Arguments:
- momentum: float32 [1536, 27648], P('fsdp', 'tp'), may hold values from -1800 to 1800
- gradient: bfloat16 [1536, 27648], P('fsdp', 'tp'), may hold values from -1800 to 1800
- basis: bfloat16 [27648, 256], P('tp'), may hold values from -0.0390625 to 0.0390625
Outputs:
- new_momentum: float32 [1536, 27648], P('fsdp', 'tp')
- new_basis: bfloat16 [27648, 256], P('tp')
- update: bfloat16 [1536, 27648], P('fsdp', 'tp')
The draws below stay inside these ranges and needn't reach their ends.
All inputs are finite; a program needn't handle non-finite values.
Results may differ from the reference program's by a relative error of at most 0.0083.
Values may be sent and summed in bfloat16 or wider, within the bound.
No kernel may reach another device: no remote copies, remote signals or barrier semaphores. Data moves between devices by JAX's collectives and lax.ppermute only.
A program may use at most 128 MiB of HBM per device.

```python
import math
import jax
import jax.numpy as jnp
from jax import lax

N = 27648
RANK = 256
M = 1536


def shared_scales(key, rise):
    row_key, col_key = jax.random.split(key)
    row_scale = jnp.exp(jax.random.uniform(row_key, (M, 1), jnp.float32, 0.0, math.log(10.0)))
    col_scale = jnp.exp(jax.random.uniform(col_key, (1, N), jnp.float32, 0.0, math.log(10.0)))
    trend = jnp.exp(math.log(rise) * jnp.arange(N, dtype=jnp.float32) / N)
    return row_scale * col_scale * trend[None, :]


def draw_momentum(key, part):
    scales = shared_scales(key, 3.0)
    key = jax.random.fold_in(key, 11)
    noise = jnp.clip(jax.random.normal(key, (M, N), jnp.float32), -4.0, 4.0)
    return (0.5 * noise * scales).astype(jnp.float32)


def draw_gradient(key, part):
    scales = shared_scales(key, 3.0)
    key = jax.random.fold_in(key, 12)
    noise = jnp.clip(jax.random.normal(key, (M, N), jnp.float32), -4.0, 4.0)
    return (0.3 * noise * scales).astype(jnp.bfloat16)


def block_levels(stream_key, shape, cuts, least, top_value):
    factor_of, own = 1.0, jax.random.fold_in(stream_key, 6)
    for position, shards_of in cuts:
        steps = jnp.exp(jax.random.uniform(jax.random.fold_in(own, position), (shards_of,), jnp.float32, least / len(cuts), top_value / len(cuts)))
        factor_of = factor_of * jnp.repeat(steps, shape[position] // shards_of).reshape([-1 if axis == position else 1 for axis in range(len(shape))])
    return factor_of


def centred(stream_key, extent, scale, bound, cuts=(), held_as=jnp.bfloat16):
    result = jax.random.normal(stream_key, extent, jnp.float32) * scale
    if len(cuts) > 0:
        result = block_levels(stream_key, extent, cuts, -0.22, 0.18) * result
    return jnp.clip(result, min=-bound, max=bound).astype(held_as)


def setup_inputs(seed: int = 0) -> dict:
    key_list = jax.random.split(jax.random.key(seed), 4)
    return {
        "momentum": draw_momentum(jax.random.fold_in(key_list[3], 71), 0),
        "gradient": draw_gradient(jax.random.fold_in(key_list[3], 71), 0),
        "basis": centred(key_list[2], (N, RANK), N ** -0.5, 0.0390625, ((0, 2),)),
    }


def reference(momentum, gradient, basis):
    base = momentum + gradient.astype(jnp.float32)
    base_b = base.astype(jnp.bfloat16)
    sketch = jnp.dot(base_b.astype(jnp.float32), basis.astype(jnp.float32), preferred_element_type=jnp.float32)
    gram = jnp.dot(sketch.T, sketch, precision=lax.Precision.HIGHEST)
    lower = jnp.linalg.cholesky(gram)
    ortho = lax.linalg.triangular_solve(lower, sketch, left_side=False, lower=True, transpose_a=True).astype(jnp.bfloat16)
    back = lax.dot_general(base_b.astype(jnp.float32), ortho.astype(jnp.float32), (((0,), (0,)), ((), ())), preferred_element_type=jnp.float32).astype(jnp.bfloat16)
    back_f = back.astype(jnp.float32)
    colsq = lax.optimization_barrier(jnp.sum(back_f * back_f, axis=0))
    new_basis = (back_f * lax.rsqrt(colsq + 1e-06)).astype(jnp.bfloat16)
    new_momentum = base - 0.05 * jnp.dot(ortho.astype(jnp.float32), back.T.astype(jnp.float32), preferred_element_type=jnp.float32)
    factor = math.sqrt(M * N / RANK)
    update = (factor * jnp.dot(ortho.astype(jnp.float32), new_basis.T.astype(jnp.float32), preferred_element_type=jnp.float32)).astype(jnp.bfloat16)
    return (new_momentum, new_basis, update)
```

```python
import math

import jax
import jax.numpy as jnp
from jax import lax
from jax.sharding import PartitionSpec as P

LANES = 128


def orthonormal(sketch, gram):
    lower = jnp.linalg.cholesky(gram)
    return lax.linalg.triangular_solve(
        lower, sketch, left_side=False, lower=True, transpose_a=True
    ).astype(jnp.bfloat16)


def local(momentum, gradient, basis):
    rows_here, cols_here = momentum.shape
    rank_cols = basis.shape[1]
    fsdp_count = lax.axis_size("fsdp")
    tp_count = lax.axis_size("tp")
    share = -(-cols_here // (fsdp_count * LANES)) * LANES
    base = momentum + gradient.astype(jnp.float32)
    base_b = base.astype(jnp.bfloat16)

    padded = jnp.pad(base_b, ((0, 0), (0, share * fsdp_count - cols_here)))
    outgoing = jnp.swapaxes(padded.reshape(rows_here, fsdp_count, share), 0, 1)
    columns = lax.all_to_all(outgoing, "fsdp", 0, 0, tiled=True)
    columns = columns.reshape(rows_here * fsdp_count, share)

    sketch = jnp.dot(base_b, basis, preferred_element_type=jnp.float32)
    if tp_count == 2:
        sketch = sketch + lax.ppermute(sketch, "tp", [(0, 1), (1, 0)])
    else:
        sketch = lax.psum(sketch, "tp")
    whole = lax.all_gather(sketch, "fsdp", axis=0, tiled=True)
    gram = jnp.dot(whole.T, whole, precision=lax.Precision.HIGHEST)
    ortho = orthonormal(whole, gram)
    ortho_here = lax.dynamic_slice_in_dim(
        ortho, lax.axis_index("fsdp") * rows_here, rows_here, axis=0
    )
    back_share = lax.dot_general(
        columns, ortho, (((0,), (0,)), ((), ())), preferred_element_type=jnp.float32
    ).astype(jnp.bfloat16)
    share_f = back_share.astype(jnp.float32)
    colsq = lax.psum(jnp.sum(share_f * share_f, axis=0), ("fsdp", "tp"))
    back = lax.all_gather(back_share, "fsdp", axis=0, tiled=True)[:cols_here]
    back_f = back.astype(jnp.float32)
    new_basis = (back_f * lax.rsqrt(colsq + 1e-06)).astype(jnp.bfloat16)
    new_momentum = base - 0.05 * jnp.dot(ortho_here, back.T, preferred_element_type=jnp.float32)
    total_rows = rows_here * fsdp_count
    total_cols = cols_here * tp_count
    factor = math.sqrt(total_rows * total_cols / rank_cols)
    update = (factor * jnp.dot(ortho_here, new_basis.T, preferred_element_type=jnp.float32)).astype(
        jnp.bfloat16
    )
    return (new_momentum, new_basis, update)


def solution(mesh):
    return jax.shard_map(
        local,
        mesh=mesh,
        in_specs=(P("fsdp", "tp"), P("fsdp", "tp"), P("tp", None)),
        out_specs=(P("fsdp", "tp"), P("tp", None), P("fsdp", "tp")),
        check_vma=False,
    )
```

```python
import functools
import math

import jax
import jax.numpy as jnp
from jax import lax
from jax.experimental import pallas as pl
from jax.experimental.pallas import tpu as pltpu
from jax.sharding import PartitionSpec as P

LANES = 128
SUBLANES = 8
PANEL = 64
LONGEST_RING = 32
VMEM_LIMIT = 48 * 1024 * 1024
FULL = lax.Precision.HIGHEST
F32 = jnp.float32
BF16 = jnp.bfloat16


def cost(flops, nbytes):
    return pl.CostEstimate(flops=flops, bytes_accessed=nbytes, transcendentals=0)


def params():
    return pltpu.CompilerParams(vmem_limit_bytes=VMEM_LIMIT)


def sketch_kernel(cols, m_ref, g_ref, b_ref, out_ref, sketch_ref):
    step = pl.program_id(0)
    share = m_ref.shape[1]
    left = cols - step * share
    base_b = (m_ref[...] + g_ref[...].astype(F32)).astype(BF16)
    basis = b_ref[...]
    if cols % share:
        lane = lax.broadcasted_iota(jnp.int32, base_b.shape, 1)
        base_b = jnp.where(lane < left, base_b, jnp.zeros_like(base_b))
        row = lax.broadcasted_iota(jnp.int32, basis.shape, 0)
        basis = jnp.where(row < left, basis, jnp.zeros_like(basis))
    out_ref[0] = base_b
    term = jnp.dot(base_b, basis, preferred_element_type=F32)

    @pl.when(step == 0)
    def _():
        sketch_ref[...] = term

    @pl.when(step > 0)
    def _():
        sketch_ref[...] += term


def sketch_call(momentum, gradient, basis, share, count):
    rows, cols = momentum.shape
    rank = basis.shape[1]
    last = pl.cdiv(cols, share) - 1
    return pl.pallas_call(
        functools.partial(sketch_kernel, cols),
        grid=(count,),
        in_specs=[
            pl.BlockSpec((rows, share), lambda i: (0, jnp.minimum(i, last))),
            pl.BlockSpec((rows, share), lambda i: (0, jnp.minimum(i, last))),
            pl.BlockSpec((share, rank), lambda i: (jnp.minimum(i, last), 0)),
        ],
        out_specs=[
            pl.BlockSpec((1, rows, share), lambda i: (i, 0, 0)),
            pl.BlockSpec((rows, rank), lambda i: (0, 0)),
        ],
        out_shape=[
            jax.ShapeDtypeStruct((count, rows, share), BF16),
            jax.ShapeDtypeStruct((rows, rank), F32),
        ],
        compiler_params=params(),
        cost_estimate=cost(2 * rows * cols * rank, rows * cols * 8 + cols * rank * 2),
        name="sketch",
    )(momentum, gradient, basis)


def spread(x, lane):
    return jnp.broadcast_to(x[:, lane : lane + 1], (x.shape[0], LANES))


def row_of(x, row):
    return jnp.broadcast_to(x[row : row + 1, :], (SUBLANES, LANES))


def eliminate(block):
    sub = lax.broadcasted_iota(jnp.int32, (SUBLANES, LANES), 0)
    groups = PANEL // SUBLANES
    top = [block[SUBLANES * g : SUBLANES * (g + 1)] for g in range(groups)]
    for g in range(groups):
        first = PANEL + SUBLANES * g
        t = top[g]
        cols = [spread(t, first + j) for j in range(SUBLANES)]
        below = [[spread(top[i], first + j) for j in range(SUBLANES)] for i in range(g + 1, groups)]
        pivots = jnp.zeros((SUBLANES, LANES), F32)
        inverse, corner = [], {}
        for j in range(SUBLANES):
            pivot = row_of(cols[j], j)
            pivots = jnp.where(sub == j, pivot, pivots)
            inverse.append(1.0 / pivot)
            factor = jnp.where(sub > j, cols[j] * inverse[j], 0.0)
            t = t - factor * row_of(t, j)
            for k in range(j + 1, SUBLANES):
                corner[j, k] = row_of(cols[k], j)
                cols[k] = cols[k] - factor * corner[j, k]
        lines = [row_of(t, j) for j in range(SUBLANES)]
        for i in range(g + 1, groups):
            entries = below[i - g - 1]
            acc = top[i]
            for j in range(SUBLANES):
                factor = entries[j] * inverse[j]
                acc = acc - factor * lines[j]
                for k in range(j + 1, SUBLANES):
                    entries[k] = entries[k] - factor * corner[j, k]
            top[i] = acc
        top[g] = t * lax.rsqrt(pivots)
    return jnp.concatenate(top, axis=0)[:, :PANEL]


def dot(a, b, dims):
    return lax.dot_general(a, b, (dims, ((), ())), precision=FULL, preferred_element_type=F32)


def factor_kernel(count, ids_ref, *refs):
    pieces, (ortho_t_ref, here_ref, whole_ref, work_ref) = refs[:count], refs[count:]
    rows, rank = pieces[0].shape
    for n, piece in enumerate(pieces):
        whole_ref[pl.ds(pl.multiple_of(ids_ref[n] * rows, SUBLANES), rows), :] = piece[...]
    total = count * rows

    work_ref[:, :rank] = jnp.zeros((rank, rank), F32)
    chunk = 4 * rows

    @pl.loop(0, total // chunk)
    def _(n):
        part = whole_ref[pl.ds(pl.multiple_of(n * chunk, SUBLANES), chunk), :]
        work_ref[:, :rank] += dot(part, part, ((0,), (0,)))

    line = lax.broadcasted_iota(jnp.int32, (rank, rank), 0)
    column = lax.broadcasted_iota(jnp.int32, (rank, rank), 1)
    work_ref[:, rank:] = jnp.where(line == column, 1.0, 0.0).astype(F32)
    eye = jnp.where(line == column, 1.0, 0.0).astype(F32)[:PANEL, :PANEL]
    for start in range(0, rank, PANEL):
        stop = start + PANEL
        diagonal = work_ref[start:stop, start:stop]
        small = eliminate(jnp.concatenate([eye, diagonal], axis=1))
        panel = dot(small, work_ref[start:stop, :], ((1,), (0,)))
        work_ref[start:stop, :] = panel
        if stop < rank:
            work_ref[stop:, :] -= dot(panel[:, stop:rank], panel, ((0,), (0,)))
    inverse = work_ref[:, rank:]
    here_ref[...] = dot(pieces[0][...], inverse, ((1,), (1,))).astype(BF16)
    for n in range(0, total, chunk):
        ortho_t_ref[:, n : n + chunk] = dot(
            inverse, whole_ref[n : n + chunk, :], ((1,), (1,))
        ).astype(BF16)


def factor_call(ids, pieces):
    count = len(pieces)
    rows, rank = pieces[0].shape
    total = count * rows
    vmem = pl.BlockSpec(memory_space=pltpu.VMEM)
    return pl.pallas_call(
        functools.partial(factor_kernel, count),
        in_specs=[pl.BlockSpec(memory_space=pltpu.SMEM)] + [vmem] * count,
        out_specs=[vmem, vmem],
        out_shape=[
            jax.ShapeDtypeStruct((rank, total), BF16),
            jax.ShapeDtypeStruct((rows, rank), BF16),
        ],
        scratch_shapes=[pltpu.VMEM((total, rank), F32), pltpu.VMEM((rank, 2 * rank), F32)],
        compiler_params=params(),
        cost_estimate=cost(40 * total * rank * rank, total * rank * 6),
        name="factor",
    )(ids, *pieces)


def back_kernel(ortho_t_ref, columns_ref, back_ref, colsq_ref):
    back_t = jnp.dot(ortho_t_ref[...], columns_ref[...], preferred_element_type=F32)
    back = back_t.T.astype(BF16)
    back_ref[...] = back
    wide = back.astype(F32)
    colsq_ref[...] = jnp.sum(wide * wide, axis=0, keepdims=True)


def back_call(ortho_t, columns):
    rank, total = ortho_t.shape
    share = columns.shape[1]
    return pl.pallas_call(
        back_kernel,
        in_specs=[pl.BlockSpec(memory_space=pltpu.VMEM)] * 2,
        out_specs=[pl.BlockSpec(memory_space=pltpu.VMEM)] * 2,
        out_shape=[
            jax.ShapeDtypeStruct((share, rank), BF16),
            jax.ShapeDtypeStruct((1, rank), F32),
        ],
        compiler_params=params(),
        cost_estimate=cost(2 * rank * total * share, total * share * 2),
        name="back",
    )(ortho_t, columns)


def output_kernel(count, factor, carried, ids_ref, m_ref, g_ref, ortho_ref, colsq_ref, *refs):
    pieces, (nm_ref, nb_ref, up_ref) = refs[:count], refs[count + carried :]
    step = pl.program_id(0)
    scale = lax.rsqrt(colsq_ref[...] + 1e-06)
    ortho = ortho_ref[...]
    over = (((1,), (1,)), ((), ()))
    for n, piece in enumerate(pieces):

        @pl.when(step == n)
        def _():
            back = piece[...]
            unit = (back.astype(F32) * scale).astype(BF16)
            nb_ref[...] = unit
            base = m_ref[...] + g_ref[...].astype(F32)
            nm_ref[...] = base - 0.05 * lax.dot_general(
                ortho, back, over, preferred_element_type=F32
            )
            up_ref[...] = (
                factor * lax.dot_general(ortho, unit, over, preferred_element_type=F32)
            ).astype(BF16)


def output_call(ids, momentum, gradient, ortho, colsq, pieces, factor, previous):
    rows, cols = momentum.shape
    share, rank = pieces[0].shape
    count = len(pieces)
    wide = pl.BlockSpec((rows, share), lambda i, ids: (0, ids[i]))
    tall = pl.BlockSpec((share, rank), lambda i, ids: (ids[i], 0))
    carried = 3 if previous else 0
    aliases = {5 + count + n: n for n in range(carried)}
    return pl.pallas_call(
        functools.partial(output_kernel, count, factor, carried),
        grid_spec=pltpu.PrefetchScalarGridSpec(
            num_scalar_prefetch=1,
            grid=(count,),
            in_specs=[
                wide,
                wide,
                pl.BlockSpec((rows, rank), lambda i, ids: (0, 0)),
                pl.BlockSpec((1, rank), lambda i, ids: (0, 0)),
            ]
            + [pl.BlockSpec((share, rank), lambda i, ids: (0, 0))] * count
            + [pl.BlockSpec(memory_space=pl.ANY)] * carried,
            out_specs=[wide, tall, wide],
        ),
        out_shape=[
            jax.ShapeDtypeStruct((rows, cols), F32),
            jax.ShapeDtypeStruct((cols, rank), BF16),
            jax.ShapeDtypeStruct((rows, cols), BF16),
        ],
        input_output_aliases=aliases,
        compiler_params=params(),
        cost_estimate=cost(
            4 * rows * share * rank * count, count * share * (rows * 12 + rank * 4)
        ),
        name="outputs",
    )(ids, momentum, gradient, ortho, colsq, *pieces, *(previous or ()))


def chip_at(position, chips):
    half = chips // 2
    return jnp.where(position < half, 2 * position, 2 * (chips - 1 - position) + 1)


def position_of(chip, chips):
    return jnp.where(chip % 2 == 0, chip // 2, chips - 1 - chip // 2)


def ring_order(chips):
    half = chips // 2
    return [2 * q for q in range(half)] + [2 * (chips - 1 - q) + 1 for q in range(half, chips)]


def ring_steps(count, by_core):
    order = ring_order(count // 2)
    after = dict(zip(order, order[1:] + order[:1]))
    before = {b: a for a, b in after.items()}
    up = [(2 * c + k, 2 * after[c] + k) for c in order for k in (0, 1)]
    down = [(2 * c + k, 2 * before[c] + k) for c in order for k in (0, 1)]
    if not by_core:
        return up, down
    return [p for p in up if p[0] % 2 == 0] + [p for p in down if p[0] % 2 == 1]


def swap_pairs(count):
    return [(n, n ^ 1) for n in range(count)]


def gather_small(x, count):
    chips = count // 2
    me = lax.axis_index("fsdp")
    place, core = position_of(me // 2, chips), me % 2
    up, down = ring_steps(count, False)
    offsets, held = [0], [x]
    ahead = behind = x
    for step in range(1, chips // 2 + 1):
        ahead = lax.ppermute(ahead, "fsdp", up)
        held.append(ahead)
        offsets.append(-step)
        if 2 * step < chips:
            behind = lax.ppermute(behind, "fsdp", down)
            held.append(behind)
            offsets.append(step)
    other = [lax.ppermute(h, "fsdp", swap_pairs(count)) for h in held]
    chip = chip_at((place + jnp.array(offsets, jnp.int32)) % chips, chips)
    ids = jnp.concatenate([2 * chip + core, 2 * chip + 1 - core])
    return held + other, ids.astype(jnp.int32)


def total_of(x, fsdp_count, tp_count):
    if tp_count != 2 or fsdp_count & (fsdp_count - 1):
        return lax.psum(x, ("fsdp", "tp"))
    x = x + lax.ppermute(x, "tp", [(0, 1), (1, 0)])
    bit = 1
    while bit < fsdp_count:
        x = x + lax.ppermute(x, "fsdp", [(n, n ^ bit) for n in range(fsdp_count)])
        bit *= 2
    return x


def local(momentum, gradient, basis):
    rows, cols = momentum.shape
    rank = basis.shape[1]
    count = lax.axis_size("fsdp")
    tp_count = lax.axis_size("tp")
    chips = count // 2
    share = -(-cols // (count * LANES)) * LANES
    factor = math.sqrt(rows * count * cols * tp_count / rank)
    me = lax.axis_index("fsdp")
    ring = count % 4 == 0 and count <= LONGEST_RING and (count - 1) * share < cols

    outgoing, sketch = sketch_call(momentum, gradient, basis, share, count)
    columns = lax.all_to_all(outgoing, "fsdp", 0, 0, tiled=True)
    columns = columns.reshape(rows * count, share)
    if tp_count == 2:
        sketch = sketch + lax.ppermute(sketch, "tp", [(0, 1), (1, 0)])
    else:
        sketch = lax.psum(sketch, "tp")

    if ring:
        pieces, ids = gather_small(sketch, count)
    else:
        whole = lax.all_gather(sketch, "fsdp", axis=0)
        pieces = [lax.dynamic_index_in_dim(whole, (me + n) % count, 0, False) for n in range(count)]
        ids = ((me + jnp.arange(count)) % count).astype(jnp.int32)
    ortho_t, ortho_here = factor_call(ids, pieces)
    back, part = back_call(ortho_t, columns)
    colsq = total_of(part, count, tp_count)

    outputs = functools.partial(output_call, factor=factor)
    if not ring:
        whole = lax.all_gather(back, "fsdp", axis=0)
        valid = -(-cols // share)
        return tuple(
            outputs(
                jnp.arange(valid, dtype=jnp.int32), momentum, gradient, ortho_here, colsq,
                [whole[n] for n in range(valid)], previous=None,
            )
        )

    place, core = position_of(me // 2, chips), me % 2
    turn = ring_steps(count, True)
    swap = swap_pairs(count)
    steps = jnp.arange(chips, dtype=jnp.int32)
    way = 1 - 2 * core
    mine = 2 * chip_at((place - way * steps) % chips, chips) + core
    theirs = 2 * chip_at((place + way * steps) % chips, chips) + 1 - core
    ids = jnp.stack([mine, theirs], axis=1).astype(jnp.int32)
    result, block = None, back
    for step in range(chips):
        if step:
            block = lax.ppermute(block, "fsdp", turn)
        other = lax.ppermute(block, "fsdp", swap)
        result = outputs(
            ids[step], momentum, gradient, ortho_here, colsq, [block, other], previous=result
        )
    return tuple(result)


def solution(mesh):
    return jax.shard_map(
        local,
        mesh=mesh,
        in_specs=(P("fsdp", "tp"), P("fsdp", "tp"), P("tp", None)),
        out_specs=(P("fsdp", "tp"), P("tp", None), P("fsdp", "tp")),
        check_vma=False,
    )
```

```python
import functools
import math

import jax
import jax.numpy as jnp
from jax import lax
from jax.experimental import pallas as pl
from jax.experimental.pallas import tpu as pltpu
from jax.sharding import PartitionSpec as P

LANES = 128
SUBLANES = 8
PANEL = 64
MIB = 1024 * 1024
FULL = lax.Precision.HIGHEST
F32 = jnp.float32
BF16 = jnp.bfloat16


def cost(flops, nbytes):
    return pl.CostEstimate(flops=flops, bytes_accessed=nbytes, transcendentals=0)


def params(mib):
    return pltpu.CompilerParams(vmem_limit_bytes=mib * MIB)


def tile_of(cols, most):
    tiles = cols // LANES
    return LANES * max(d for d in range(1, most // LANES + 1) if tiles % d == 0)


def sketch_kernel(m_ref, g_ref, b_ref, sketch_ref):
    base_b = (m_ref[...] + g_ref[...].astype(F32)).astype(BF16)
    term = jnp.dot(base_b, b_ref[...], preferred_element_type=F32)

    @pl.when(pl.program_id(0) == 0)
    def _():
        sketch_ref[...] = term

    @pl.when(pl.program_id(0) > 0)
    def _():
        sketch_ref[...] += term


def sketch_call(momentum, gradient, basis):
    rows, cols = momentum.shape
    rank = basis.shape[1]
    tile = tile_of(cols, 1536)
    return pl.pallas_call(
        sketch_kernel,
        grid=(cols // tile,),
        in_specs=[
            pl.BlockSpec((rows, tile), lambda i: (0, i)),
            pl.BlockSpec((rows, tile), lambda i: (0, i)),
            pl.BlockSpec((tile, rank), lambda i: (i, 0)),
        ],
        out_specs=pl.BlockSpec((rows, rank), lambda i: (0, 0)),
        out_shape=jax.ShapeDtypeStruct((rows, rank), F32),
        compiler_params=params(60),
        cost_estimate=cost(2 * rows * cols * rank, rows * cols * 6 + cols * rank * 2),
        name="sketch",
    )(momentum, gradient, basis)


def pack_kernel(cols, m_ref, g_ref, after_ref, out_ref):
    step = pl.program_id(0)
    share = m_ref.shape[1]
    left = cols - step * share

    @pl.when(left >= share)
    def _():
        out_ref[0] = (m_ref[...] + g_ref[...].astype(F32)).astype(BF16)

    @pl.when(left < share)
    def _():
        lane = lax.broadcasted_iota(jnp.int32, m_ref.shape, 1)
        base = m_ref[...] + g_ref[...].astype(F32)
        out_ref[0] = jnp.where(lane < left, base, 0.0).astype(BF16)


def pack_call(momentum, gradient, share, count, after):
    rows, cols = momentum.shape
    last = pl.cdiv(cols, share) - 1
    block = pl.BlockSpec((rows, share), lambda i: (0, jnp.minimum(i, last)))
    return pl.pallas_call(
        functools.partial(pack_kernel, cols),
        grid=(count,),
        in_specs=[block, block, pl.BlockSpec(memory_space=pl.ANY)],
        out_specs=pl.BlockSpec((1, rows, share), lambda i: (i, 0, 0)),
        out_shape=jax.ShapeDtypeStruct((count, rows, share), BF16),
        compiler_params=params(48),
        cost_estimate=cost(rows * cols, rows * cols * 8),
        name="pack",
    )(momentum, gradient, after)


def spread(x, lane):
    return jnp.broadcast_to(x[:, lane : lane + 1], (x.shape[0], LANES))


def row_of(x, row):
    return jnp.broadcast_to(x[row : row + 1, :], (SUBLANES, LANES))


def eliminate(block):
    sub = lax.broadcasted_iota(jnp.int32, (SUBLANES, LANES), 0)
    groups = PANEL // SUBLANES
    top = [block[SUBLANES * g : SUBLANES * (g + 1)] for g in range(groups)]
    for g in range(groups):
        first = PANEL + SUBLANES * g
        t = top[g]
        cols = [spread(t, first + j) for j in range(SUBLANES)]
        below = [[spread(top[i], first + j) for j in range(SUBLANES)] for i in range(g + 1, groups)]
        pivots = jnp.zeros((SUBLANES, LANES), F32)
        inverse, corner = [], {}
        for j in range(SUBLANES):
            pivot = row_of(cols[j], j)
            pivots = jnp.where(sub == j, pivot, pivots)
            inverse.append(1.0 / pivot)
            factor = jnp.where(sub > j, cols[j] * inverse[j], 0.0)
            t = t - factor * row_of(t, j)
            for k in range(j + 1, SUBLANES):
                corner[j, k] = row_of(cols[k], j)
                cols[k] = cols[k] - factor * corner[j, k]
        lines = [row_of(t, j) for j in range(SUBLANES)]
        for i in range(g + 1, groups):
            entries = below[i - g - 1]
            acc = top[i]
            for j in range(SUBLANES):
                factor = entries[j] * inverse[j]
                acc = acc - factor * lines[j]
                for k in range(j + 1, SUBLANES):
                    entries[k] = entries[k] - factor * corner[j, k]
            top[i] = acc
        top[g] = t * lax.rsqrt(pivots)
    return jnp.concatenate(top, axis=0)[:, :PANEL]


def dot(a, b, dims):
    return lax.dot_general(a, b, (dims, ((), ())), precision=FULL, preferred_element_type=F32)


def factor_kernel(count, ids_ref, *refs):
    pieces, (ortho_t_ref, here_ref, whole_ref, work_ref) = refs[:count], refs[count:]
    rows, rank = pieces[0].shape
    for n, piece in enumerate(pieces):
        whole_ref[pl.ds(pl.multiple_of(ids_ref[n] * rows, SUBLANES), rows), :] = piece[...]
    total = count * rows

    work_ref[:, :rank] = jnp.zeros((rank, rank), F32)
    chunk = 4 * rows

    @pl.loop(0, total // chunk)
    def _(n):
        part = whole_ref[pl.ds(pl.multiple_of(n * chunk, SUBLANES), chunk), :]
        work_ref[:, :rank] += dot(part, part, ((0,), (0,)))

    line = lax.broadcasted_iota(jnp.int32, (rank, rank), 0)
    column = lax.broadcasted_iota(jnp.int32, (rank, rank), 1)
    work_ref[:, rank:] = jnp.where(line == column, 1.0, 0.0).astype(F32)
    eye = jnp.where(line == column, 1.0, 0.0).astype(F32)[:PANEL, :PANEL]
    for start in range(0, rank, PANEL):
        stop = start + PANEL
        diagonal = work_ref[start:stop, start:stop]
        small = eliminate(jnp.concatenate([eye, diagonal], axis=1))
        panel = dot(small, work_ref[start:stop, :], ((1,), (0,)))
        work_ref[start:stop, :] = panel
        if stop < rank:
            work_ref[stop:, :] -= dot(panel[:, stop:rank], panel, ((0,), (0,)))
    inverse = work_ref[:, rank:]
    here_ref[...] = dot(pieces[0][...], inverse, ((1,), (1,))).astype(BF16)
    for n in range(0, total, chunk):
        ortho_t_ref[:, n : n + chunk] = dot(
            inverse, whole_ref[n : n + chunk, :], ((1,), (1,))
        ).astype(BF16)


def factor_call(ids, pieces):
    count = len(pieces)
    rows, rank = pieces[0].shape
    total = count * rows
    vmem = pl.BlockSpec(memory_space=pltpu.VMEM)
    return pl.pallas_call(
        functools.partial(factor_kernel, count),
        in_specs=[pl.BlockSpec(memory_space=pltpu.SMEM)] + [vmem] * count,
        out_specs=[vmem, vmem],
        out_shape=[
            jax.ShapeDtypeStruct((rank, total), BF16),
            jax.ShapeDtypeStruct((rows, rank), BF16),
        ],
        scratch_shapes=[pltpu.VMEM((total, rank), F32), pltpu.VMEM((rank, 2 * rank), F32)],
        compiler_params=params(24),
        cost_estimate=cost(40 * total * rank * rank, total * rank * 6),
        name="factor",
    )(ids, *pieces)


def back_kernel(ortho_t_ref, columns_ref, back_ref, colsq_ref):
    back_t = jnp.dot(ortho_t_ref[...], columns_ref[...], preferred_element_type=F32)
    back = back_t.T.astype(BF16)
    back_ref[...] = back
    wide = back.astype(F32)
    colsq_ref[...] = jnp.sum(wide * wide, axis=0, keepdims=True)


def back_call(ortho_t, columns):
    rank, total = ortho_t.shape
    share = columns.shape[1]
    return pl.pallas_call(
        back_kernel,
        in_specs=[pl.BlockSpec(memory_space=pltpu.VMEM)] * 2,
        out_specs=[pl.BlockSpec(memory_space=pltpu.VMEM)] * 2,
        out_shape=[
            jax.ShapeDtypeStruct((share, rank), BF16),
            jax.ShapeDtypeStruct((1, rank), F32),
        ],
        compiler_params=params(24),
        cost_estimate=cost(2 * rank * total * share, total * share * 2),
        name="back",
    )(ortho_t, columns)


def output_kernel(count, factor, carried, ids_ref, m_ref, g_ref, ortho_ref, colsq_ref, *refs):
    pieces, (nm_ref, nb_ref, up_ref) = refs[:count], refs[count + carried :]
    step = pl.program_id(0)
    scale = lax.rsqrt(colsq_ref[...] + 1e-06)
    ortho = ortho_ref[...]
    over = (((1,), (1,)), ((), ()))
    for n, piece in enumerate(pieces):

        @pl.when(step == n)
        def _():
            back = piece[...]
            unit = (back.astype(F32) * scale).astype(BF16)
            nb_ref[...] = unit
            base = m_ref[...] + g_ref[...].astype(F32)
            nm_ref[...] = base - 0.05 * lax.dot_general(
                ortho, back, over, preferred_element_type=F32
            )
            up_ref[...] = (
                factor * lax.dot_general(ortho, unit, over, preferred_element_type=F32)
            ).astype(BF16)


def output_call(ids, momentum, gradient, ortho, colsq, pieces, factor, previous):
    rows, cols = momentum.shape
    share, rank = pieces[0].shape
    count = len(pieces)
    wide = pl.BlockSpec((rows, share), lambda i, ids: (0, ids[i]))
    tall = pl.BlockSpec((share, rank), lambda i, ids: (ids[i], 0))
    carried = 3 if previous else 0
    aliases = {5 + count + n: n for n in range(carried)}
    return pl.pallas_call(
        functools.partial(output_kernel, count, factor, carried),
        grid_spec=pltpu.PrefetchScalarGridSpec(
            num_scalar_prefetch=1,
            grid=(count,),
            in_specs=[
                wide,
                wide,
                pl.BlockSpec((rows, rank), lambda i, ids: (0, 0)),
                pl.BlockSpec((1, rank), lambda i, ids: (0, 0)),
            ]
            + [pl.BlockSpec((share, rank), lambda i, ids: (0, 0))] * count
            + [pl.BlockSpec(memory_space=pl.ANY)] * carried,
            out_specs=[wide, tall, wide],
        ),
        out_shape=[
            jax.ShapeDtypeStruct((rows, cols), F32),
            jax.ShapeDtypeStruct((cols, rank), BF16),
            jax.ShapeDtypeStruct((rows, cols), BF16),
        ],
        input_output_aliases=aliases,
        compiler_params=params(32),
        cost_estimate=cost(
            4 * rows * share * rank * count, count * share * (rows * 12 + rank * 4)
        ),
        name="outputs",
    )(ids, momentum, gradient, ortho, colsq, *pieces, *(previous or ()))


def chip_at(position, chips):
    half = chips // 2
    return jnp.where(position < half, 2 * position, 2 * (chips - 1 - position) + 1)


def position_of(chip, chips):
    return jnp.where(chip % 2 == 0, chip // 2, chips - 1 - chip // 2)


def ring_order(chips):
    half = chips // 2
    return [2 * q for q in range(half)] + [2 * (chips - 1 - q) + 1 for q in range(half, chips)]


def ring_steps(count, by_core):
    order = ring_order(count // 2)
    after = dict(zip(order, order[1:] + order[:1]))
    before = {b: a for a, b in after.items()}
    up = [(2 * c + k, 2 * after[c] + k) for c in order for k in (0, 1)]
    down = [(2 * c + k, 2 * before[c] + k) for c in order for k in (0, 1)]
    if not by_core:
        return up, down
    return [p for p in up if p[0] % 2 == 0] + [p for p in down if p[0] % 2 == 1]


def swap_pairs(count):
    return [(n, n ^ 1) for n in range(count)]


def gather_small(x, count):
    chips = count // 2
    me = lax.axis_index("fsdp")
    place, core = position_of(me // 2, chips), me % 2
    up, down = ring_steps(count, False)
    offsets, held = [0], [x]
    ahead = behind = x
    for step in range(1, chips // 2 + 1):
        ahead = lax.ppermute(ahead, "fsdp", up)
        held.append(ahead)
        offsets.append(-step)
        if 2 * step < chips:
            behind = lax.ppermute(behind, "fsdp", down)
            held.append(behind)
            offsets.append(step)
    other = [lax.ppermute(h, "fsdp", swap_pairs(count)) for h in held]
    chip = chip_at((place + jnp.array(offsets, jnp.int32)) % chips, chips)
    ids = jnp.concatenate([2 * chip + core, 2 * chip + 1 - core])
    return held + other, ids.astype(jnp.int32)


def tie(x, *work):
    return lax.optimization_barrier((x, *work))[0] if work else x


def sum_rounds(count, tp_count):
    rounds = [("tp", [(0, 1), (1, 0)])]
    bit = 1
    while bit < count:
        rounds.append(("fsdp", [(n, n ^ bit) for n in range(count)]))
        bit *= 2
    return rounds


def local(momentum, gradient, basis):
    rows, cols = momentum.shape
    rank = basis.shape[1]
    count = lax.axis_size("fsdp")
    tp_count = lax.axis_size("tp")
    chips = count // 2
    share = -(-cols // (count * LANES)) * LANES
    factor = math.sqrt(rows * count * cols * tp_count / rank)
    me = lax.axis_index("fsdp")
    ring = tp_count == 2 and count in (4, 8, 16, 32) and (count - 1) * share < cols

    sketch = sketch_call(momentum, gradient, basis)
    if tp_count == 2:
        sketch = sketch + lax.ppermute(sketch, "tp", [(0, 1), (1, 0)])
    else:
        sketch = lax.psum(sketch, "tp")

    if ring:
        pieces, ids = gather_small(sketch, count)
    else:
        whole = lax.all_gather(sketch, "fsdp", axis=0)
        pieces = [lax.dynamic_index_in_dim(whole, (me + n) % count, 0, False) for n in range(count)]
        ids = ((me + jnp.arange(count)) % count).astype(jnp.int32)
    outgoing = pack_call(momentum, gradient, share, count, pieces[min(4, count - 1)])
    columns = lax.all_to_all(outgoing, "fsdp", 0, 0, tiled=True)
    columns = columns.reshape(rows * count, share)
    ortho_t, ortho_here = factor_call(ids, pieces)
    back, part = back_call(ortho_t, columns)

    outputs = functools.partial(output_call, factor=factor)
    if not ring:
        colsq = lax.psum(part, ("fsdp", "tp"))
        whole = lax.all_gather(back, "fsdp", axis=0)
        valid = -(-cols // share)
        return tuple(
            outputs(
                jnp.arange(valid, dtype=jnp.int32), momentum, gradient, ortho_here, colsq,
                [whole[n] for n in range(valid)], previous=None,
            )
        )

    place, core = position_of(me // 2, chips), me % 2
    turn = ring_steps(count, True)
    swap = swap_pairs(count)
    steps = jnp.arange(chips, dtype=jnp.int32)
    way = 1 - 2 * core
    mine = 2 * chip_at((place - way * steps) % chips, chips) + core
    theirs = 2 * chip_at((place + way * steps) % chips, chips) + 1 - core
    ids = jnp.stack([mine, theirs], axis=1).astype(jnp.int32)
    rounds = sum_rounds(count, tp_count)
    colsq, result = part, None
    blocks, others = [back], []
    written = 0
    waiting = ()
    for step in range(chips):
        if step + 1 < chips:
            blocks.append(lax.ppermute(tie(blocks[step], *waiting), "fsdp", turn))
        others.append(lax.ppermute(blocks[step], "fsdp", swap))
        for axis, pairs in rounds[:2]:
            colsq = colsq + lax.ppermute(colsq, axis, pairs)
        done, rounds = not rounds, rounds[2:]
        waiting = (colsq,)
        if done and step > written + 1:
            ready = slice(written, min(written + 2, step))
            written = ready.stop
            result = outputs(
                ids[ready].reshape(-1), momentum, gradient, ortho_here, colsq,
                [x for pair in zip(blocks[ready], others[ready]) for x in pair], previous=result,
            )
            waiting = tuple(result)
    for n in range(written, chips):
        result = outputs(
            ids[n], momentum, gradient, ortho_here, colsq, [blocks[n], others[n]], previous=result
        )
    return tuple(result)


def solution(mesh):
    return jax.shard_map(
        local,
        mesh=mesh,
        in_specs=(P("fsdp", "tp"), P("fsdp", "tp"), P("tp", None)),
        out_specs=(P("fsdp", "tp"), P("tp", None), P("fsdp", "tp")),
        check_vma=False,
    )
```

```python
import functools
import math

import jax
import jax.numpy as jnp
from jax import lax
from jax.experimental import pallas as pl
from jax.experimental.pallas import tpu as pltpu
from jax.sharding import PartitionSpec as P

LANES = 128
SUBLANES = 8
PANEL = 64
MIB = 1024 * 1024
FULL = lax.Precision.HIGHEST
F32 = jnp.float32
BF16 = jnp.bfloat16


def cost(flops, nbytes):
    return pl.CostEstimate(flops=flops, bytes_accessed=nbytes, transcendentals=0)


def params(mib):
    return pltpu.CompilerParams(vmem_limit_bytes=mib * MIB)


def spread(x, lane):
    return jnp.broadcast_to(x[:, lane : lane + 1], (x.shape[0], LANES))


def row_of(x, row):
    return jnp.broadcast_to(x[row : row + 1, :], (SUBLANES, LANES))


def eliminate(block):
    sub = lax.broadcasted_iota(jnp.int32, (SUBLANES, LANES), 0)
    groups = PANEL // SUBLANES
    top = [block[SUBLANES * g : SUBLANES * (g + 1)] for g in range(groups)]
    for g in range(groups):
        first = PANEL + SUBLANES * g
        t = top[g]
        cols = [spread(t, first + j) for j in range(SUBLANES)]
        below = [[spread(top[i], first + j) for j in range(SUBLANES)] for i in range(g + 1, groups)]
        pivots = jnp.zeros((SUBLANES, LANES), F32)
        inverse, corner = [], {}
        for j in range(SUBLANES):
            pivot = row_of(cols[j], j)
            pivots = jnp.where(sub == j, pivot, pivots)
            inverse.append(1.0 / pivot)
            factor = jnp.where(sub > j, cols[j] * inverse[j], 0.0)
            t = t - factor * row_of(t, j)
            for k in range(j + 1, SUBLANES):
                corner[j, k] = row_of(cols[k], j)
                cols[k] = cols[k] - factor * corner[j, k]
        lines = [row_of(t, j) for j in range(SUBLANES)]
        for i in range(g + 1, groups):
            entries = below[i - g - 1]
            acc = top[i]
            for j in range(SUBLANES):
                factor = entries[j] * inverse[j]
                acc = acc - factor * lines[j]
                for k in range(j + 1, SUBLANES):
                    entries[k] = entries[k] - factor * corner[j, k]
            top[i] = acc
        top[g] = t * lax.rsqrt(pivots)
    return jnp.concatenate(top, axis=0)[:, :PANEL]


def dot(a, b, dims):
    return lax.dot_general(a, b, (dims, ((), ())), precision=FULL, preferred_element_type=F32)


def factor_kernel(count, ids_ref, *refs):
    pieces, (ortho_t_ref, here_ref, whole_ref, work_ref) = refs[:count], refs[count:]
    rows, rank = pieces[0].shape
    for n, piece in enumerate(pieces):
        whole_ref[pl.ds(pl.multiple_of(ids_ref[n] * rows, SUBLANES), rows), :] = piece[...]
    total = count * rows

    work_ref[:, :rank] = jnp.zeros((rank, rank), F32)
    chunk = 4 * rows

    @pl.loop(0, total // chunk)
    def _(n):
        part = whole_ref[pl.ds(pl.multiple_of(n * chunk, SUBLANES), chunk), :]
        work_ref[:, :rank] += dot(part, part, ((0,), (0,)))

    line = lax.broadcasted_iota(jnp.int32, (rank, rank), 0)
    column = lax.broadcasted_iota(jnp.int32, (rank, rank), 1)
    work_ref[:, rank:] = jnp.where(line == column, 1.0, 0.0).astype(F32)
    eye = jnp.where(line == column, 1.0, 0.0).astype(F32)[:PANEL, :PANEL]
    for start in range(0, rank, PANEL):
        stop = start + PANEL
        diagonal = work_ref[start:stop, start:stop]
        small = eliminate(jnp.concatenate([eye, diagonal], axis=1))
        panel = dot(small, work_ref[start:stop, :], ((1,), (0,)))
        work_ref[start:stop, :] = panel
        if stop < rank:
            work_ref[stop:, :] -= dot(panel[:, stop:rank], panel, ((0,), (0,)))
    inverse = work_ref[:, rank:]
    here_ref[...] = dot(pieces[0][...], inverse, ((1,), (1,))).astype(BF16)
    for n in range(0, total, chunk):
        ortho_t_ref[:, n : n + chunk] = dot(
            inverse, whole_ref[n : n + chunk, :], ((1,), (1,))
        ).astype(BF16)


def factor_call(ids, pieces):
    count = len(pieces)
    rows, rank = pieces[0].shape
    total = count * rows
    vmem = pl.BlockSpec(memory_space=pltpu.VMEM)
    return pl.pallas_call(
        functools.partial(factor_kernel, count),
        in_specs=[pl.BlockSpec(memory_space=pltpu.SMEM)] + [vmem] * count,
        out_specs=[vmem, vmem],
        out_shape=[
            jax.ShapeDtypeStruct((rank, total), BF16),
            jax.ShapeDtypeStruct((rows, rank), BF16),
        ],
        scratch_shapes=[pltpu.VMEM((total, rank), F32), pltpu.VMEM((rank, 2 * rank), F32)],
        compiler_params=params(24),
        cost_estimate=cost(40 * total * rank * rank, total * rank * 6),
        name="factor",
    )(ids, *pieces)


def back_kernel(ortho_t_ref, columns_ref, colsq_ref, *part_refs):
    back_t = jnp.dot(ortho_t_ref[...], columns_ref[...], preferred_element_type=F32)
    back = back_t.T.astype(BF16)
    start = 0
    for part_ref in part_refs:
        stop = start + part_ref.shape[0]
        part_ref[...] = back[start:stop]
        start = stop
    wide = back.astype(F32)
    colsq_ref[...] = jnp.sum(wide * wide, axis=0, keepdims=True)


def back_call(ortho_t, columns, parts):
    rank, total = ortho_t.shape
    share = columns.shape[1]
    vmem = pl.BlockSpec(memory_space=pltpu.VMEM)
    return pl.pallas_call(
        back_kernel,
        in_specs=[vmem] * 2,
        out_specs=[vmem] * (1 + len(parts)),
        out_shape=[jax.ShapeDtypeStruct((1, rank), F32)]
        + [jax.ShapeDtypeStruct((part, rank), BF16) for part in parts],
        compiler_params=params(24),
        cost_estimate=cost(2 * rank * total * share, total * share * 2),
        name="back",
    )(ortho_t, columns)


def output_kernel(parts, factor, carried, ids_ref, m_ref, g_ref, ortho_ref, colsq_ref, *refs):
    count = len(refs) - carried - 3
    pieces, (nm_ref, nb_ref, up_ref) = refs[:count], refs[count + carried :]
    step = pl.program_id(0)
    scale = lax.rsqrt(colsq_ref[...] + 1e-06)
    ortho = ortho_ref[...]
    over = (((1,), (1,)), ((), ()))

    def write(piece, here):
        back = piece[...]
        unit = (back.astype(F32) * scale).astype(BF16)
        nb_ref[here, :] = unit
        base = m_ref[:, here] + g_ref[:, here].astype(F32)
        nm_ref[:, here] = base - 0.05 * lax.dot_general(
            ortho, back, over, preferred_element_type=F32
        )
        up_ref[:, here] = (
            factor * lax.dot_general(ortho, unit, over, preferred_element_type=F32)
        ).astype(BF16)

    for n in range(count // parts):

        @pl.when(step == n)
        def _():
            start = 0
            for piece in pieces[n * parts : (n + 1) * parts]:
                stop = start + piece.shape[0]
                write(piece, slice(start, stop))
                start = stop


def output_call(ids, momentum, gradient, ortho, colsq, blocks, factor, previous):
    rows, cols = momentum.shape
    rank = ortho.shape[1]
    count, parts = len(blocks), len(blocks[0])
    pieces = [part for block in blocks for part in block]
    share = sum(part.shape[0] for part in blocks[0])
    wide = pl.BlockSpec((rows, share), lambda i, ids: (0, ids[i]))
    tall = pl.BlockSpec((share, rank), lambda i, ids: (ids[i], 0))
    carried = 3 if previous else 0
    aliases = {5 + len(pieces) + n: n for n in range(carried)}
    return pl.pallas_call(
        functools.partial(output_kernel, parts, factor, carried),
        grid_spec=pltpu.PrefetchScalarGridSpec(
            num_scalar_prefetch=1,
            grid=(count,),
            in_specs=[
                wide,
                wide,
                pl.BlockSpec((rows, rank), lambda i, ids: (0, 0)),
                pl.BlockSpec((1, rank), lambda i, ids: (0, 0)),
            ]
            + [pl.BlockSpec(part.shape, lambda i, ids: (0, 0)) for part in pieces]
            + [pl.BlockSpec(memory_space=pl.ANY)] * carried,
            out_specs=[wide, tall, wide],
        ),
        out_shape=[
            jax.ShapeDtypeStruct((rows, cols), F32),
            jax.ShapeDtypeStruct((cols, rank), BF16),
            jax.ShapeDtypeStruct((rows, cols), BF16),
        ],
        input_output_aliases=aliases,
        compiler_params=params(24),
        cost_estimate=cost(
            4 * rows * share * rank * count, count * share * (rows * 12 + rank * 4)
        ),
        name="outputs",
    )(ids, momentum, gradient, ortho, colsq, *pieces, *(previous or ()))


def chip_at(position, chips):
    half = chips // 2
    return jnp.where(position < half, 2 * position, 2 * (chips - 1 - position) + 1)


def position_of(chip, chips):
    return jnp.where(chip % 2 == 0, chip // 2, chips - 1 - chip // 2)


def ring_order(chips):
    half = chips // 2
    return [2 * q for q in range(half)] + [2 * (chips - 1 - q) + 1 for q in range(half, chips)]


def ring_steps(count, by_core):
    order = ring_order(count // 2)
    after = dict(zip(order, order[1:] + order[:1]))
    before = {b: a for a, b in after.items()}
    up = [(2 * c + k, 2 * after[c] + k) for c in order for k in (0, 1)]
    down = [(2 * c + k, 2 * before[c] + k) for c in order for k in (0, 1)]
    if not by_core:
        return up, down
    return [p for p in up if p[0] % 2 == 0] + [p for p in down if p[0] % 2 == 1]


def swap_pairs(count):
    return [(n, n ^ 1) for n in range(count)]


def gather_small(x, count):
    chips = count // 2
    me = lax.axis_index("fsdp")
    place, core = position_of(me // 2, chips), me % 2
    up, down = ring_steps(count, False)
    offsets, held = [0], [x]
    ahead = behind = x
    for step in range(1, chips // 2 + 1):
        ahead, behind = lax.optimization_barrier((ahead, behind))
        ahead = lax.ppermute(ahead, "fsdp", up)
        held.append(ahead)
        offsets.append(-step)
        if 2 * step < chips:
            behind = lax.ppermute(behind, "fsdp", down)
            held.append(behind)
            offsets.append(step)
    other = [lax.ppermute(h, "fsdp", swap_pairs(count)) for h in held]
    chip = chip_at((place + jnp.array(offsets, jnp.int32)) % chips, chips)
    ids = jnp.concatenate([2 * chip + core, 2 * chip + 1 - core])
    return held + other, ids.astype(jnp.int32), held


def tie(x, *work):
    return lax.optimization_barrier((x, *work))[0] if work else x


def sum_rounds(count, tp_count):
    rounds = [("tp", [(0, 1), (1, 0)])]
    bit = 1
    while bit < count:
        rounds.append(("fsdp", [(n, n ^ bit) for n in range(count)]))
        bit *= 2
    return rounds


def local(momentum, gradient, basis):
    rows, cols = momentum.shape
    rank = basis.shape[1]
    count = lax.axis_size("fsdp")
    tp_count = lax.axis_size("tp")
    chips = count // 2
    share = -(-cols // (count * LANES)) * LANES
    factor = math.sqrt(rows * count * cols * tp_count / rank)
    me = lax.axis_index("fsdp")
    ring = tp_count == 2 and count in (4, 8, 16, 32) and (count - 1) * share < cols

    base_b = (momentum + gradient.astype(F32)).astype(BF16)
    sketch = jnp.dot(base_b, basis, preferred_element_type=F32)
    outgoing = jnp.pad(base_b, ((0, 0), (0, share * count - cols)))
    outgoing = jnp.swapaxes(outgoing.reshape(rows, count, share), 0, 1)
    if tp_count == 2:
        sketch = sketch + lax.ppermute(sketch, "tp", [(0, 1), (1, 0)])
    else:
        sketch = lax.psum(sketch, "tp")

    if ring:
        pieces, ids, travelled = gather_small(sketch, count)
        outgoing = tie(outgoing, *travelled)
    else:
        whole = lax.all_gather(sketch, "fsdp", axis=0)
        pieces = [lax.dynamic_index_in_dim(whole, (me + n) % count, 0, False) for n in range(count)]
        ids = ((me + jnp.arange(count)) % count).astype(jnp.int32)
    columns = lax.all_to_all(outgoing, "fsdp", 0, 0, tiled=True)
    columns = columns.reshape(rows * count, share)
    ortho_t, ortho_here = factor_call(ids, pieces)
    momentum = pltpu.with_memory_space_constraint(momentum, pltpu.HBM)
    tiles = share // LANES
    cuts = [share]
    if ring and tiles > 1:
        cuts = [share - tiles // 2 * LANES, tiles // 2 * LANES]
    part, *back = back_call(ortho_t, columns, cuts)

    outputs = functools.partial(output_call, factor=factor)
    if not ring:
        colsq = lax.psum(part, ("fsdp", "tp"))
        whole = lax.all_gather(back[0], "fsdp", axis=0)
        valid = -(-cols // share)
        return tuple(
            outputs(
                jnp.arange(valid, dtype=jnp.int32), momentum, gradient, ortho_here, colsq,
                [[whole[n]] for n in range(valid)], previous=None,
            )
        )

    place, core = position_of(me // 2, chips), me % 2
    turn = ring_steps(count, True)
    swap = swap_pairs(count)
    steps = jnp.arange(chips, dtype=jnp.int32)
    way = 1 - 2 * core
    mine = 2 * chip_at((place - way * steps) % chips, chips) + core
    theirs = 2 * chip_at((place + way * steps) % chips, chips) + 1 - core
    ids = jnp.stack([mine, theirs], axis=1).astype(jnp.int32)
    rounds = sum_rounds(count, tp_count)
    colsq, result = part, None
    mine, theirs = [list(back)], []
    written, waiting = 0, ()
    for step in range(chips):
        mine.append([])
        theirs.append([])
        for n in range(len(cuts)):
            block = mine[step][n]
            if step + 1 < chips:
                mine[step + 1].append(lax.ppermute(tie(block, *waiting), "fsdp", turn))
            theirs[step].append(lax.ppermute(block, "fsdp", swap))
            if rounds:
                axis, pairs = rounds.pop(0)
                colsq = colsq + lax.ppermute(tie(colsq, block), axis, pairs)
                waiting = ()
            elif written + 1 < step:
                result = outputs(
                    ids[written], momentum, gradient, ortho_here, colsq,
                    [mine[written], theirs[written]], previous=result,
                )
                written += 1
                waiting = tuple(result)
    for n in range(written, chips):
        result = outputs(
            ids[n], momentum, gradient, ortho_here, colsq, [mine[n], theirs[n]], previous=result
        )
    return tuple(result)


def solution(mesh):
    return jax.shard_map(
        local,
        mesh=mesh,
        in_specs=(P("fsdp", "tp"), P("fsdp", "tp"), P("tp", None)),
        out_specs=(P("fsdp", "tp"), P("tp", None), P("fsdp", "tp")),
        check_vma=False,
    )
```

```python
import functools
import math

import jax
import jax.numpy as jnp
from jax import lax
from jax.experimental import pallas as pl
from jax.experimental.pallas import tpu as pltpu
from jax.sharding import PartitionSpec as P

LANES = 128
SUBLANES = 8
PANEL = 64
MIB = 1024 * 1024
FULL = lax.Precision.HIGHEST
F32 = jnp.float32
BF16 = jnp.bfloat16


def cost(flops, nbytes):
    return pl.CostEstimate(flops=flops, bytes_accessed=nbytes, transcendentals=0)


def params(mib):
    return pltpu.CompilerParams(vmem_limit_bytes=mib * MIB)


def pack_kernel(ids_ref, base_ref, *out_refs):
    for n, out_ref in enumerate(out_refs):
        share = out_ref.shape[1]
        start = pl.multiple_of(ids_ref[n] * share, LANES)
        out_ref[...] = base_ref[:, pl.ds(start, share)]


def pack_call(ids, base_b, share):
    rows = base_b.shape[0]
    count = base_b.shape[1] // share
    vmem = pl.BlockSpec(memory_space=pltpu.VMEM)
    return pl.pallas_call(
        pack_kernel,
        in_specs=[pl.BlockSpec(memory_space=pltpu.SMEM), vmem],
        out_specs=[vmem] * count,
        out_shape=[jax.ShapeDtypeStruct((rows, share), BF16)] * count,
        compiler_params=params(16),
        cost_estimate=cost(0, 4 * rows * share * count),
        name="pack",
    )(ids, base_b)


def spread(x, lane):
    return jnp.broadcast_to(x[:, lane : lane + 1], (x.shape[0], LANES))


def row_of(x, row):
    return jnp.broadcast_to(x[row : row + 1, :], (SUBLANES, LANES))


def eliminate(block):
    sub = lax.broadcasted_iota(jnp.int32, (SUBLANES, LANES), 0)
    groups = PANEL // SUBLANES
    top = [block[SUBLANES * g : SUBLANES * (g + 1)] for g in range(groups)]
    for g in range(groups):
        first = PANEL + SUBLANES * g
        t = top[g]
        cols = [spread(t, first + j) for j in range(SUBLANES)]
        below = [[spread(top[i], first + j) for j in range(SUBLANES)] for i in range(g + 1, groups)]
        pivots = jnp.zeros((SUBLANES, LANES), F32)
        inverse, corner = [], {}
        for j in range(SUBLANES):
            pivot = row_of(cols[j], j)
            pivots = jnp.where(sub == j, pivot, pivots)
            inverse.append(1.0 / pivot)
            factor = jnp.where(sub > j, cols[j] * inverse[j], 0.0)
            t = t - factor * row_of(t, j)
            for k in range(j + 1, SUBLANES):
                corner[j, k] = row_of(cols[k], j)
                cols[k] = cols[k] - factor * corner[j, k]
        lines = [row_of(t, j) for j in range(SUBLANES)]
        for i in range(g + 1, groups):
            entries = below[i - g - 1]
            acc = top[i]
            for j in range(SUBLANES):
                factor = entries[j] * inverse[j]
                acc = acc - factor * lines[j]
                for k in range(j + 1, SUBLANES):
                    entries[k] = entries[k] - factor * corner[j, k]
            top[i] = acc
        top[g] = t * lax.rsqrt(pivots)
    return jnp.concatenate(top, axis=0)[:, :PANEL]


def dot(a, b, dims):
    return lax.dot_general(a, b, (dims, ((), ())), precision=FULL, preferred_element_type=F32)


def factor_kernel(count, ids_ref, *refs):
    pieces, (ortho_t_ref, here_ref, whole_ref, work_ref) = refs[:count], refs[count:]
    rows, rank = pieces[0].shape
    for n, piece in enumerate(pieces):
        whole_ref[pl.ds(pl.multiple_of(ids_ref[n] * rows, SUBLANES), rows), :] = piece[...]
    total = count * rows

    work_ref[:, :rank] = jnp.zeros((rank, rank), F32)
    chunk = 4 * rows

    @pl.loop(0, total // chunk)
    def _(n):
        part = whole_ref[pl.ds(pl.multiple_of(n * chunk, SUBLANES), chunk), :]
        work_ref[:, :rank] += dot(part, part, ((0,), (0,)))

    line = lax.broadcasted_iota(jnp.int32, (rank, rank), 0)
    column = lax.broadcasted_iota(jnp.int32, (rank, rank), 1)
    work_ref[:, rank:] = jnp.where(line == column, 1.0, 0.0).astype(F32)
    eye = jnp.where(line == column, 1.0, 0.0).astype(F32)[:PANEL, :PANEL]
    for start in range(0, rank, PANEL):
        stop = start + PANEL
        diagonal = work_ref[start:stop, start:stop]
        small = eliminate(jnp.concatenate([eye, diagonal], axis=1))
        panel = dot(small, work_ref[start:stop, :], ((1,), (0,)))
        work_ref[start:stop, :] = panel
        if stop < rank:
            work_ref[stop:, :] -= dot(panel[:, stop:rank], panel, ((0,), (0,)))
    inverse = work_ref[:, rank:]
    here_ref[...] = dot(pieces[0][...], inverse, ((1,), (1,))).astype(BF16)
    for n in range(0, total, chunk):
        ortho_t_ref[:, n : n + chunk] = dot(
            inverse, whole_ref[n : n + chunk, :], ((1,), (1,))
        ).astype(BF16)


def factor_call(ids, pieces):
    count = len(pieces)
    rows, rank = pieces[0].shape
    total = count * rows
    vmem = pl.BlockSpec(memory_space=pltpu.VMEM)
    return pl.pallas_call(
        functools.partial(factor_kernel, count),
        in_specs=[pl.BlockSpec(memory_space=pltpu.SMEM)] + [vmem] * count,
        out_specs=[vmem, vmem],
        out_shape=[
            jax.ShapeDtypeStruct((rank, total), BF16),
            jax.ShapeDtypeStruct((rows, rank), BF16),
        ],
        scratch_shapes=[pltpu.VMEM((total, rank), F32), pltpu.VMEM((rank, 2 * rank), F32)],
        compiler_params=params(24),
        cost_estimate=cost(40 * total * rank * rank, total * rank * 6),
        name="factor",
    )(ids, *pieces)


def back_kernel(pieces, ids_ref, ortho_t_ref, *refs):
    columns, (colsq_ref, *part_refs), whole_ref = refs[:pieces], refs[pieces:-1], refs[-1]
    rows = columns[0].shape[0]
    for n, piece in enumerate(columns):
        whole_ref[pl.ds(pl.multiple_of(ids_ref[n] * rows, 16), rows), :] = piece[...]
    back_t = jnp.dot(ortho_t_ref[...], whole_ref[...], preferred_element_type=F32)
    back = back_t.T.astype(BF16)
    start = 0
    for part_ref in part_refs:
        stop = start + part_ref.shape[0]
        part_ref[...] = back[start:stop]
        start = stop
    wide = back.astype(F32)
    colsq_ref[...] = jnp.sum(wide * wide, axis=0, keepdims=True)


def back_call(ids, ortho_t, columns, parts):
    rank, total = ortho_t.shape
    share = columns[0].shape[1]
    vmem = pl.BlockSpec(memory_space=pltpu.VMEM)
    return pl.pallas_call(
        functools.partial(back_kernel, len(columns)),
        in_specs=[pl.BlockSpec(memory_space=pltpu.SMEM), vmem] + [vmem] * len(columns),
        out_specs=[vmem] * (1 + len(parts)),
        out_shape=[jax.ShapeDtypeStruct((1, rank), F32)]
        + [jax.ShapeDtypeStruct((part, rank), BF16) for part in parts],
        scratch_shapes=[pltpu.VMEM((total, share), BF16)],
        compiler_params=params(24),
        cost_estimate=cost(2 * rank * total * share, total * share * 2),
        name="back",
    )(ids, ortho_t, *columns)


def output_kernel(parts, factor, carried, ids_ref, m_ref, g_ref, ortho_ref, colsq_ref, *refs):
    count = len(refs) - carried - 3
    pieces, (nm_ref, nb_ref, up_ref) = refs[:count], refs[count + carried :]
    step = pl.program_id(0)
    scale = lax.rsqrt(colsq_ref[...] + 1e-06)
    ortho = ortho_ref[...]
    over = (((1,), (1,)), ((), ()))

    def write(piece, here):
        back = piece[...]
        unit = (back.astype(F32) * scale).astype(BF16)
        nb_ref[here, :] = unit
        base = m_ref[:, here] + g_ref[:, here].astype(F32)
        nm_ref[:, here] = base - 0.05 * lax.dot_general(
            ortho, back, over, preferred_element_type=F32
        )
        up_ref[:, here] = (
            factor * lax.dot_general(ortho, unit, over, preferred_element_type=F32)
        ).astype(BF16)

    for n in range(count // parts):

        @pl.when(step == n)
        def _():
            start = 0
            for piece in pieces[n * parts : (n + 1) * parts]:
                stop = start + piece.shape[0]
                write(piece, slice(start, stop))
                start = stop


def output_call(ids, momentum, gradient, ortho, colsq, blocks, factor, previous):
    rows, cols = momentum.shape
    rank = ortho.shape[1]
    count, parts = len(blocks), len(blocks[0])
    pieces = [part for block in blocks for part in block]
    share = sum(part.shape[0] for part in blocks[0])
    wide = pl.BlockSpec((rows, share), lambda i, ids: (0, ids[i]))
    tall = pl.BlockSpec((share, rank), lambda i, ids: (ids[i], 0))
    carried = 3 if previous else 0
    aliases = {5 + len(pieces) + n: n for n in range(carried)}
    return pl.pallas_call(
        functools.partial(output_kernel, parts, factor, carried),
        grid_spec=pltpu.PrefetchScalarGridSpec(
            num_scalar_prefetch=1,
            grid=(count,),
            in_specs=[
                wide,
                wide,
                pl.BlockSpec((rows, rank), lambda i, ids: (0, 0)),
                pl.BlockSpec((1, rank), lambda i, ids: (0, 0)),
            ]
            + [pl.BlockSpec(part.shape, lambda i, ids: (0, 0)) for part in pieces]
            + [pl.BlockSpec(memory_space=pl.ANY)] * carried,
            out_specs=[wide, tall, wide],
        ),
        out_shape=[
            jax.ShapeDtypeStruct((rows, cols), F32),
            jax.ShapeDtypeStruct((cols, rank), BF16),
            jax.ShapeDtypeStruct((rows, cols), BF16),
        ],
        input_output_aliases=aliases,
        compiler_params=params(24),
        cost_estimate=cost(
            4 * rows * share * rank * count, count * share * (rows * 12 + rank * 4)
        ),
        name="outputs",
    )(ids, momentum, gradient, ortho, colsq, *pieces, *(previous or ()))


def chip_at(position, chips):
    half = chips // 2
    return jnp.where(position < half, 2 * position, 2 * (chips - 1 - position) + 1)


def position_of(chip, chips):
    return jnp.where(chip % 2 == 0, chip // 2, chips - 1 - chip // 2)


def ring_order(chips):
    half = chips // 2
    return [2 * q for q in range(half)] + [2 * (chips - 1 - q) + 1 for q in range(half, chips)]


def ring_steps(count, by_core):
    order = ring_order(count // 2)
    after = dict(zip(order, order[1:] + order[:1]))
    before = {b: a for a, b in after.items()}
    up = [(2 * c + k, 2 * after[c] + k) for c in order for k in (0, 1)]
    down = [(2 * c + k, 2 * before[c] + k) for c in order for k in (0, 1)]
    if not by_core:
        return up, down
    return [p for p in up if p[0] % 2 == 0] + [p for p in down if p[0] % 2 == 1]


def swap_pairs(count):
    return [(n, n ^ 1) for n in range(count)]


def tie(x, *work):
    return lax.optimization_barrier((x, *work))[0] if work else x


def gather_and_exchange(sketch, outgoing, count):
    chips = count // 2
    me = lax.axis_index("fsdp")
    place, core = position_of(me // 2, chips), me % 2
    up, down = ring_steps(count, False)
    columns = {0: outgoing[0]}

    def exchange(window, *after):
        for k in window:
            pairs = [(n, n ^ k) for n in range(count)]
            columns[k] = lax.ppermute(tie(outgoing[k], *after), "fsdp", pairs)

    far = [[k + chips] + [k] * (k > 0) for k in range(chips)]
    exchange(far[0], sketch)
    sketch = sketch + lax.ppermute(sketch, "tp", [(0, 1), (1, 0)])
    offsets, held = [0], [sketch]
    ahead = behind = sketch
    for step in range(1, chips // 2 + 1):
        sent = [columns[k] for k in far[step - 2]] if step > 1 else []
        ahead, behind = lax.optimization_barrier((ahead, behind, *sent))[:2]
        exchange(far[step], ahead, behind)
        ahead = lax.ppermute(ahead, "fsdp", up)
        held.append(ahead)
        offsets.append(-step)
        if 2 * step < chips:
            behind = lax.ppermute(behind, "fsdp", down)
            held.append(behind)
            offsets.append(step)
    for window in far[chips // 2 + 1 :]:
        exchange(window, ahead, behind)
    other = [lax.ppermute(h, "fsdp", swap_pairs(count)) for h in held]
    chip = chip_at((place + jnp.array(offsets, jnp.int32)) % chips, chips)
    ids = jnp.concatenate([2 * chip + core, 2 * chip + 1 - core])
    return held + other, ids.astype(jnp.int32), [columns[k] for k in range(count)]


def sum_rounds(count, tp_count):
    rounds = [("tp", [(0, 1), (1, 0)])]
    bit = 1
    while bit < count:
        rounds.append(("fsdp", [(n, n ^ bit) for n in range(count)]))
        bit *= 2
    return rounds


def local(momentum, gradient, basis):
    rows, cols = momentum.shape
    rank = basis.shape[1]
    count = lax.axis_size("fsdp")
    tp_count = lax.axis_size("tp")
    chips = count // 2
    share = -(-cols // (count * LANES)) * LANES
    factor = math.sqrt(rows * count * cols * tp_count / rank)
    me = lax.axis_index("fsdp")
    ring = tp_count == 2 and count in (4, 8, 16, 32) and (count - 1) * share < cols

    base_b = (momentum + gradient.astype(F32)).astype(BF16)
    sketch = jnp.dot(base_b, basis, preferred_element_type=F32)
    padded = jnp.pad(base_b, ((0, 0), (0, share * count - cols)))
    if ring:
        partners = me ^ jnp.arange(count, dtype=jnp.int32)
        outgoing = pack_call(partners, padded, share)
        pieces, ids, columns = gather_and_exchange(sketch, outgoing, count)
    else:
        outgoing = jnp.swapaxes(padded.reshape(rows, count, share), 0, 1)
        columns = lax.all_to_all(outgoing, "fsdp", 0, 0, tiled=True)
        columns = [columns.reshape(rows * count, share)]
        partners = jnp.zeros((1,), jnp.int32)
        whole = lax.all_gather(lax.psum(sketch, "tp"), "fsdp", axis=0)
        pieces = [lax.dynamic_index_in_dim(whole, (me + n) % count, 0, False) for n in range(count)]
        ids = ((me + jnp.arange(count)) % count).astype(jnp.int32)
    ortho_t, ortho_here = factor_call(ids, pieces)
    momentum = pltpu.with_memory_space_constraint(momentum, pltpu.HBM)
    tiles = share // LANES
    cuts = [share]
    if ring and tiles > 1:
        cuts = [share - tiles // 2 * LANES, tiles // 2 * LANES]
    part, *back = back_call(partners, ortho_t, columns, cuts)

    outputs = functools.partial(output_call, factor=factor)
    if not ring:
        colsq = lax.psum(part, ("fsdp", "tp"))
        whole = lax.all_gather(back[0], "fsdp", axis=0)
        valid = -(-cols // share)
        return tuple(
            outputs(
                jnp.arange(valid, dtype=jnp.int32), momentum, gradient, ortho_here, colsq,
                [[whole[n]] for n in range(valid)], previous=None,
            )
        )

    place, core = position_of(me // 2, chips), me % 2
    turn = ring_steps(count, True)
    swap = swap_pairs(count)
    steps = jnp.arange(chips, dtype=jnp.int32)
    way = 1 - 2 * core
    mine = 2 * chip_at((place - way * steps) % chips, chips) + core
    theirs = 2 * chip_at((place + way * steps) % chips, chips) + 1 - core
    ids = jnp.stack([mine, theirs], axis=1).astype(jnp.int32)
    rounds = sum_rounds(count, tp_count)
    colsq, result = part, None
    mine, theirs = [list(back)], []
    written, waiting = 0, ()
    for step in range(chips):
        mine.append([])
        theirs.append([])
        for n in range(len(cuts)):
            block = mine[step][n]
            if step + 1 < chips:
                mine[step + 1].append(lax.ppermute(tie(block, *waiting), "fsdp", turn))
            theirs[step].append(lax.ppermute(block, "fsdp", swap))
            if rounds:
                axis, pairs = rounds.pop(0)
                colsq = colsq + lax.ppermute(tie(colsq, block), axis, pairs)
                waiting = ()
            elif written + 1 < step:
                result = outputs(
                    ids[written], momentum, gradient, ortho_here, colsq,
                    [mine[written], theirs[written]], previous=result,
                )
                written += 1
                waiting = tuple(result)
    for n in range(written, chips):
        result = outputs(
            ids[n], momentum, gradient, ortho_here, colsq, [mine[n], theirs[n]], previous=result
        )
    return tuple(result)


def solution(mesh):
    return jax.shard_map(
        local,
        mesh=mesh,
        in_specs=(P("fsdp", "tp"), P("fsdp", "tp"), P("tp", None)),
        out_specs=(P("fsdp", "tp"), P("tp", None), P("fsdp", "tp")),
        check_vma=False,
    )
```

```python
import functools
import math

import jax
import jax.numpy as jnp
from jax import lax
from jax.experimental import pallas as pl
from jax.experimental.pallas import tpu as pltpu
from jax.sharding import PartitionSpec as P

LANES = 128
SUBLANES = 8
PANEL = 64
MIB = 1024 * 1024
FULL = lax.Precision.HIGHEST
F32 = jnp.float32
BF16 = jnp.bfloat16


def cost(flops, nbytes):
    return pl.CostEstimate(flops=flops, bytes_accessed=nbytes, transcendentals=0)


def params(mib):
    return pltpu.CompilerParams(vmem_limit_bytes=mib * MIB)


def by_width(block, cols, share, start, stop, act):
    last = (cols - 1) // share
    width, short = stop - start, max(0, min(cols - last * share, stop) - start)
    if short == width:
        act(width)
        return

    @pl.when(block < last)
    def _():
        act(width)

    if short:

        @pl.when(block == last)
        def _():
            act(short)


def pack_kernel(ids_ref, base_ref, *out_refs):
    cols = base_ref.shape[1]
    for n, out_ref in enumerate(out_refs):
        share = out_ref.shape[1]
        start = pl.multiple_of(ids_ref[n] * share, LANES)

        def fill(width):
            out_ref[:, :width] = base_ref[:, pl.ds(start, width)].astype(BF16)
            if width < share:
                out_ref[:, width:] = jnp.zeros((out_ref.shape[0], share - width), BF16)

        by_width(ids_ref[n], cols, share, 0, share, fill)


def pack_call(ids, base, share):
    rows = base.shape[0]
    count = ids.shape[0]
    vmem = pl.BlockSpec(memory_space=pltpu.VMEM)
    return pl.pallas_call(
        pack_kernel,
        in_specs=[pl.BlockSpec(memory_space=pltpu.SMEM), vmem],
        out_specs=[vmem] * count,
        out_shape=[jax.ShapeDtypeStruct((rows, share), BF16)] * count,
        compiler_params=params(16),
        cost_estimate=cost(0, 6 * rows * share * count),
        name="pack",
    )(ids, base)


def spread(x, lane):
    return jnp.broadcast_to(x[:, lane : lane + 1], (x.shape[0], LANES))


def row_of(x, row):
    return jnp.broadcast_to(x[row : row + 1, :], (SUBLANES, LANES))


def eliminate(block):
    sub = lax.broadcasted_iota(jnp.int32, (SUBLANES, LANES), 0)
    groups = PANEL // SUBLANES
    top = [block[SUBLANES * g : SUBLANES * (g + 1)] for g in range(groups)]
    for g in range(groups):
        first = PANEL + SUBLANES * g
        t = top[g]
        cols = [spread(t, first + j) for j in range(SUBLANES)]
        below = [[spread(top[i], first + j) for j in range(SUBLANES)] for i in range(g + 1, groups)]
        pivots = jnp.zeros((SUBLANES, LANES), F32)
        inverse, corner = [], {}
        for j in range(SUBLANES):
            pivot = row_of(cols[j], j)
            pivots = jnp.where(sub == j, pivot, pivots)
            inverse.append(1.0 / pivot)
            factor = jnp.where(sub > j, cols[j] * inverse[j], 0.0)
            t = t - factor * row_of(t, j)
            for k in range(j + 1, SUBLANES):
                corner[j, k] = row_of(cols[k], j)
                cols[k] = cols[k] - factor * corner[j, k]
        lines = [row_of(t, j) for j in range(SUBLANES)]
        for i in range(g + 1, groups):
            entries = below[i - g - 1]
            acc = top[i]
            for j in range(SUBLANES):
                factor = entries[j] * inverse[j]
                acc = acc - factor * lines[j]
                for k in range(j + 1, SUBLANES):
                    entries[k] = entries[k] - factor * corner[j, k]
            top[i] = acc
        top[g] = t * lax.rsqrt(pivots)
    return jnp.concatenate(top, axis=0)[:, :PANEL]


def dot(a, b, dims):
    return lax.dot_general(a, b, (dims, ((), ())), precision=FULL, preferred_element_type=F32)


def factor_kernel(count, ids_ref, *refs):
    pieces, (ortho_t_ref, here_ref, whole_ref, work_ref) = refs[:count], refs[count:]
    rows, rank = pieces[0].shape
    for n, piece in enumerate(pieces):
        whole_ref[pl.ds(pl.multiple_of(ids_ref[n] * rows, SUBLANES), rows), :] = piece[...]
    total = count * rows

    work_ref[:, :rank] = jnp.zeros((rank, rank), F32)
    chunk = 4 * rows

    @pl.loop(0, total // chunk)
    def _(n):
        part = whole_ref[pl.ds(pl.multiple_of(n * chunk, SUBLANES), chunk), :]
        work_ref[:, :rank] += dot(part, part, ((0,), (0,)))

    line = lax.broadcasted_iota(jnp.int32, (rank, rank), 0)
    column = lax.broadcasted_iota(jnp.int32, (rank, rank), 1)
    work_ref[:, rank:] = jnp.where(line == column, 1.0, 0.0).astype(F32)
    eye = jnp.where(line == column, 1.0, 0.0).astype(F32)[:PANEL, :PANEL]
    for start in range(0, rank, PANEL):
        stop = start + PANEL
        diagonal = work_ref[start:stop, start:stop]
        small = eliminate(jnp.concatenate([eye, diagonal], axis=1))
        panel = dot(small, work_ref[start:stop, :], ((1,), (0,)))
        work_ref[start:stop, :] = panel
        if stop < rank:
            work_ref[stop:, :] -= dot(panel[:, stop:rank], panel, ((0,), (0,)))
    inverse = work_ref[:, rank:]
    here_ref[...] = dot(pieces[0][...], inverse, ((1,), (1,))).astype(BF16)
    for n in range(0, total, chunk):
        ortho_t_ref[:, n : n + chunk] = dot(
            inverse, whole_ref[n : n + chunk, :], ((1,), (1,))
        ).astype(BF16)


def factor_call(ids, pieces):
    count = len(pieces)
    rows, rank = pieces[0].shape
    total = count * rows
    vmem = pl.BlockSpec(memory_space=pltpu.VMEM)
    return pl.pallas_call(
        functools.partial(factor_kernel, count),
        in_specs=[pl.BlockSpec(memory_space=pltpu.SMEM)] + [vmem] * count,
        out_specs=[vmem, vmem],
        out_shape=[
            jax.ShapeDtypeStruct((rank, total), BF16),
            jax.ShapeDtypeStruct((rows, rank), BF16),
        ],
        scratch_shapes=[pltpu.VMEM((total, rank), F32), pltpu.VMEM((rank, 2 * rank), F32)],
        compiler_params=params(24),
        cost_estimate=cost(40 * total * rank * rank, total * rank * 6),
        name="factor",
    )(ids, *pieces)


def back_kernel(pieces, ids_ref, ortho_t_ref, *refs):
    columns, (colsq_ref, *part_refs), whole_ref = refs[:pieces], refs[pieces:-1], refs[-1]
    rows = columns[0].shape[0]
    for n, piece in enumerate(columns):
        whole_ref[pl.ds(pl.multiple_of(ids_ref[n] * rows, 16), rows), :] = piece[...]
    back_t = jnp.dot(ortho_t_ref[...], whole_ref[...], preferred_element_type=F32)
    back = back_t.T.astype(BF16)
    start = 0
    for part_ref in part_refs:
        stop = start + part_ref.shape[0]
        part_ref[...] = back[start:stop]
        start = stop
    wide = back.astype(F32)
    colsq_ref[...] = jnp.sum(wide * wide, axis=0, keepdims=True)


def back_call(ids, ortho_t, columns, parts):
    rank, total = ortho_t.shape
    share = columns[0].shape[1]
    vmem = pl.BlockSpec(memory_space=pltpu.VMEM)
    return pl.pallas_call(
        functools.partial(back_kernel, len(columns)),
        in_specs=[pl.BlockSpec(memory_space=pltpu.SMEM), vmem] + [vmem] * len(columns),
        out_specs=[vmem] * (1 + len(parts)),
        out_shape=[jax.ShapeDtypeStruct((1, rank), F32)]
        + [jax.ShapeDtypeStruct((part, rank), BF16) for part in parts],
        scratch_shapes=[pltpu.VMEM((total, share), BF16)],
        compiler_params=params(24),
        cost_estimate=cost(2 * rank * total * share, total * share * 2),
        name="back",
    )(ids, ortho_t, *columns)


def output_kernel(parts, factor, ids_ref, base_ref, ortho_ref, colsq_ref, *refs):
    *pieces, nm_ref, nb_ref, up_ref, nm_tile, nb_tile, up_tile, sems = refs
    share, cols = nm_tile.shape[2], nm_ref.shape[1]
    scale = lax.rsqrt(colsq_ref[...] + 1e-06)
    ortho = ortho_ref[...]
    over = (((1,), (1,)), ((), ()))

    def copies(n, part, start, width):
        there = pl.ds(pl.multiple_of(ids_ref[n] * share + start, LANES), width)
        here = slice(start, start + width)
        return (
            pltpu.make_async_copy(nm_tile.at[n, :, here], nm_ref.at[:, there], sems.at[n, part, 0]),
            pltpu.make_async_copy(nb_tile.at[n, here, :], nb_ref.at[there, :], sems.at[n, part, 1]),
            pltpu.make_async_copy(up_tile.at[n, :, here], up_ref.at[:, there], sems.at[n, part, 2]),
        )

    ranges = []
    for n in range(nm_tile.shape[0]):
        start = 0
        for part in range(parts):
            piece = pieces[n * parts + part]
            stop = start + piece.shape[0]

            def compute(width):
                here = slice(start, start + width)
                there = pl.ds(pl.multiple_of(ids_ref[n] * share + start, LANES), width)
                back = piece[:width, :]
                unit = (back.astype(F32) * scale).astype(BF16)
                nb_tile[n, here, :] = unit
                nm_tile[n, :, here] = base_ref[:, there] - 0.05 * lax.dot_general(
                    ortho, back, over, preferred_element_type=F32
                )
                up_tile[n, :, here] = (
                    factor * lax.dot_general(ortho, unit, over, preferred_element_type=F32)
                ).astype(BF16)
                for copy in copies(n, part, start, width):
                    copy.start()

            by_width(ids_ref[n], cols, share, start, stop, compute)
            ranges.append((n, part, start, stop))
            start = stop

    for n, part, start, stop in ranges:

        def wait(width):
            for copy in copies(n, part, start, width):
                copy.wait()

        by_width(ids_ref[n], cols, share, start, stop, wait)


def output_call(ids, base, cols, ortho, colsq, blocks, factor, previous):
    rows, rank = ortho.shape
    count, parts = len(blocks), len(blocks[0])
    pieces = [part for block in blocks for part in block]
    share = sum(part.shape[0] for part in blocks[0])
    previous = previous or ()
    vmem, hbm = pl.BlockSpec(memory_space=pltpu.VMEM), pl.BlockSpec(memory_space=pltpu.HBM)
    return pl.pallas_call(
        functools.partial(output_kernel, parts, factor),
        in_specs=[pl.BlockSpec(memory_space=pltpu.SMEM)]
        + [vmem] * (3 + len(pieces))
        + [hbm] * len(previous),
        out_specs=[hbm] * 3,
        out_shape=[
            jax.ShapeDtypeStruct((rows, cols), F32),
            jax.ShapeDtypeStruct((cols, rank), BF16),
            jax.ShapeDtypeStruct((rows, cols), BF16),
        ],
        scratch_shapes=[
            pltpu.VMEM((count, rows, share), F32),
            pltpu.VMEM((count, share, rank), BF16),
            pltpu.VMEM((count, rows, share), BF16),
            pltpu.SemaphoreType.DMA((count, parts, 3)),
        ],
        input_output_aliases={4 + len(pieces) + n: n for n in range(len(previous))},
        compiler_params=params(16),
        cost_estimate=cost(
            4 * rows * share * rank * count, count * share * (rows * 10 + rank * 4)
        ),
        name="outputs",
    )(ids, base, ortho, colsq, *pieces, *previous)


def chip_at(position, chips):
    half = chips // 2
    return jnp.where(position < half, 2 * position, 2 * (chips - 1 - position) + 1)


def position_of(chip, chips):
    return jnp.where(chip % 2 == 0, chip // 2, chips - 1 - chip // 2)


def ring_order(chips):
    half = chips // 2
    return [2 * q for q in range(half)] + [2 * (chips - 1 - q) + 1 for q in range(half, chips)]


def ring_steps(count, by_core):
    order = ring_order(count // 2)
    after = dict(zip(order, order[1:] + order[:1]))
    before = {b: a for a, b in after.items()}
    up = [(2 * c + k, 2 * after[c] + k) for c in order for k in (0, 1)]
    down = [(2 * c + k, 2 * before[c] + k) for c in order for k in (0, 1)]
    if not by_core:
        return up, down
    return [p for p in up if p[0] % 2 == 0] + [p for p in down if p[0] % 2 == 1]


def swap_pairs(count):
    return [(n, n ^ 1) for n in range(count)]


def tie(x, *work):
    return lax.optimization_barrier((x, *work))[0] if work else x


def exchange_windows(count):
    if count != 16:
        far = [[k + count // 2] + [k] * (k > 0) for k in range(count // 2)]
        steps = count // 4 + 1
        return far[:steps] + [sum(far[steps:], [])]
    return [[8, 4], [9, 5], [10, 6], [11, 7], [12, 1, 2, 3], [13, 14, 15]]


def gather_and_exchange(sketch, outgoing, count):
    chips = count // 2
    me = lax.axis_index("fsdp")
    place, core = position_of(me // 2, chips), me % 2
    up, down = ring_steps(count, False)
    columns = {0: outgoing[0]}

    def exchange(window, *after):
        for k in window:
            pairs = [(n, n ^ k) for n in range(count)]
            columns[k] = lax.ppermute(tie(outgoing[k], *after), "fsdp", pairs)

    windows = exchange_windows(count)
    swap = swap_pairs(count)
    exchange(windows[0], sketch)
    sketch = sketch + lax.ppermute(sketch, "tp", [(0, 1), (1, 0)])
    offsets, held, other = [0], [sketch], []
    ahead = behind = sketch
    arrived, earlier = [sketch], []
    for step in range(1, chips // 2 + 1):
        work = [columns[k] for k in windows[step - 2]] if step > 1 else []
        ahead, behind, *_ = lax.optimization_barrier((ahead, behind, *work, *earlier))
        exchange(windows[step], ahead, behind)
        earlier = [lax.ppermute(x, "fsdp", swap) for x in arrived]
        other += earlier
        ahead = lax.ppermute(ahead, "fsdp", up)
        arrived = [ahead]
        offsets.append(-step)
        if 2 * step < chips:
            behind = lax.ppermute(behind, "fsdp", down)
            arrived.append(behind)
            offsets.append(step)
        held += arrived
    for window in windows[chips // 2 + 1 :]:
        exchange(window, ahead, behind)
    other += [lax.ppermute(x, "fsdp", swap) for x in arrived]
    chip = chip_at((place + jnp.array(offsets, jnp.int32)) % chips, chips)
    ids = jnp.concatenate([2 * chip + core, 2 * chip + 1 - core])
    return held + other, ids.astype(jnp.int32), [columns[k] for k in range(count)]


def sum_rounds(count):
    rounds, bit = [("tp", [1])], 1
    while bit < count:
        rounds.append(("fsdp", [bit, 2 * bit, 3 * bit] if 2 * bit < count else [bit]))
        bit *= 4
    return rounds


def sum_round(x, axis, distances):
    size = lax.axis_size(axis)
    terms = [x]
    for d in distances:
        terms.append(lax.ppermute(x, axis, [(n, n ^ d) for n in range(size)]))
    if len(terms) == 2:
        return terms[0] + terms[1]
    return (terms[0] + terms[1]) + (terms[2] + terms[3])


def local(momentum, gradient, basis):
    rows, cols = momentum.shape
    rank = basis.shape[1]
    count = lax.axis_size("fsdp")
    tp_count = lax.axis_size("tp")
    chips = count // 2
    share = -(-cols // (count * LANES)) * LANES
    factor = math.sqrt(rows * count * cols * tp_count / rank)
    me = lax.axis_index("fsdp")
    ring = tp_count == 2 and count in (4, 8, 16, 32) and (count - 1) * share < cols

    base = momentum + gradient.astype(F32)
    base_b = base.astype(BF16)
    sketch = jnp.dot(base_b, basis, preferred_element_type=F32)
    base = pltpu.with_memory_space_constraint(base, pltpu.VMEM)
    if ring:
        partners = me ^ jnp.arange(count, dtype=jnp.int32)
        outgoing = pack_call(partners, base, share)
        pieces, ids, columns = gather_and_exchange(sketch, outgoing, count)
    else:
        padded = jnp.pad(base_b, ((0, 0), (0, share * count - cols)))
        outgoing = jnp.swapaxes(padded.reshape(rows, count, share), 0, 1)
        columns = lax.all_to_all(outgoing, "fsdp", 0, 0, tiled=True)
        columns = [columns.reshape(rows * count, share)]
        partners = jnp.zeros((1,), jnp.int32)
        whole = lax.all_gather(lax.psum(sketch, "tp"), "fsdp", axis=0)
        pieces = [lax.dynamic_index_in_dim(whole, (me + n) % count, 0, False) for n in range(count)]
        ids = ((me + jnp.arange(count)) % count).astype(jnp.int32)
    ortho_t, ortho_here = factor_call(ids, pieces)
    tiles = share // LANES
    cuts = [share]
    if ring and tiles > 1:
        cuts = [share - tiles // 2 * LANES, tiles // 2 * LANES]
    part, *back = back_call(partners, ortho_t, columns, cuts)

    outputs = functools.partial(output_call, factor=factor)
    if not ring:
        colsq = lax.psum(part, ("fsdp", "tp"))
        whole = lax.all_gather(back[0], "fsdp", axis=0)
        valid = -(-cols // share)
        return tuple(
            outputs(
                jnp.arange(valid, dtype=jnp.int32), base, cols, ortho_here, colsq,
                [[whole[n]] for n in range(valid)], previous=None,
            )
        )

    place, core = position_of(me // 2, chips), me % 2
    turn = ring_steps(count, True)
    swap = swap_pairs(count)
    steps = jnp.arange(chips, dtype=jnp.int32)
    way = 1 - 2 * core
    mine = 2 * chip_at((place - way * steps) % chips, chips) + core
    theirs = 2 * chip_at((place + way * steps) % chips, chips) + 1 - core
    ids = jnp.stack([mine, theirs], axis=1).astype(jnp.int32)
    rounds = sum_rounds(count)
    colsq, result = part, None
    mine, theirs = [list(back)], []
    written, waiting = 0, ()
    for step in range(chips):
        mine.append([])
        theirs.append([])
        if step == 1:
            waiting += tuple(mine[1])
        for n in range(len(cuts)):
            block = mine[step][n]
            if step + 1 < chips:
                mine[step + 1].append(lax.ppermute(tie(block, *waiting), "fsdp", turn))
            theirs[step].append(lax.ppermute(block, "fsdp", swap))
            waiting = ()
            if rounds:
                colsq = sum_round(tie(colsq, block), *rounds.pop(0))
            elif written + 1 < step:
                result = outputs(
                    ids[written], base, cols, ortho_here, colsq,
                    [mine[written], theirs[written]], previous=result,
                )
                written += 1
                waiting = tuple(result)
    for n in range(written, chips):
        result = outputs(
            ids[n], base, cols, ortho_here, colsq, [mine[n], theirs[n]], previous=result
        )
    return tuple(result)


def solution(mesh):
    return jax.shard_map(
        local,
        mesh=mesh,
        in_specs=(P("fsdp", "tp"), P("fsdp", "tp"), P("tp", None)),
        out_specs=(P("fsdp", "tp"), P("tp", None), P("fsdp", "tp")),
        check_vma=False,
    )
```

```python
import functools
import math

import jax
import jax.numpy as jnp
from jax import lax
from jax.experimental import pallas as pl
from jax.experimental.pallas import tpu as pltpu
from jax.sharding import PartitionSpec as P

LANES = 128
SUBLANES = 8
PANEL = 64
MIB = 1024 * 1024
FULL = lax.Precision.HIGHEST
F32 = jnp.float32
BF16 = jnp.bfloat16


def cost(flops, nbytes):
    return pl.CostEstimate(flops=flops, bytes_accessed=nbytes, transcendentals=0)


def params(mib):
    return pltpu.CompilerParams(vmem_limit_bytes=mib * MIB)


def by_width(block, cols, share, start, stop, act):
    last = (cols - 1) // share
    width, short = stop - start, max(0, min(cols - last * share, stop) - start)
    if short == width:
        act(width)
        return

    @pl.when(block < last)
    def _():
        act(width)

    if short:

        @pl.when(block == last)
        def _():
            act(short)


def pack_kernel(ids_ref, base_ref, *out_refs):
    cols = base_ref.shape[1]
    for n, out_ref in enumerate(out_refs):
        share = out_ref.shape[1]
        start = pl.multiple_of(ids_ref[n] * share, LANES)

        def fill(width):
            out_ref[:, :width] = base_ref[:, pl.ds(start, width)].astype(BF16)
            if width < share:
                out_ref[:, width:] = jnp.zeros((out_ref.shape[0], share - width), BF16)

        by_width(ids_ref[n], cols, share, 0, share, fill)


def pack_call(ids, base, share):
    rows = base.shape[0]
    count = ids.shape[0]
    vmem = pl.BlockSpec(memory_space=pltpu.VMEM)
    return pl.pallas_call(
        pack_kernel,
        in_specs=[pl.BlockSpec(memory_space=pltpu.SMEM), vmem],
        out_specs=[vmem] * count,
        out_shape=[jax.ShapeDtypeStruct((rows, share), BF16)] * count,
        compiler_params=params(16),
        cost_estimate=cost(0, 6 * rows * share * count),
        name="pack",
    )(ids, base)


def spread(x, lane):
    return jnp.broadcast_to(x[:, lane : lane + 1], (x.shape[0], LANES))


def row_of(x, row):
    return jnp.broadcast_to(x[row : row + 1, :], (SUBLANES, LANES))


def eliminate(block):
    sub = lax.broadcasted_iota(jnp.int32, (SUBLANES, LANES), 0)
    groups = PANEL // SUBLANES
    top = [block[SUBLANES * g : SUBLANES * (g + 1)] for g in range(groups)]
    for g in range(groups):
        first = PANEL + SUBLANES * g
        t = top[g]
        cols = [spread(t, first + j) for j in range(SUBLANES)]
        below = [[spread(top[i], first + j) for j in range(SUBLANES)] for i in range(g + 1, groups)]
        pivots = jnp.zeros((SUBLANES, LANES), F32)
        inverse, corner = [], {}
        for j in range(SUBLANES):
            pivot = row_of(cols[j], j)
            pivots = jnp.where(sub == j, pivot, pivots)
            inverse.append(1.0 / pivot)
            factor = jnp.where(sub > j, cols[j] * inverse[j], 0.0)
            t = t - factor * row_of(t, j)
            for k in range(j + 1, SUBLANES):
                corner[j, k] = row_of(cols[k], j)
                cols[k] = cols[k] - factor * corner[j, k]
        lines = [row_of(t, j) for j in range(SUBLANES)]
        for i in range(g + 1, groups):
            entries = below[i - g - 1]
            acc = top[i]
            for j in range(SUBLANES):
                factor = entries[j] * inverse[j]
                acc = acc - factor * lines[j]
                for k in range(j + 1, SUBLANES):
                    entries[k] = entries[k] - factor * corner[j, k]
            top[i] = acc
        top[g] = t * lax.rsqrt(pivots)
    return jnp.concatenate(top, axis=0)[:, :PANEL]


def dot(a, b, dims):
    return lax.dot_general(a, b, (dims, ((), ())), precision=FULL, preferred_element_type=F32)


def factor_kernel(count, ids_ref, *refs):
    pieces, (ortho_t_ref, here_ref, whole_ref, work_ref) = refs[:count], refs[count:]
    rows, rank = pieces[0].shape
    for n, piece in enumerate(pieces):
        whole_ref[pl.ds(pl.multiple_of(ids_ref[n] * rows, SUBLANES), rows), :] = piece[...]
    total = count * rows

    work_ref[:, :rank] = jnp.zeros((rank, rank), F32)
    chunk = 4 * rows

    @pl.loop(0, total // chunk)
    def _(n):
        part = whole_ref[pl.ds(pl.multiple_of(n * chunk, SUBLANES), chunk), :]
        work_ref[:, :rank] += dot(part, part, ((0,), (0,)))

    line = lax.broadcasted_iota(jnp.int32, (rank, rank), 0)
    column = lax.broadcasted_iota(jnp.int32, (rank, rank), 1)
    work_ref[:, rank:] = jnp.where(line == column, 1.0, 0.0).astype(F32)
    eye = jnp.where(line == column, 1.0, 0.0).astype(F32)[:PANEL, :PANEL]
    for start in range(0, rank, PANEL):
        stop = start + PANEL
        diagonal = work_ref[start:stop, start:stop]
        small = eliminate(jnp.concatenate([eye, diagonal], axis=1))
        panel = dot(small, work_ref[start:stop, :], ((1,), (0,)))
        work_ref[start:stop, :] = panel
        if stop < rank:
            work_ref[stop:, :] -= dot(panel[:, stop:rank], panel, ((0,), (0,)))
    inverse = work_ref[:, rank:]
    here_ref[...] = dot(pieces[0][...], inverse, ((1,), (1,))).astype(BF16)
    for n in range(0, total, chunk):
        ortho_t_ref[:, n : n + chunk] = dot(
            inverse, whole_ref[n : n + chunk, :], ((1,), (1,))
        ).astype(BF16)


def factor_call(ids, pieces):
    count = len(pieces)
    rows, rank = pieces[0].shape
    total = count * rows
    vmem = pl.BlockSpec(memory_space=pltpu.VMEM)
    return pl.pallas_call(
        functools.partial(factor_kernel, count),
        in_specs=[pl.BlockSpec(memory_space=pltpu.SMEM)] + [vmem] * count,
        out_specs=[vmem, vmem],
        out_shape=[
            jax.ShapeDtypeStruct((rank, total), BF16),
            jax.ShapeDtypeStruct((rows, rank), BF16),
        ],
        scratch_shapes=[pltpu.VMEM((total, rank), F32), pltpu.VMEM((rank, 2 * rank), F32)],
        compiler_params=params(24),
        cost_estimate=cost(40 * total * rank * rank, total * rank * 6),
        name="factor",
    )(ids, *pieces)


def back_kernel(pieces, ids_ref, base_ref, ortho_t_ref, *refs):
    columns, (colsq_ref, *part_refs), whole_ref = refs[:pieces], refs[pieces:-1], refs[-1]
    rows = columns[0].shape[0]
    for n, piece in enumerate(columns):
        whole_ref[pl.ds(pl.multiple_of(ids_ref[n] * rows, 16), rows), :] = piece[...]
    back_t = jnp.dot(ortho_t_ref[...], whole_ref[...], preferred_element_type=F32)
    back = back_t.T.astype(BF16)
    start = 0
    for part_ref in part_refs:
        stop = start + part_ref.shape[0]
        part_ref[...] = back[start:stop]
        start = stop
    wide = back.astype(F32)
    colsq_ref[...] = jnp.sum(wide * wide, axis=0, keepdims=True)


def back_call(ids, base, ortho_t, columns, parts):
    rank, total = ortho_t.shape
    share = columns[0].shape[1]
    vmem = pl.BlockSpec(memory_space=pltpu.VMEM)
    return pl.pallas_call(
        functools.partial(back_kernel, len(columns)),
        in_specs=[pl.BlockSpec(memory_space=pltpu.SMEM)] + [vmem] * (2 + len(columns)),
        out_specs=[vmem] * (1 + len(parts)),
        out_shape=[jax.ShapeDtypeStruct((1, rank), F32)]
        + [jax.ShapeDtypeStruct((part, rank), BF16) for part in parts],
        scratch_shapes=[pltpu.VMEM((total, share), BF16)],
        compiler_params=params(24),
        cost_estimate=cost(2 * rank * total * share, total * share * 2),
        name="back",
    )(ids, base, ortho_t, *columns)


def output_kernel(parts, factor, ids_ref, base_ref, ortho_ref, colsq_ref, *refs):
    *pieces, nm_ref, nb_ref, up_ref, nm_tile, nb_tile, up_tile, sems = refs
    share, cols = nm_tile.shape[2], nm_ref.shape[1]
    scale = lax.rsqrt(colsq_ref[...] + 1e-06)
    ortho = ortho_ref[...]
    over = (((1,), (1,)), ((), ()))

    def copies(n, part, start, width):
        there = pl.ds(pl.multiple_of(ids_ref[n] * share + start, LANES), width)
        here = slice(start, start + width)
        return (
            pltpu.make_async_copy(nm_tile.at[n, :, here], nm_ref.at[:, there], sems.at[n, part, 0]),
            pltpu.make_async_copy(nb_tile.at[n, here, :], nb_ref.at[there, :], sems.at[n, part, 1]),
            pltpu.make_async_copy(up_tile.at[n, :, here], up_ref.at[:, there], sems.at[n, part, 2]),
        )

    ranges = []
    for n in range(nm_tile.shape[0]):
        start = 0
        for part in range(parts):
            piece = pieces[n * parts + part]
            stop = start + piece.shape[0]

            def compute(width):
                here = slice(start, start + width)
                there = pl.ds(pl.multiple_of(ids_ref[n] * share + start, LANES), width)
                back = piece[:width, :]
                unit = (back.astype(F32) * scale).astype(BF16)
                nb_tile[n, here, :] = unit
                nm_tile[n, :, here] = base_ref[:, there] - 0.05 * lax.dot_general(
                    ortho, back, over, preferred_element_type=F32
                )
                up_tile[n, :, here] = (
                    factor * lax.dot_general(ortho, unit, over, preferred_element_type=F32)
                ).astype(BF16)
                for copy in copies(n, part, start, width):
                    copy.start()

            by_width(ids_ref[n], cols, share, start, stop, compute)
            ranges.append((n, part, start, stop))
            start = stop

    for n, part, start, stop in ranges:

        def wait(width):
            for copy in copies(n, part, start, width):
                copy.wait()

        by_width(ids_ref[n], cols, share, start, stop, wait)


def output_call(ids, base, cols, ortho, colsq, blocks, factor, previous):
    rows, rank = ortho.shape
    count, parts = len(blocks), len(blocks[0])
    pieces = [part for block in blocks for part in block]
    share = sum(part.shape[0] for part in blocks[0])
    previous = previous or ()
    vmem, hbm = pl.BlockSpec(memory_space=pltpu.VMEM), pl.BlockSpec(memory_space=pltpu.HBM)
    return pl.pallas_call(
        functools.partial(output_kernel, parts, factor),
        in_specs=[pl.BlockSpec(memory_space=pltpu.SMEM)]
        + [vmem] * (3 + len(pieces))
        + [hbm] * len(previous),
        out_specs=[hbm] * 3,
        out_shape=[
            jax.ShapeDtypeStruct((rows, cols), F32),
            jax.ShapeDtypeStruct((cols, rank), BF16),
            jax.ShapeDtypeStruct((rows, cols), BF16),
        ],
        scratch_shapes=[
            pltpu.VMEM((count, rows, share), F32),
            pltpu.VMEM((count, share, rank), BF16),
            pltpu.VMEM((count, rows, share), BF16),
            pltpu.SemaphoreType.DMA((count, parts, 3)),
        ],
        input_output_aliases={4 + len(pieces) + n: n for n in range(len(previous))},
        compiler_params=params(16),
        cost_estimate=cost(
            4 * rows * share * rank * count, count * share * (rows * 10 + rank * 4)
        ),
        name="outputs",
    )(ids, base, ortho, colsq, *pieces, *previous)


def chip_at(position, chips):
    half = chips // 2
    return jnp.where(position < half, 2 * position, 2 * (chips - 1 - position) + 1)


def position_of(chip, chips):
    return jnp.where(chip % 2 == 0, chip // 2, chips - 1 - chip // 2)


def ring_order(chips):
    half = chips // 2
    return [2 * q for q in range(half)] + [2 * (chips - 1 - q) + 1 for q in range(half, chips)]


def ring_steps(count, by_core):
    order = ring_order(count // 2)
    after = dict(zip(order, order[1:] + order[:1]))
    before = {b: a for a, b in after.items()}
    up = [(2 * c + k, 2 * after[c] + k) for c in order for k in (0, 1)]
    down = [(2 * c + k, 2 * before[c] + k) for c in order for k in (0, 1)]
    if not by_core:
        return up, down
    return [p for p in up if p[0] % 2 == 0] + [p for p in down if p[0] % 2 == 1]


def swap_pairs(count):
    return [(n, n ^ 1) for n in range(count)]


def tie(x, *work):
    return lax.optimization_barrier((x, *work))[0] if work else x


def exchange_windows(count):
    if count != 16:
        far = [[k + count // 2] + [k] * (k > 0) for k in range(count // 2)]
        steps = count // 4 + 1
        return far[:steps] + [sum(far[steps:], [])]
    return [[8, 4], [9, 5], [10, 6], [11, 7], [12, 1, 2, 3], [13, 14, 15]]


def gather_and_exchange(sketch, outgoing, count):
    chips = count // 2
    me = lax.axis_index("fsdp")
    place, core = position_of(me // 2, chips), me % 2
    up, down = ring_steps(count, False)
    columns = {0: outgoing[0]}

    def exchange(window, *after):
        for k in window:
            pairs = [(n, n ^ k) for n in range(count)]
            columns[k] = lax.ppermute(tie(outgoing[k], *after), "fsdp", pairs)

    windows = exchange_windows(count)
    swap = swap_pairs(count)
    exchange(windows[0], sketch)
    sketch = sketch + lax.ppermute(sketch, "tp", [(0, 1), (1, 0)])
    offsets, held, other = [0], [sketch], []
    ahead = behind = sketch
    arrived, earlier = [sketch], []
    for step in range(1, chips // 2 + 1):
        work = [columns[k] for k in windows[step - 2]] if step > 1 else []
        ahead, behind, *_ = lax.optimization_barrier((ahead, behind, *work, *earlier))
        exchange(windows[step], ahead, behind)
        earlier = [lax.ppermute(x, "fsdp", swap) for x in arrived]
        other += earlier
        ahead = lax.ppermute(ahead, "fsdp", up)
        arrived = [ahead]
        offsets.append(-step)
        if 2 * step < chips:
            behind = lax.ppermute(behind, "fsdp", down)
            arrived.append(behind)
            offsets.append(step)
        held += arrived
    for window in windows[chips // 2 + 1 :]:
        exchange(window, ahead, behind)
    other += [lax.ppermute(x, "fsdp", swap) for x in arrived]
    chip = chip_at((place + jnp.array(offsets, jnp.int32)) % chips, chips)
    ids = jnp.concatenate([2 * chip + core, 2 * chip + 1 - core])
    return held + other, ids.astype(jnp.int32), [columns[k] for k in range(count)]


def sum_rounds(count):
    rounds, bit = [("tp", [1])], 1
    while bit < count:
        rounds.append(("fsdp", [bit, 2 * bit, 3 * bit] if 2 * bit < count else [bit]))
        bit *= 4
    return rounds


def sum_round(x, axis, distances):
    size = lax.axis_size(axis)
    terms = [x]
    for d in distances:
        terms.append(lax.ppermute(x, axis, [(n, n ^ d) for n in range(size)]))
    if len(terms) == 2:
        return terms[0] + terms[1]
    return (terms[0] + terms[1]) + (terms[2] + terms[3])


def local(momentum, gradient, basis):
    rows, cols = momentum.shape
    rank = basis.shape[1]
    count = lax.axis_size("fsdp")
    tp_count = lax.axis_size("tp")
    chips = count // 2
    share = -(-cols // (count * LANES)) * LANES
    factor = math.sqrt(rows * count * cols * tp_count / rank)
    me = lax.axis_index("fsdp")
    ring = tp_count == 2 and count in (4, 8, 16, 32) and (count - 1) * share < cols

    base = momentum + gradient.astype(F32)
    base_b = base.astype(BF16)
    sketch = jnp.dot(base_b, basis, preferred_element_type=F32)
    base = pltpu.with_memory_space_constraint(base, pltpu.VMEM)
    if ring:
        partners = me ^ jnp.arange(count, dtype=jnp.int32)
        outgoing = pack_call(partners, base, share)
        pieces, ids, columns = gather_and_exchange(sketch, outgoing, count)
    else:
        padded = jnp.pad(base_b, ((0, 0), (0, share * count - cols)))
        outgoing = jnp.swapaxes(padded.reshape(rows, count, share), 0, 1)
        columns = lax.all_to_all(outgoing, "fsdp", 0, 0, tiled=True)
        columns = [columns.reshape(rows * count, share)]
        partners = jnp.zeros((1,), jnp.int32)
        whole = lax.all_gather(lax.psum(sketch, "tp"), "fsdp", axis=0)
        pieces = [lax.dynamic_index_in_dim(whole, (me + n) % count, 0, False) for n in range(count)]
        ids = ((me + jnp.arange(count)) % count).astype(jnp.int32)
    ortho_t, ortho_here = factor_call(ids, pieces)
    tiles = share // LANES
    cuts = [share]
    if ring and tiles > 1:
        cuts = [share - tiles // 2 * LANES, tiles // 2 * LANES]
    part, *back = back_call(partners, base, ortho_t, columns, cuts)

    outputs = functools.partial(output_call, factor=factor)
    if not ring:
        colsq = lax.psum(part, ("fsdp", "tp"))
        whole = lax.all_gather(back[0], "fsdp", axis=0)
        valid = -(-cols // share)
        return tuple(
            outputs(
                jnp.arange(valid, dtype=jnp.int32), base, cols, ortho_here, colsq,
                [[whole[n]] for n in range(valid)], previous=None,
            )
        )

    place, core = position_of(me // 2, chips), me % 2
    turn = ring_steps(count, True)
    swap = swap_pairs(count)
    steps = jnp.arange(chips, dtype=jnp.int32)
    way = 1 - 2 * core
    mine = 2 * chip_at((place - way * steps) % chips, chips) + core
    theirs = 2 * chip_at((place + way * steps) % chips, chips) + 1 - core
    ids = jnp.stack([mine, theirs], axis=1).astype(jnp.int32)
    colsq, result = part, None
    rounds = sum_rounds(count)

    def write(ids, blocks):
        return outputs(ids, base, cols, ortho_here, colsq, blocks, previous=result)

    mine, theirs = [list(back)], []
    written, waiting = 0, ()
    for step in range(chips):
        mine.append([])
        theirs.append([])
        if step == 1:
            waiting += (*mine[1], colsq)
        elif step == 2:
            waiting += (colsq,)
        for n in range(len(cuts)):
            block = tie(mine[step][n], *waiting)
            waiting = ()
            if step + 1 < chips:
                mine[step + 1].append(lax.ppermute(block, "fsdp", turn))
            theirs[step].append(lax.ppermute(block, "fsdp", swap))
            for _ in range(2 if step == 0 else 1):
                if rounds and n == 0:
                    colsq = sum_round(tie(colsq, block), *rounds.pop(0))
            ready = step if step + 1 == chips else step + n - 1
            if step > 1 and written < ready:
                result = write(ids[written], [mine[written], theirs[written]])
                written += 1
                waiting = tuple(result)
    for n in range(written, chips - 1):
        result = write(ids[n], [mine[n], theirs[n]])
    result = write(ids[-1, :1], [mine[chips - 1]])
    result = write(ids[-1, 1:], [theirs[chips - 1]])
    return tuple(result)


def solution(mesh):
    return jax.shard_map(
        local,
        mesh=mesh,
        in_specs=(P("fsdp", "tp"), P("fsdp", "tp"), P("tp", None)),
        out_specs=(P("fsdp", "tp"), P("tp", None), P("fsdp", "tp")),
        check_vma=False,
    )
```

```python
import functools
import math

import jax
import jax.numpy as jnp
from jax import lax
from jax.experimental import pallas as pl
from jax.experimental.pallas import tpu as pltpu
from jax.sharding import PartitionSpec as P

LANES = 128
SUBLANES = 8
PANEL = 64
MIB = 1024 * 1024
FULL = lax.Precision.HIGHEST
F32 = jnp.float32
BF16 = jnp.bfloat16


def cost(flops, nbytes):
    return pl.CostEstimate(flops=flops, bytes_accessed=nbytes, transcendentals=0)


def params(mib):
    return pltpu.CompilerParams(vmem_limit_bytes=mib * MIB)


def by_width(block, cols, share, start, stop, act):
    last = (cols - 1) // share
    width, short = stop - start, max(0, min(cols - last * share, stop) - start)
    if short == width:
        act(width)
        return

    @pl.when(block < last)
    def _():
        act(width)

    if short:

        @pl.when(block == last)
        def _():
            act(short)


def pack_kernel(ids_ref, base_ref, *out_refs):
    cols = base_ref.shape[1]
    for n, out_ref in enumerate(out_refs):
        share = out_ref.shape[1]
        start = pl.multiple_of(ids_ref[n] * share, LANES)

        def fill(width):
            out_ref[:, :width] = base_ref[:, pl.ds(start, width)].astype(BF16)
            if width < share:
                out_ref[:, width:] = jnp.zeros((out_ref.shape[0], share - width), BF16)

        by_width(ids_ref[n], cols, share, 0, share, fill)


def pack_call(ids, base, share):
    rows = base.shape[0]
    count = ids.shape[0]
    vmem = pl.BlockSpec(memory_space=pltpu.VMEM)
    return pl.pallas_call(
        pack_kernel,
        in_specs=[pl.BlockSpec(memory_space=pltpu.SMEM), vmem],
        out_specs=[vmem] * count,
        out_shape=[jax.ShapeDtypeStruct((rows, share), BF16)] * count,
        compiler_params=params(16),
        cost_estimate=cost(0, 6 * rows * share * count),
        name="pack",
    )(ids, base)


def spread(x, lane):
    return jnp.broadcast_to(x[:, lane : lane + 1], (x.shape[0], LANES))


def row_of(x, row):
    return jnp.broadcast_to(x[row : row + 1, :], (SUBLANES, LANES))


def eliminate(block):
    sub = lax.broadcasted_iota(jnp.int32, (SUBLANES, LANES), 0)
    groups = PANEL // SUBLANES
    top = [block[SUBLANES * g : SUBLANES * (g + 1)] for g in range(groups)]
    for g in range(groups):
        first = PANEL + SUBLANES * g
        t = top[g]
        cols = [spread(t, first + j) for j in range(SUBLANES)]
        below = [[spread(top[i], first + j) for j in range(SUBLANES)] for i in range(g + 1, groups)]
        pivots = jnp.zeros((SUBLANES, LANES), F32)
        inverse, corner = [], {}
        for j in range(SUBLANES):
            pivot = row_of(cols[j], j)
            pivots = jnp.where(sub == j, pivot, pivots)
            inverse.append(1.0 / pivot)
            factor = jnp.where(sub > j, cols[j] * inverse[j], 0.0)
            t = t - factor * row_of(t, j)
            for k in range(j + 1, SUBLANES):
                corner[j, k] = row_of(cols[k], j)
                cols[k] = cols[k] - factor * corner[j, k]
        lines = [row_of(t, j) for j in range(SUBLANES)]
        for i in range(g + 1, groups):
            entries = below[i - g - 1]
            acc = top[i]
            for j in range(SUBLANES):
                factor = entries[j] * inverse[j]
                acc = acc - factor * lines[j]
                for k in range(j + 1, SUBLANES):
                    entries[k] = entries[k] - factor * corner[j, k]
            top[i] = acc
        top[g] = t * lax.rsqrt(pivots)
    return jnp.concatenate(top, axis=0)[:, :PANEL]


def dot(a, b, dims):
    return lax.dot_general(a, b, (dims, ((), ())), precision=FULL, preferred_element_type=F32)


def factor_kernel(count, ids_ref, *refs):
    pieces, (ortho_t_ref, here_ref, whole_ref, work_ref) = refs[:count], refs[count:]
    rows, rank = pieces[0].shape
    for n, piece in enumerate(pieces):
        whole_ref[pl.ds(pl.multiple_of(ids_ref[n] * rows, SUBLANES), rows), :] = piece[...]
    total = count * rows

    work_ref[:, :rank] = jnp.zeros((rank, rank), F32)
    chunk = 4 * rows

    @pl.loop(0, total // chunk)
    def _(n):
        part = whole_ref[pl.ds(pl.multiple_of(n * chunk, SUBLANES), chunk), :]
        work_ref[:, :rank] += dot(part, part, ((0,), (0,)))

    line = lax.broadcasted_iota(jnp.int32, (rank, rank), 0)
    column = lax.broadcasted_iota(jnp.int32, (rank, rank), 1)
    work_ref[:, rank:] = jnp.where(line == column, 1.0, 0.0).astype(F32)
    eye = jnp.where(line == column, 1.0, 0.0).astype(F32)[:PANEL, :PANEL]
    for start in range(0, rank, PANEL):
        stop = start + PANEL
        diagonal = work_ref[start:stop, start:stop]
        small = eliminate(jnp.concatenate([eye, diagonal], axis=1))
        panel = dot(small, work_ref[start:stop, :], ((1,), (0,)))
        work_ref[start:stop, :] = panel
        if stop < rank:
            work_ref[stop:, :] -= dot(panel[:, stop:rank], panel, ((0,), (0,)))
    inverse = work_ref[:, rank:]
    here_ref[...] = dot(pieces[0][...], inverse, ((1,), (1,))).astype(BF16)
    for n in range(0, total, chunk):
        ortho_t_ref[:, n : n + chunk] = dot(
            inverse, whole_ref[n : n + chunk, :], ((1,), (1,))
        ).astype(BF16)


def factor_call(ids, pieces):
    count = len(pieces)
    rows, rank = pieces[0].shape
    total = count * rows
    vmem = pl.BlockSpec(memory_space=pltpu.VMEM)
    return pl.pallas_call(
        functools.partial(factor_kernel, count),
        in_specs=[pl.BlockSpec(memory_space=pltpu.SMEM)] + [vmem] * count,
        out_specs=[vmem, vmem],
        out_shape=[
            jax.ShapeDtypeStruct((rank, total), BF16),
            jax.ShapeDtypeStruct((rows, rank), BF16),
        ],
        scratch_shapes=[pltpu.VMEM((total, rank), F32), pltpu.VMEM((rank, 2 * rank), F32)],
        compiler_params=params(24),
        cost_estimate=cost(40 * total * rank * rank, total * rank * 6),
        name="factor",
    )(ids, *pieces)


def back_kernel(pieces, ids_ref, base_ref, ortho_t_ref, *refs):
    columns, (colsq_ref, *part_refs), whole_ref = refs[:pieces], refs[pieces:-1], refs[-1]
    rows = columns[0].shape[0]
    for n, piece in enumerate(columns):
        whole_ref[pl.ds(pl.multiple_of(ids_ref[n] * rows, 16), rows), :] = piece[...]
    back_t = jnp.dot(ortho_t_ref[...], whole_ref[...], preferred_element_type=F32)
    back = back_t.T.astype(BF16)
    start = 0
    for part_ref in part_refs:
        stop = start + part_ref.shape[0]
        part_ref[...] = back[start:stop]
        start = stop
    wide = back.astype(F32)
    colsq_ref[...] = jnp.sum(wide * wide, axis=0, keepdims=True)


def back_call(ids, base, ortho_t, columns, parts):
    rank, total = ortho_t.shape
    share = columns[0].shape[1]
    vmem = pl.BlockSpec(memory_space=pltpu.VMEM)
    return pl.pallas_call(
        functools.partial(back_kernel, len(columns)),
        in_specs=[pl.BlockSpec(memory_space=pltpu.SMEM)] + [vmem] * (2 + len(columns)),
        out_specs=[vmem] * (1 + len(parts)),
        out_shape=[jax.ShapeDtypeStruct((1, rank), F32)]
        + [jax.ShapeDtypeStruct((part, rank), BF16) for part in parts],
        scratch_shapes=[pltpu.VMEM((total, share), BF16)],
        compiler_params=params(24),
        cost_estimate=cost(2 * rank * total * share, total * share * 2),
        name="back",
    )(ids, base, ortho_t, *columns)


def output_kernel(share, first, factor, ids_ref, base_ref, ortho_ref, colsq_ref, *refs):
    piece_ref, *_, nm_ref, nb_ref, up_ref, nm_tile, nb_tile, up_tile, sems = refs
    count, full = nm_tile.shape[0], nm_tile.shape[2]
    cols = nm_ref.shape[1]
    scale = lax.rsqrt(colsq_ref[...] + 1e-06)
    ortho = ortho_ref[...]
    over = (((1,), (1,)), ((), ()))

    def copies(n, width):
        there = pl.ds(pl.multiple_of(ids_ref[n] * share + first, LANES), width)
        sides = (
            (nm_tile.at[n, :, :width], nm_ref.at[:, there]),
            (nb_tile.at[n, :width, :], nb_ref.at[there, :]),
            (up_tile.at[n, :, :width], up_ref.at[:, there]),
        )
        return [
            pltpu.make_async_copy(source, target, sems.at[n, which])
            for which, (source, target) in enumerate(sides)
        ]

    for n in range(count):

        def compute(width):
            there = pl.ds(pl.multiple_of(ids_ref[n] * share + first, LANES), width)
            back = piece_ref[n * full : n * full + width, :]
            unit = (back.astype(F32) * scale).astype(BF16)
            nb_tile[n, :width, :] = unit
            nm_tile[n, :, :width] = base_ref[:, there] - 0.05 * lax.dot_general(
                ortho, back, over, preferred_element_type=F32
            )
            up_tile[n, :, :width] = (
                factor * lax.dot_general(ortho, unit, over, preferred_element_type=F32)
            ).astype(BF16)
            for copy in copies(n, width):
                copy.start()

        by_width(ids_ref[n], cols, share, first, first + full, compute)

    for n in range(count):

        def wait(width):
            for copy in copies(n, width):
                copy.wait()

        by_width(ids_ref[n], cols, share, first, first + full, wait)


def output_call(ids, base, ortho, colsq, share, first, blocks, factor, previous):
    rows, cols = base.shape
    rank = ortho.shape[1]
    count = ids.shape[0]
    width = blocks.shape[0] // count
    previous = previous or ()
    vmem, hbm = pl.BlockSpec(memory_space=pltpu.VMEM), pl.BlockSpec(memory_space=pltpu.HBM)
    return pl.pallas_call(
        functools.partial(output_kernel, share, first, factor),
        in_specs=[pl.BlockSpec(memory_space=pltpu.SMEM)] + [vmem] * 4 + [hbm] * len(previous),
        out_specs=[hbm] * 3,
        out_shape=[
            jax.ShapeDtypeStruct((rows, cols), F32),
            jax.ShapeDtypeStruct((cols, rank), BF16),
            jax.ShapeDtypeStruct((rows, cols), BF16),
        ],
        scratch_shapes=[
            pltpu.VMEM((count, rows, width), F32),
            pltpu.VMEM((count, width, rank), BF16),
            pltpu.VMEM((count, rows, width), BF16),
            pltpu.SemaphoreType.DMA((count, 3)),
        ],
        input_output_aliases={5 + n: n for n in range(len(previous))},
        compiler_params=params(24),
        cost_estimate=cost(
            4 * rows * width * rank * count, count * width * (rows * 10 + rank * 4)
        ),
        name="outputs",
    )(ids, base, ortho, colsq, blocks, *previous)


def chip_at(position, chips):
    half = chips // 2
    return jnp.where(position < half, 2 * position, 2 * (chips - 1 - position) + 1)


def position_of(chip, chips):
    return jnp.where(chip % 2 == 0, chip // 2, chips - 1 - chip // 2)


def ring_order(chips):
    half = chips // 2
    return [2 * q for q in range(half)] + [2 * (chips - 1 - q) + 1 for q in range(half, chips)]


def ring_steps(count):
    order = ring_order(count // 2)
    after = dict(zip(order, order[1:] + order[:1]))
    up = [(2 * c + k, 2 * after[c] + k) for c in order for k in (0, 1)]
    return up, [(b, a) for a, b in up]


def swap_pairs(count):
    return [(n, n ^ 1) for n in range(count)]


def tie(x, *work):
    return lax.optimization_barrier((x, *work))[0] if work else x


def exchange_windows(count):
    if count != 16:
        far = [[k + count // 2] + [k] * (k > 0) for k in range(count // 2)]
        steps = count // 4 + 1
        return far[:steps] + [sum(far[steps:], [])]
    return [[8, 4], [9, 5], [10, 6], [11, 7], [12, 1, 2, 3], [13, 14, 15]]


def gather_and_exchange(sketch, outgoing, count):
    chips = count // 2
    me = lax.axis_index("fsdp")
    place, core = position_of(me // 2, chips), me % 2
    up, down = ring_steps(count)
    columns = {0: outgoing[0]}

    def exchange(window, *after):
        for k in window:
            pairs = [(n, n ^ k) for n in range(count)]
            columns[k] = lax.ppermute(tie(outgoing[k], *after), "fsdp", pairs)

    windows = exchange_windows(count)
    swap = swap_pairs(count)
    exchange(windows[0], sketch)
    sketch = sketch + lax.ppermute(sketch, "tp", [(0, 1), (1, 0)])
    offsets, held, other = [0], [sketch], []
    ahead = behind = sketch
    arrived, earlier = [sketch], []
    for step in range(1, chips // 2 + 1):
        work = [columns[k] for k in windows[step - 2]] if step > 1 else []
        ahead, behind, *_ = lax.optimization_barrier((ahead, behind, *work, *earlier))
        exchange(windows[step], ahead, behind)
        earlier = [lax.ppermute(x, "fsdp", swap) for x in arrived]
        other += earlier
        ahead = lax.ppermute(ahead, "fsdp", up)
        arrived = [ahead]
        offsets.append(-step)
        if 2 * step < chips:
            behind = lax.ppermute(behind, "fsdp", down)
            arrived.append(behind)
            offsets.append(step)
        held += arrived
    for window in windows[chips // 2 + 1 :]:
        exchange(window, ahead, behind)
    other += [lax.ppermute(x, "fsdp", swap) for x in arrived]
    chip = chip_at((place + jnp.array(offsets, jnp.int32)) % chips, chips)
    ids = jnp.concatenate([2 * chip + core, 2 * chip + 1 - core])
    return held + other, ids.astype(jnp.int32), [columns[k] for k in range(count)]


def sum_rounds(count):
    rounds, bit = [("tp", [1])], 1
    while bit < count:
        rounds.append(("fsdp", [bit, 2 * bit, 3 * bit] if 2 * bit < count else [bit]))
        bit *= 4
    return rounds


def sum_round(x, axis, distances):
    size = lax.axis_size(axis)
    terms = [x]
    for d in distances:
        terms.append(lax.ppermute(x, axis, [(n, n ^ d) for n in range(size)]))
    if len(terms) == 2:
        return terms[0] + terms[1]
    return (terms[0] + terms[1]) + (terms[2] + terms[3])


def local(momentum, gradient, basis):
    rows, cols = momentum.shape
    rank = basis.shape[1]
    count = lax.axis_size("fsdp")
    tp_count = lax.axis_size("tp")
    chips = count // 2
    share = -(-cols // (count * LANES)) * LANES
    factor = math.sqrt(rows * count * cols * tp_count / rank)
    me = lax.axis_index("fsdp")
    ring = tp_count == 2 and count in (4, 8, 16, 32) and (count - 1) * share < cols

    base = momentum + gradient.astype(F32)
    base_b = base.astype(BF16)
    sketch = jnp.dot(base_b, basis, preferred_element_type=F32)
    base = pltpu.with_memory_space_constraint(base, pltpu.VMEM)
    if ring:
        partners = me ^ jnp.arange(count, dtype=jnp.int32)
        outgoing = pack_call(partners, base, share)
        pieces, ids, columns = gather_and_exchange(sketch, outgoing, count)
    else:
        padded = jnp.pad(base_b, ((0, 0), (0, share * count - cols)))
        outgoing = jnp.swapaxes(padded.reshape(rows, count, share), 0, 1)
        columns = lax.all_to_all(outgoing, "fsdp", 0, 0, tiled=True)
        columns = [columns.reshape(rows * count, share)]
        partners = jnp.zeros((1,), jnp.int32)
        whole = lax.all_gather(lax.psum(sketch, "tp"), "fsdp", axis=0)
        pieces = [lax.dynamic_index_in_dim(whole, (me + n) % count, 0, False) for n in range(count)]
        ids = ((me + jnp.arange(count)) % count).astype(jnp.int32)
    ortho_t, ortho_here = factor_call(ids, pieces)
    tiles = share // LANES
    cuts = [share]
    if ring and tiles > 1:
        cuts = [share - tiles // 2 * LANES, tiles // 2 * LANES]
    part, *back = back_call(partners, base, ortho_t, columns, cuts)

    if ring:
        groups = [list(range(core, count, 2)) for core in (0, 1)]
        colsq = part
        for axis, distances in sum_rounds(count):
            colsq = sum_round(colsq, axis, distances)
        chip = 2 * jnp.arange(chips, dtype=jnp.int32)
        owners = [chip + me % 2, chip + 1 - me % 2]
    else:
        colsq = lax.psum(part, ("fsdp", "tp"))
        owners = [jnp.arange(-(-cols // share), dtype=jnp.int32)]
    result, first = None, 0
    for piece in back:
        if ring:
            mine = lax.all_gather(piece, "fsdp", axis=0, tiled=True, axis_index_groups=groups)
            mine = tie(mine, *(result or (colsq,)))
            gathered = [mine, lax.ppermute(mine, "fsdp", swap_pairs(count))]
        else:
            gathered = [lax.all_gather(piece, "fsdp", axis=0, tiled=True)[: owners[0].size * share]]
        for ids, blocks in zip(owners, gathered):
            result = output_call(
                ids, base, ortho_here, colsq, share, first, blocks, factor, result
            )
        first += piece.shape[0]
    return tuple(result)


def solution(mesh):
    return jax.shard_map(
        local,
        mesh=mesh,
        in_specs=(P("fsdp", "tp"), P("fsdp", "tp"), P("tp", None)),
        out_specs=(P("fsdp", "tp"), P("tp", None), P("fsdp", "tp")),
        check_vma=False,
    )
```

```python
import functools
import math

import jax
import jax.numpy as jnp
from jax import lax
from jax.experimental import pallas as pl
from jax.experimental.pallas import tpu as pltpu
from jax.sharding import PartitionSpec as P

LANES = 128
SUBLANES = 8
PANEL = 64
MIB = 1024 * 1024
FULL = lax.Precision.HIGHEST
F32 = jnp.float32
BF16 = jnp.bfloat16


def cost(flops, nbytes):
    return pl.CostEstimate(flops=flops, bytes_accessed=nbytes, transcendentals=0)


def params(mib):
    return pltpu.CompilerParams(vmem_limit_bytes=mib * MIB)


def by_width(block, cols, share, start, stop, act):
    last = (cols - 1) // share
    width, short = stop - start, max(0, min(cols - last * share, stop) - start)
    if short == width:
        act(width)
        return

    @pl.when(block < last)
    def _():
        act(width)

    if short:

        @pl.when(block == last)
        def _():
            act(short)


def pack_kernel(ids_ref, base_ref, *out_refs):
    cols = base_ref.shape[1]
    for n, out_ref in enumerate(out_refs):
        share = out_ref.shape[1]
        start = pl.multiple_of(ids_ref[n] * share, LANES)

        def fill(width):
            out_ref[:, :width] = base_ref[:, pl.ds(start, width)].astype(BF16)
            if width < share:
                out_ref[:, width:] = jnp.zeros((out_ref.shape[0], share - width), BF16)

        by_width(ids_ref[n], cols, share, 0, share, fill)


def pack_call(ids, base, share):
    rows = base.shape[0]
    count = ids.shape[0]
    vmem = pl.BlockSpec(memory_space=pltpu.VMEM)
    return pl.pallas_call(
        pack_kernel,
        in_specs=[pl.BlockSpec(memory_space=pltpu.SMEM), vmem],
        out_specs=[vmem] * count,
        out_shape=[jax.ShapeDtypeStruct((rows, share), BF16)] * count,
        compiler_params=params(16),
        cost_estimate=cost(0, 6 * rows * share * count),
        name="pack",
    )(ids, base)


def spread(x, lane):
    return jnp.broadcast_to(x[:, lane : lane + 1], (x.shape[0], LANES))


def row_of(x, row):
    return jnp.broadcast_to(x[row : row + 1, :], (SUBLANES, LANES))


def eliminate(block):
    sub = lax.broadcasted_iota(jnp.int32, (SUBLANES, LANES), 0)
    groups = PANEL // SUBLANES
    top = [block[SUBLANES * g : SUBLANES * (g + 1)] for g in range(groups)]
    for g in range(groups):
        first = PANEL + SUBLANES * g
        t = top[g]
        cols = [spread(t, first + j) for j in range(SUBLANES)]
        below = [[spread(top[i], first + j) for j in range(SUBLANES)] for i in range(g + 1, groups)]
        pivots = jnp.zeros((SUBLANES, LANES), F32)
        inverse, corner = [], {}
        for j in range(SUBLANES):
            pivot = row_of(cols[j], j)
            pivots = jnp.where(sub == j, pivot, pivots)
            inverse.append(1.0 / pivot)
            factor = jnp.where(sub > j, cols[j] * inverse[j], 0.0)
            t = t - factor * row_of(t, j)
            for k in range(j + 1, SUBLANES):
                corner[j, k] = row_of(cols[k], j)
                cols[k] = cols[k] - factor * corner[j, k]
        lines = [row_of(t, j) for j in range(SUBLANES)]
        for i in range(g + 1, groups):
            entries = below[i - g - 1]
            acc = top[i]
            for j in range(SUBLANES):
                factor = entries[j] * inverse[j]
                acc = acc - factor * lines[j]
                for k in range(j + 1, SUBLANES):
                    entries[k] = entries[k] - factor * corner[j, k]
            top[i] = acc
        top[g] = t * lax.rsqrt(pivots)
    return jnp.concatenate(top, axis=0)[:, :PANEL]


def dot(a, b, dims):
    return lax.dot_general(a, b, (dims, ((), ())), precision=FULL, preferred_element_type=F32)


def factor_kernel(count, ids_ref, base_ref, *refs):
    pieces, (ortho_t_ref, here_ref, whole_ref, work_ref, corner_ref) = refs[:count], refs[count:]
    corner_ref[...] = base_ref[:SUBLANES, :LANES]
    rows, rank = pieces[0].shape
    for n, piece in enumerate(pieces):
        whole_ref[pl.ds(pl.multiple_of(ids_ref[n] * rows, SUBLANES), rows), :] = piece[...]
    total = count * rows

    work_ref[:, :rank] = jnp.zeros((rank, rank), F32)
    chunk = 4 * rows

    @pl.loop(0, total // chunk)
    def _(n):
        part = whole_ref[pl.ds(pl.multiple_of(n * chunk, SUBLANES), chunk), :]
        work_ref[:, :rank] += dot(part, part, ((0,), (0,)))

    line = lax.broadcasted_iota(jnp.int32, (rank, rank), 0)
    column = lax.broadcasted_iota(jnp.int32, (rank, rank), 1)
    work_ref[:, rank:] = jnp.where(line == column, 1.0, 0.0).astype(F32)
    eye = jnp.where(line == column, 1.0, 0.0).astype(F32)[:PANEL, :PANEL]
    for start in range(0, rank, PANEL):
        stop = start + PANEL
        diagonal = work_ref[start:stop, start:stop]
        small = eliminate(jnp.concatenate([eye, diagonal], axis=1))
        panel = dot(small, work_ref[start:stop, :], ((1,), (0,)))
        work_ref[start:stop, :] = panel
        if stop < rank:
            work_ref[stop:, :] -= dot(panel[:, stop:rank], panel, ((0,), (0,)))
    inverse = work_ref[:, rank:]
    here_ref[...] = dot(pieces[0][...], inverse, ((1,), (1,))).astype(BF16)
    for n in range(0, total, chunk):
        ortho_t_ref[:, n : n + chunk] = dot(
            inverse, whole_ref[n : n + chunk, :], ((1,), (1,))
        ).astype(BF16)


def factor_call(ids, base, pieces):
    count = len(pieces)
    rows, rank = pieces[0].shape
    total = count * rows
    vmem = pl.BlockSpec(memory_space=pltpu.VMEM)
    return pl.pallas_call(
        functools.partial(factor_kernel, count),
        in_specs=[pl.BlockSpec(memory_space=pltpu.SMEM)] + [vmem] * (1 + count),
        out_specs=[vmem, vmem],
        out_shape=[
            jax.ShapeDtypeStruct((rank, total), BF16),
            jax.ShapeDtypeStruct((rows, rank), BF16),
        ],
        scratch_shapes=[
            pltpu.VMEM((total, rank), F32),
            pltpu.VMEM((rank, 2 * rank), F32),
            pltpu.VMEM((SUBLANES, LANES), F32),
        ],
        compiler_params=params(24),
        cost_estimate=cost(40 * total * rank * rank, total * rank * 6),
        name="factor",
    )(ids, base, *pieces)


def back_kernel(pieces, ids_ref, base_ref, ortho_t_ref, *refs):
    columns, (colsq_ref, back_ref, whole_ref, corner_ref) = refs[:pieces], refs[pieces:]
    corner_ref[...] = base_ref[:SUBLANES, :LANES]
    rows = columns[0].shape[0]
    for n, piece in enumerate(columns):
        whole_ref[pl.ds(pl.multiple_of(ids_ref[n] * rows, 16), rows), :] = piece[...]
    back_t = jnp.dot(ortho_t_ref[...], whole_ref[...], preferred_element_type=F32)
    back = back_t.T.astype(BF16)
    back_ref[...] = back
    wide = back.astype(F32)
    colsq_ref[...] = jnp.sum(wide * wide, axis=0, keepdims=True)


def back_call(ids, base, ortho_t, columns):
    rank, total = ortho_t.shape
    share = columns[0].shape[1]
    vmem = pl.BlockSpec(memory_space=pltpu.VMEM)
    return pl.pallas_call(
        functools.partial(back_kernel, len(columns)),
        in_specs=[pl.BlockSpec(memory_space=pltpu.SMEM)] + [vmem] * (2 + len(columns)),
        out_specs=[vmem] * 2,
        out_shape=[
            jax.ShapeDtypeStruct((1, rank), F32),
            jax.ShapeDtypeStruct((share, rank), BF16),
        ],
        scratch_shapes=[pltpu.VMEM((total, share), BF16), pltpu.VMEM((SUBLANES, LANES), F32)],
        compiler_params=params(24),
        cost_estimate=cost(2 * rank * total * share, total * share * 2),
        name="back",
    )(ids, base, ortho_t, *columns)


def output_kernel(places, factor, ids_ref, base_ref, ortho_ref, colsq_ref, *refs):
    *pieces, nm_ref, nb_ref, up_ref, nm_tile, nb_tile, up_tile, sems = refs
    count, share, cols = nm_tile.shape[0], nm_tile.shape[2], nm_ref.shape[1]
    scale = lax.rsqrt(colsq_ref[...] + 1e-06)
    ortho = ortho_ref[...]
    over = (((1,), (1,)), ((), ()))

    def copies(n, width):
        there = pl.ds(pl.multiple_of(ids_ref[places[n]] * share, LANES), width)
        sides = (
            (nm_tile.at[n, :, :width], nm_ref.at[:, there]),
            (nb_tile.at[n, :width, :], nb_ref.at[there, :]),
            (up_tile.at[n, :, :width], up_ref.at[:, there]),
        )
        return [
            pltpu.make_async_copy(source, target, sems.at[n, which])
            for which, (source, target) in enumerate(sides)
        ]

    for n in range(count):

        def compute(width):
            there = pl.ds(pl.multiple_of(ids_ref[places[n]] * share, LANES), width)
            back = pieces[n][:width, :]
            unit = (back.astype(F32) * scale).astype(BF16)
            nb_tile[n, :width, :] = unit
            nm_tile[n, :, :width] = base_ref[:, there] - 0.05 * lax.dot_general(
                ortho, back, over, preferred_element_type=F32
            )
            up_tile[n, :, :width] = (
                factor * lax.dot_general(ortho, unit, over, preferred_element_type=F32)
            ).astype(BF16)
            for copy in copies(n, width):
                copy.start()

        by_width(ids_ref[places[n]], cols, share, 0, share, compute)

    for n in range(count):

        def wait(width):
            for copy in copies(n, width):
                copy.wait()

        by_width(ids_ref[places[n]], cols, share, 0, share, wait)


def output_call(ids, places, blocks, colsq, previous, base, ortho, factor):
    rows, cols = base.shape
    share, rank = blocks[0].shape
    count = len(blocks)
    previous = previous or ()
    vmem, hbm = pl.BlockSpec(memory_space=pltpu.VMEM), pl.BlockSpec(memory_space=pltpu.HBM)
    return pl.pallas_call(
        functools.partial(output_kernel, tuple(places), factor),
        in_specs=[pl.BlockSpec(memory_space=pltpu.SMEM)]
        + [vmem] * (3 + count)
        + [hbm] * len(previous),
        out_specs=[hbm] * 3,
        out_shape=[
            jax.ShapeDtypeStruct((rows, cols), F32),
            jax.ShapeDtypeStruct((cols, rank), BF16),
            jax.ShapeDtypeStruct((rows, cols), BF16),
        ],
        scratch_shapes=[
            pltpu.VMEM((count, rows, share), F32),
            pltpu.VMEM((count, share, rank), BF16),
            pltpu.VMEM((count, rows, share), BF16),
            pltpu.SemaphoreType.DMA((count, 3)),
        ],
        input_output_aliases={4 + count + n: n for n in range(len(previous))},
        compiler_params=params(16),
        cost_estimate=cost(
            4 * rows * share * rank * count, count * share * (rows * 10 + rank * 4)
        ),
        name="outputs",
    )(ids, base, ortho, colsq, *blocks, *previous)


def chip_at(position, chips):
    half = chips // 2
    return jnp.where(position < half, 2 * position, 2 * (chips - 1 - position) + 1)


def position_of(chip, chips):
    return jnp.where(chip % 2 == 0, chip // 2, chips - 1 - chip // 2)


def ring_order(chips):
    half = chips // 2
    return [2 * q for q in range(half)] + [2 * (chips - 1 - q) + 1 for q in range(half, chips)]


def ring_steps(count):
    order = ring_order(count // 2)
    after = dict(zip(order, order[1:] + order[:1]))
    up = [(2 * c + k, 2 * after[c] + k) for c in order for k in (0, 1)]
    down = [(b, a) for a, b in up]
    first = [p for p in up if p[0] % 2 == 0] + [p for p in down if p[0] % 2 == 1]
    second = [p for p in down if p[0] % 2 == 0] + [p for p in up if p[0] % 2 == 1]
    return first, second


def owners(hops, count):
    me = lax.axis_index("fsdp")
    chips, core = count // 2, me % 2
    hops = hops * (2 * core - 1)
    place = position_of(me // 2, chips)
    mine = 2 * chip_at((place + hops) % chips, chips) + core
    theirs = 2 * chip_at((place - hops) % chips, chips) + 1 - core
    return jnp.stack([mine, theirs], axis=1).astype(jnp.int32)


def swap_pairs(count):
    return [(n, n ^ 1) for n in range(count)]


def tie(x, *work):
    return lax.optimization_barrier((x, *work))[0] if work else x


def exchange_windows(count):
    if count != 16:
        far = [[k + count // 2] + [k] * (k > 0) for k in range(count // 2)]
        steps = count // 4 + 1
        return far[:steps] + [sum(far[steps:], [])]
    return [[8, 4], [9, 5], [10, 6], [11, 7], [12, 1, 2, 3], [13, 14, 15]]


def gather_and_exchange(sketch, outgoing, count):
    chips = count // 2
    me = lax.axis_index("fsdp")
    first, second = ring_steps(count)
    columns = {0: outgoing[0]}

    def exchange(window, *after):
        for k in window:
            pairs = [(n, n ^ k) for n in range(count)]
            columns[k] = lax.ppermute(tie(outgoing[k], *after), "fsdp", pairs)

    windows = exchange_windows(count)
    swap = swap_pairs(count)
    exchange(windows[0], sketch)
    sketch = sketch + lax.ppermute(sketch, "tp", [(0, 1), (1, 0)])
    offsets, held, other = [0], [sketch], []
    ahead = behind = sketch
    arrived, earlier = [sketch], []
    for step in range(1, chips // 2 + 1):
        work = [columns[k] for k in windows[step - 2]] if step > 1 else []
        ahead, behind, *_ = lax.optimization_barrier((ahead, behind, *work, *earlier))
        exchange(windows[step], ahead, behind)
        earlier = [lax.ppermute(x, "fsdp", swap) for x in arrived]
        other += earlier
        ahead = lax.ppermute(ahead, "fsdp", first)
        arrived = [ahead]
        offsets.append(step)
        if 2 * step < chips:
            behind = lax.ppermute(behind, "fsdp", second)
            arrived.append(behind)
            offsets.append(-step)
        held += arrived
    for window in windows[chips // 2 + 1 :]:
        exchange(window, ahead, behind)
    other += [lax.ppermute(x, "fsdp", swap) for x in arrived]
    ids = owners(jnp.array(offsets, jnp.int32), count)
    ids = jnp.concatenate([ids[:, 0], ids[:, 1]])
    return held + other, ids.astype(jnp.int32), [columns[k] for k in range(count)]


def sum_rounds(count):
    rounds, bit = [("tp", [1])], 1
    while bit < count:
        rounds.append(("fsdp", [bit, 2 * bit, 3 * bit] if 2 * bit < count else [bit]))
        bit *= 4
    return rounds


def sum_round(x, axis, distances):
    size = lax.axis_size(axis)
    terms = [x]
    for d in distances:
        terms.append(lax.ppermute(x, axis, [(n, n ^ d) for n in range(size)]))
    if len(terms) == 2:
        return terms[0] + terms[1]
    return (terms[0] + terms[1]) + (terms[2] + terms[3])


def local(momentum, gradient, basis):
    rows, cols = momentum.shape
    rank = basis.shape[1]
    count = lax.axis_size("fsdp")
    tp_count = lax.axis_size("tp")
    chips = count // 2
    share = -(-cols // (count * LANES)) * LANES
    factor = math.sqrt(rows * count * cols * tp_count / rank)
    me = lax.axis_index("fsdp")
    ring = tp_count == 2 and count in (4, 8, 16, 32) and (count - 1) * share < cols

    base = momentum + gradient.astype(F32)
    base_b = base.astype(BF16)
    sketch = jnp.dot(base_b, basis, preferred_element_type=F32)
    base = pltpu.with_memory_space_constraint(base, pltpu.VMEM)
    if ring:
        partners = me ^ jnp.arange(count, dtype=jnp.int32)
        outgoing = pack_call(partners, base, share)
        pieces, ids, columns = gather_and_exchange(sketch, outgoing, count)
    else:
        padded = jnp.pad(base_b, ((0, 0), (0, share * count - cols)))
        outgoing = jnp.swapaxes(padded.reshape(rows, count, share), 0, 1)
        columns = lax.all_to_all(outgoing, "fsdp", 0, 0, tiled=True)
        columns = [columns.reshape(rows * count, share)]
        partners = jnp.zeros((1,), jnp.int32)
        whole = lax.all_gather(lax.psum(sketch, "tp"), "fsdp", axis=0)
        pieces = [lax.dynamic_index_in_dim(whole, (me + n) % count, 0, False) for n in range(count)]
        ids = ((me + jnp.arange(count)) % count).astype(jnp.int32)
    ortho_t, ortho_here = factor_call(ids, base, pieces)
    part, back = back_call(partners, base, ortho_t, columns)
    write = functools.partial(output_call, base=base, ortho=ortho_here, factor=factor)
    if not ring:
        whole = lax.all_gather(back, "fsdp", axis=0)
        valid = -(-cols // share)
        colsq, blocks = lax.psum(part, ("fsdp", "tp")), [whole[n] for n in range(valid)]
        return tuple(
            write(jnp.arange(valid, dtype=jnp.int32), range(valid), blocks, colsq, None)
        )

    turns, swap = ring_steps(count), swap_pairs(count)
    hops = [0] + [h * sign for h in range(1, chips // 2 + 1) for sign in (1, -1)][: chips - 1]
    ids = owners(jnp.array(hops, jnp.int32), count)
    write = functools.partial(write, ids.reshape(-1))
    rounds = sum_rounds(count)
    colsq, result, waiting = part, None, ()
    arrived, blocks, written = {0: back}, [], 0
    for n in range(chips):
        block = tie(arrived[n], *waiting)
        waiting = ()
        for later in (1, 2) if n == 0 else (n + 2,):
            if later < chips:
                arrived[later] = lax.ppermute(block, "fsdp", turns[(later + 1) % 2])
        blocks += [block, lax.ppermute(block, "fsdp", swap)]
        for _ in range(2 if n == 0 else 1):
            if rounds:
                colsq = sum_round(tie(colsq, block), *rounds.pop(0))
                waiting = (colsq,)
        ready = 2 * n if n + 1 < chips else 2 * n + 1
        if n >= 2 and ready >= written + 3:
            result = write(range(written, ready), blocks[written:ready], colsq, result)
            written, waiting = ready, tuple(result)
    return tuple(write(range(written, 2 * chips), blocks[written:], colsq, result))


def solution(mesh):
    return jax.shard_map(
        local,
        mesh=mesh,
        in_specs=(P("fsdp", "tp"), P("fsdp", "tp"), P("tp", None)),
        out_specs=(P("fsdp", "tp"), P("tp", None), P("fsdp", "tp")),
        check_vma=False,
    )
```

```python
import functools
import math

import jax
import jax.numpy as jnp
from jax import lax
from jax.experimental import pallas as pl
from jax.experimental.pallas import tpu as pltpu
from jax.sharding import PartitionSpec as P

LANES = 128
SUBLANES = 8
PANEL = 64
MIB = 1024 * 1024
FULL = lax.Precision.HIGHEST
F32 = jnp.float32
BF16 = jnp.bfloat16


def cost(flops, nbytes):
    return pl.CostEstimate(flops=flops, bytes_accessed=nbytes, transcendentals=0)


def params(mib):
    return pltpu.CompilerParams(vmem_limit_bytes=mib * MIB)


def by_width(block, cols, share, start, stop, act):
    last = (cols - 1) // share
    width, short = stop - start, max(0, min(cols - last * share, stop) - start)
    if short == width:
        act(width)
        return

    @pl.when(block < last)
    def _():
        act(width)

    if short:

        @pl.when(block == last)
        def _():
            act(short)


def pack_kernel(me_ref, base_ref, near_ref, *far_refs):
    cols = base_ref.shape[1]
    group = near_ref.shape[0]
    share = near_ref.shape[2]
    me = me_ref[0]
    first = me & ~(group - 1)
    near = [(first + n, near_ref.at[n]) for n in range(group)]
    far = [(me ^ (group + n), ref) for n, ref in enumerate(far_refs)]
    for owner, out_ref in near + far:

        def fill(width):
            start = pl.multiple_of(owner * share, LANES)
            out_ref[:, :width] = base_ref[:, pl.ds(start, width)].astype(BF16)
            if width < share:
                out_ref[:, width:] = jnp.zeros((out_ref.shape[0], share - width), BF16)

        by_width(owner, cols, share, 0, share, fill)


def pack_call(me, base, share, count):
    rows, half = base.shape[0], count // 2
    vmem = pl.BlockSpec(memory_space=pltpu.VMEM)
    return pl.pallas_call(
        pack_kernel,
        in_specs=[pl.BlockSpec(memory_space=pltpu.SMEM), vmem],
        out_specs=[vmem] * (1 + half),
        out_shape=[jax.ShapeDtypeStruct((half, rows, share), BF16)]
        + [jax.ShapeDtypeStruct((rows, share), BF16)] * half,
        compiler_params=params(16),
        cost_estimate=cost(0, 6 * rows * share * count),
        name="pack",
    )(me, base)


def spread(x, lane):
    return jnp.broadcast_to(x[:, lane : lane + 1], (x.shape[0], LANES))


def row_of(x, row):
    return jnp.broadcast_to(x[row : row + 1, :], (SUBLANES, LANES))


def eliminate(block):
    sub = lax.broadcasted_iota(jnp.int32, (SUBLANES, LANES), 0)
    groups = PANEL // SUBLANES
    top = [block[SUBLANES * g : SUBLANES * (g + 1)] for g in range(groups)]
    for g in range(groups):
        first = PANEL + SUBLANES * g
        t = top[g]
        cols = [spread(t, first + j) for j in range(SUBLANES)]
        below = [[spread(top[i], first + j) for j in range(SUBLANES)] for i in range(g + 1, groups)]
        pivots = jnp.zeros((SUBLANES, LANES), F32)
        inverse, corner = [], {}
        for j in range(SUBLANES):
            pivot = row_of(cols[j], j)
            pivots = jnp.where(sub == j, pivot, pivots)
            inverse.append(1.0 / pivot)
            factor = jnp.where(sub > j, cols[j] * inverse[j], 0.0)
            t = t - factor * row_of(t, j)
            for k in range(j + 1, SUBLANES):
                corner[j, k] = row_of(cols[k], j)
                cols[k] = cols[k] - factor * corner[j, k]
        lines = [row_of(t, j) for j in range(SUBLANES)]
        for i in range(g + 1, groups):
            entries = below[i - g - 1]
            acc = top[i]
            for j in range(SUBLANES):
                factor = entries[j] * inverse[j]
                acc = acc - factor * lines[j]
                for k in range(j + 1, SUBLANES):
                    entries[k] = entries[k] - factor * corner[j, k]
            top[i] = acc
        top[g] = t * lax.rsqrt(pivots)
    return jnp.concatenate(top, axis=0)[:, :PANEL]


def dot(a, b, dims):
    return lax.dot_general(a, b, (dims, ((), ())), precision=FULL, preferred_element_type=F32)


def factor_kernel(stacks, owner, me_ref, base_ref, *refs):
    stacked, (ortho_t_ref, here_ref, whole_ref, work_ref, corner_ref) = refs[:stacks], refs[stacks:]
    corner_ref[...] = base_ref[:SUBLANES, :LANES]
    rows, rank = here_ref.shape
    total = whole_ref.shape[0]
    pieces = [stack.at[n] for stack in stacked for n in range(stack.shape[0])]
    for n, piece in enumerate(pieces):
        start = pl.multiple_of(owner(me_ref[0], n) * rows, SUBLANES)
        whole_ref[pl.ds(start, rows), :] = piece[...]

    work_ref[:, :rank] = jnp.zeros((rank, rank), F32)
    chunk = 4 * rows

    @pl.loop(0, total // chunk)
    def _(n):
        part = whole_ref[pl.ds(pl.multiple_of(n * chunk, SUBLANES), chunk), :]
        work_ref[:, :rank] += dot(part, part, ((0,), (0,)))

    line = lax.broadcasted_iota(jnp.int32, (rank, rank), 0)
    column = lax.broadcasted_iota(jnp.int32, (rank, rank), 1)
    work_ref[:, rank:] = jnp.where(line == column, 1.0, 0.0).astype(F32)
    eye = jnp.where(line == column, 1.0, 0.0).astype(F32)[:PANEL, :PANEL]
    for start in range(0, rank, PANEL):
        stop = start + PANEL
        diagonal = work_ref[start:stop, start:stop]
        small = eliminate(jnp.concatenate([eye, diagonal], axis=1))
        panel = dot(small, work_ref[start:stop, :], ((1,), (0,)))
        work_ref[start:stop, :] = panel
        if stop < rank:
            work_ref[stop:, :] -= dot(panel[:, stop:rank], panel, ((0,), (0,)))
    inverse = work_ref[:, rank:]
    start = pl.multiple_of(me_ref[0] * rows, SUBLANES)
    here_ref[...] = dot(whole_ref[pl.ds(start, rows), :], inverse, ((1,), (1,))).astype(BF16)
    for n in range(0, total, chunk):
        ortho_t_ref[:, n : n + chunk] = dot(
            inverse, whole_ref[n : n + chunk, :], ((1,), (1,))
        ).astype(BF16)


def factor_call(me, owner, base, stacked):
    _, rows, rank = stacked[0].shape
    total = rows * sum(stack.shape[0] for stack in stacked)
    vmem = pl.BlockSpec(memory_space=pltpu.VMEM)
    return pl.pallas_call(
        functools.partial(factor_kernel, len(stacked), owner),
        in_specs=[pl.BlockSpec(memory_space=pltpu.SMEM)] + [vmem] * (1 + len(stacked)),
        out_specs=[vmem, vmem],
        out_shape=[
            jax.ShapeDtypeStruct((rank, total), BF16),
            jax.ShapeDtypeStruct((rows, rank), BF16),
        ],
        scratch_shapes=[
            pltpu.VMEM((total, rank), F32),
            pltpu.VMEM((rank, 2 * rank), F32),
            pltpu.VMEM((SUBLANES, LANES), F32),
        ],
        compiler_params=params(24),
        cost_estimate=cost(40 * total * rank * rank, total * rank * 6),
        name="factor",
    )(me, base, *stacked)


def back_kernel(me_ref, base_ref, ortho_t_ref, near_ref, *refs):
    *far, colsq_ref, back_ref, whole_ref, corner_ref = refs
    corner_ref[...] = base_ref[:SUBLANES, :LANES]
    group, rows, _ = near_ref.shape
    me = me_ref[0]
    first = me & ~(group - 1) if far else 0
    pieces = [(first + n, near_ref.at[n]) for n in range(group)]
    pieces += [(me ^ (group + n), ref) for n, ref in enumerate(far)]
    for owner, piece in pieces:
        whole_ref[pl.ds(pl.multiple_of(owner * rows, 16), rows), :] = piece[...]
    back_t = jnp.dot(ortho_t_ref[...], whole_ref[...], preferred_element_type=F32)
    back = back_t.T.astype(BF16)
    back_ref[...] = back
    wide = back.astype(F32)
    colsq_ref[...] = jnp.sum(wide * wide, axis=0, keepdims=True)


def back_call(me, base, ortho_t, near, far):
    rank, total = ortho_t.shape
    share = near.shape[2]
    vmem = pl.BlockSpec(memory_space=pltpu.VMEM)
    return pl.pallas_call(
        back_kernel,
        in_specs=[pl.BlockSpec(memory_space=pltpu.SMEM)] + [vmem] * (3 + len(far)),
        out_specs=[vmem] * 2,
        out_shape=[
            jax.ShapeDtypeStruct((1, rank), F32),
            jax.ShapeDtypeStruct((share, rank), BF16),
        ],
        scratch_shapes=[pltpu.VMEM((total, share), BF16), pltpu.VMEM((SUBLANES, LANES), F32)],
        compiler_params=params(24),
        cost_estimate=cost(2 * rank * total * share, total * share * 2),
        name="back",
    )(me, base, ortho_t, near, *far)


def output_kernel(owner, factor, me_ref, base_ref, ortho_ref, colsq_ref, *refs):
    *pieces, nm_ref, nb_ref, up_ref, nm_tile, nb_tile, up_tile, sems = refs
    count, share, cols = nm_tile.shape[0], nm_tile.shape[2], nm_ref.shape[1]
    scale = lax.rsqrt(colsq_ref[...] + 1e-06)
    ortho = ortho_ref[...]
    over = (((1,), (1,)), ((), ()))

    def copies(n, width):
        there = pl.ds(pl.multiple_of(owner(me_ref[0], n) * share, LANES), width)
        sides = (
            (nm_tile.at[n, :, :width], nm_ref.at[:, there]),
            (nb_tile.at[n, :width, :], nb_ref.at[there, :]),
            (up_tile.at[n, :, :width], up_ref.at[:, there]),
        )
        return [
            pltpu.make_async_copy(source, target, sems.at[n, which])
            for which, (source, target) in enumerate(sides)
        ]

    for n in range(count):

        def compute(width):
            there = pl.ds(pl.multiple_of(owner(me_ref[0], n) * share, LANES), width)
            back = pieces[n][:width, :]
            unit = (back.astype(F32) * scale).astype(BF16)
            nb_tile[n, :width, :] = unit
            nm_tile[n, :, :width] = base_ref[:, there] - 0.05 * lax.dot_general(
                ortho, back, over, preferred_element_type=F32
            )
            up_tile[n, :, :width] = (
                factor * lax.dot_general(ortho, unit, over, preferred_element_type=F32)
            ).astype(BF16)
            for copy in copies(n, width):
                copy.start()

        by_width(owner(me_ref[0], n), cols, share, 0, share, compute)

    for n in range(count):

        def wait(width):
            for copy in copies(n, width):
                copy.wait()

        by_width(owner(me_ref[0], n), cols, share, 0, share, wait)


def output_call(owner, blocks, colsq, previous, me, base, ortho, factor):
    rows, cols = base.shape
    share, rank = blocks[0].shape
    count = len(blocks)
    previous = previous or ()
    vmem, hbm = pl.BlockSpec(memory_space=pltpu.VMEM), pl.BlockSpec(memory_space=pltpu.HBM)
    return pl.pallas_call(
        functools.partial(output_kernel, owner, factor),
        in_specs=[pl.BlockSpec(memory_space=pltpu.SMEM)]
        + [vmem] * (3 + count)
        + [hbm] * len(previous),
        out_specs=[hbm] * 3,
        out_shape=[
            jax.ShapeDtypeStruct((rows, cols), F32),
            jax.ShapeDtypeStruct((cols, rank), BF16),
            jax.ShapeDtypeStruct((rows, cols), BF16),
        ],
        scratch_shapes=[
            pltpu.VMEM((count, rows, share), F32),
            pltpu.VMEM((count, share, rank), BF16),
            pltpu.VMEM((count, rows, share), BF16),
            pltpu.SemaphoreType.DMA((count, 3)),
        ],
        input_output_aliases={4 + count + n: n for n in range(len(previous))},
        compiler_params=params(16),
        cost_estimate=cost(
            4 * rows * share * rank * count, count * share * (rows * 10 + rank * 4)
        ),
        name="outputs",
    )(me, base, ortho, colsq, *blocks, *previous)


def ring_order(chips):
    half = chips // 2
    return [2 * q for q in range(half)] + [2 * (chips - 1 - q) + 1 for q in range(half, chips)]


def ring_steps(count):
    order = ring_order(count // 2)
    after = dict(zip(order, order[1:] + order[:1]))
    up = [(2 * c + k, 2 * after[c] + k) for c in order for k in (0, 1)]
    down = [(b, a) for a, b in up]
    first = [p for p in up if p[0] % 2 == 0] + [p for p in down if p[0] % 2 == 1]
    second = [p for p in down if p[0] % 2 == 0] + [p for p in up if p[0] % 2 == 1]
    return first, second


def ring_owner(count, hops, other, me):
    chips = count // 2
    half = chips // 2
    core, chip = me & 1, me >> 1
    place = jnp.where((chip & 1) == 0, chip >> 1, chips - 1 - (chip >> 1))
    forward = hops * (2 * core - 1)
    place = lax.rem(place + chips + (-forward if other else forward), chips)
    chip = jnp.where(place < half, 2 * place, 2 * (chips - 1 - place) + 1)
    return 2 * chip + (1 - core if other else core)


def owner_of(ways):
    return lambda me, n: ways[n](me)


def swap_pairs(count):
    return [(n, n ^ 1) for n in range(count)]


def tie(x, *work):
    return lax.optimization_barrier((x, *work))[0] if work else x


def gather_and_exchange(sketch, near, far, count):
    chips = count // 2
    first, second = ring_steps(count)
    columns = []

    def exchange(*after):
        k = len(columns)
        pairs = [(n, n ^ (chips + k)) for n in range(count)]
        columns.append(lax.ppermute(tie(far[k], *after), "fsdp", pairs))

    exchange(sketch)
    sketch = sketch + lax.ppermute(sketch, "tp", [(0, 1), (1, 0)])
    hops, held = [0], [sketch]
    ahead = behind = sketch
    for step in range(1, chips // 2 + 1):
        work = columns[step - 2 : step - 1] if step > 1 else []
        ahead, behind, *_ = lax.optimization_barrier((ahead, behind, *work))
        exchange(ahead, behind)
        ahead = lax.ppermute(ahead, "fsdp", first)
        held.append(ahead)
        hops.append(step)
        if 2 * step < chips:
            behind = lax.ppermute(behind, "fsdp", second)
            held.append(behind)
            hops.append(-step)
    while len(columns) < chips:
        exchange(ahead, behind)
    groups = [list(range(chips)), list(range(chips, count))]
    near = lax.all_to_all(
        tie(near, ahead, behind), "fsdp", 0, 0, tiled=True, axis_index_groups=groups
    )
    held = jnp.stack(held)
    other = lax.ppermute(held, "fsdp", swap_pairs(count))
    ways = [(h, far) for far in (False, True) for h in hops]
    return [held, other], ways, near, columns


def total_of(x):
    x = x + lax.ppermute(x, "tp", [(0, 1), (1, 0)])
    copies = jnp.broadcast_to(x[None], (lax.axis_size("fsdp"), *x.shape))
    return jnp.sum(lax.all_to_all(copies, "fsdp", 0, 0, tiled=True), axis=0)


def local(momentum, gradient, basis):
    rows, cols = momentum.shape
    rank = basis.shape[1]
    count = lax.axis_size("fsdp")
    tp_count = lax.axis_size("tp")
    chips = count // 2
    share = -(-cols // (count * LANES)) * LANES
    factor = math.sqrt(rows * count * cols * tp_count / rank)
    me = lax.axis_index("fsdp")
    ring = tp_count == 2 and count in (16, 32) and (count - 1) * share < cols

    base = momentum + gradient.astype(F32)
    base_b = base.astype(BF16)
    sketch = jnp.dot(base_b, basis, preferred_element_type=F32)
    base = pltpu.with_memory_space_constraint(base, pltpu.VMEM)
    here = me.reshape(1)
    if ring:
        near, *far = pack_call(here, base, share, count)
        pieces, ways, near, far = gather_and_exchange(sketch, near, far, count)
        owner = owner_of([functools.partial(ring_owner, count, *way) for way in ways])
    else:
        padded = jnp.pad(base_b, ((0, 0), (0, share * count - cols)))
        near = jnp.swapaxes(padded.reshape(rows, count, share), 0, 1)
        near, far = lax.all_to_all(near, "fsdp", 0, 0, tiled=True), []
        whole = lax.all_gather(lax.psum(sketch, "tp"), "fsdp", axis=0)
        pieces, owner = [whole], lambda me, n: n
    ortho_t, ortho_here = factor_call(here, owner, base, pieces)
    part, back = back_call(here, base, ortho_t, near, far)
    write = functools.partial(output_call, me=here, base=base, ortho=ortho_here, factor=factor)
    if not ring:
        whole = lax.all_gather(back, "fsdp", axis=0)
        blocks = [whole[n] for n in range(-(-cols // share))]
        colsq = lax.psum(part, ("fsdp", "tp"))
        return tuple(write(lambda me, n: n, blocks, colsq, None))

    turns, swap = ring_steps(count), swap_pairs(count)
    colsq, result, waiting = part, None, {}
    arrived, blocks, owners, written = {0: back}, [], [], 0
    ready = {chips - 3: 2 * chips - 8, chips - 2: 2 * chips - 4, chips - 1: 2 * chips - 1}
    for n in range(chips):
        block = tie(arrived[n], *waiting.get(n, ()))
        for later in (1, 2) if n == 0 else (n + 2,):
            if later < chips:
                arrived[later] = lax.ppermute(block, "fsdp", turns[(later + 1) % 2])
        blocks += [block, lax.ppermute(block, "fsdp", swap)]
        hops = (n + 1) // 2 if n % 2 else -(n // 2)
        owners += [functools.partial(ring_owner, count, hops, far) for far in (False, True)]
        waiting[n + 2] = (blocks[-1],)
        if n == 0:
            colsq = total_of(part)
        if n == 2:
            waiting[n + 2] += (colsq,)
        if n in ready:
            upto = ready[n]
            result = write(owner_of(owners[written:upto]), blocks[written:upto], colsq, result)
            written, waiting[n + 1] = upto, tuple(result) + waiting.get(n + 1, ())
    return tuple(write(owner_of(owners[written:]), blocks[written:], colsq, result))


def solution(mesh):
    return jax.shard_map(
        local,
        mesh=mesh,
        in_specs=(P("fsdp", "tp"), P("fsdp", "tp"), P("tp", None)),
        out_specs=(P("fsdp", "tp"), P("tp", None), P("fsdp", "tp")),
        check_vma=False,
    )
```

```python
import functools
import math

import jax
import jax.numpy as jnp
from jax import lax
from jax.experimental import pallas as pl
from jax.experimental.pallas import tpu as pltpu
from jax.sharding import PartitionSpec as P

LANES = 128
SUBLANES = 8
PANEL = 64
MIB = 1024 * 1024
FULL = lax.Precision.HIGHEST
F32 = jnp.float32
BF16 = jnp.bfloat16


def cost(flops, nbytes):
    return pl.CostEstimate(flops=flops, bytes_accessed=nbytes, transcendentals=0)


def params(mib):
    return pltpu.CompilerParams(vmem_limit_bytes=mib * MIB)


def by_width(block, cols, share, start, stop, act):
    last = (cols - 1) // share
    width, short = stop - start, max(0, min(cols - last * share, stop) - start)
    if short == width:
        act(width)
        return

    @pl.when(block < last)
    def _():
        act(width)

    if short:

        @pl.when(block == last)
        def _():
            act(short)


def pack_kernel(base_ref, *out_refs):
    cols = base_ref.shape[1]
    share = out_refs[0].shape[1]
    me = lax.axis_index("fsdp")
    for n, out_ref in enumerate(out_refs):
        owner = me ^ n

        def fill(width):
            start = pl.multiple_of(owner * share, LANES)
            out_ref[:, :width] = base_ref[:, pl.ds(start, width)].astype(BF16)
            if width < share:
                out_ref[:, width:] = jnp.zeros((out_ref.shape[0], share - width), BF16)

        by_width(owner, cols, share, 0, share, fill)


def pack_call(base, share, count):
    rows = base.shape[0]
    vmem = pl.BlockSpec(memory_space=pltpu.VMEM)
    return pl.pallas_call(
        pack_kernel,
        in_specs=[vmem],
        out_specs=[vmem] * count,
        out_shape=[jax.ShapeDtypeStruct((rows, share), BF16)] * count,
        compiler_params=params(16),
        cost_estimate=cost(0, 6 * rows * share * count),
        name="pack",
    )(base)


def spread(x, lane):
    return jnp.broadcast_to(x[:, lane : lane + 1], (x.shape[0], LANES))


def row_of(x, row):
    return jnp.broadcast_to(x[row : row + 1, :], (SUBLANES, LANES))


def eliminate(block):
    sub = lax.broadcasted_iota(jnp.int32, (SUBLANES, LANES), 0)
    groups = PANEL // SUBLANES
    top = [block[SUBLANES * g : SUBLANES * (g + 1)] for g in range(groups)]
    for g in range(groups):
        first = PANEL + SUBLANES * g
        t = top[g]
        cols = [spread(t, first + j) for j in range(SUBLANES)]
        below = [[spread(top[i], first + j) for j in range(SUBLANES)] for i in range(g + 1, groups)]
        pivots = jnp.zeros((SUBLANES, LANES), F32)
        inverse, corner = [], {}
        for j in range(SUBLANES):
            pivot = row_of(cols[j], j)
            pivots = jnp.where(sub == j, pivot, pivots)
            inverse.append(1.0 / pivot)
            factor = jnp.where(sub > j, cols[j] * inverse[j], 0.0)
            t = t - factor * row_of(t, j)
            for k in range(j + 1, SUBLANES):
                corner[j, k] = row_of(cols[k], j)
                cols[k] = cols[k] - factor * corner[j, k]
        lines = [row_of(t, j) for j in range(SUBLANES)]
        for i in range(g + 1, groups):
            entries = below[i - g - 1]
            acc = top[i]
            for j in range(SUBLANES):
                factor = entries[j] * inverse[j]
                acc = acc - factor * lines[j]
                for k in range(j + 1, SUBLANES):
                    entries[k] = entries[k] - factor * corner[j, k]
            top[i] = acc
        top[g] = t * lax.rsqrt(pivots)
    return jnp.concatenate(top, axis=0)[:, :PANEL]


def dot(a, b, dims):
    return lax.dot_general(a, b, (dims, ((), ())), precision=FULL, preferred_element_type=F32)


def factor_kernel(stacks, owner, base_ref, *refs):
    me = lax.axis_index("fsdp")
    stacked, (ortho_t_ref, here_ref, whole_ref, work_ref, corner_ref) = refs[:stacks], refs[stacks:]
    corner_ref[...] = base_ref[:SUBLANES, :LANES]
    rows, rank = here_ref.shape
    total = whole_ref.shape[0]
    pieces = [stack.at[n] for stack in stacked for n in range(stack.shape[0])]
    for n, piece in enumerate(pieces):
        start = pl.multiple_of(owner(me, n) * rows, SUBLANES)
        whole_ref[pl.ds(start, rows), :] = piece[...]

    work_ref[:, :rank] = jnp.zeros((rank, rank), F32)
    chunk = 4 * rows

    @pl.loop(0, total // chunk)
    def _(n):
        part = whole_ref[pl.ds(pl.multiple_of(n * chunk, SUBLANES), chunk), :]
        work_ref[:, :rank] += dot(part, part, ((0,), (0,)))

    line = lax.broadcasted_iota(jnp.int32, (rank, rank), 0)
    column = lax.broadcasted_iota(jnp.int32, (rank, rank), 1)
    work_ref[:, rank:] = jnp.where(line == column, 1.0, 0.0).astype(F32)
    eye = jnp.where(line == column, 1.0, 0.0).astype(F32)[:PANEL, :PANEL]
    for start in range(0, rank, PANEL):
        stop = start + PANEL
        diagonal = work_ref[start:stop, start:stop]
        small = eliminate(jnp.concatenate([eye, diagonal], axis=1))
        panel = dot(small, work_ref[start:stop, :], ((1,), (0,)))
        work_ref[start:stop, :] = panel
        if stop < rank:
            work_ref[stop:, :] -= dot(panel[:, stop:rank], panel, ((0,), (0,)))
    inverse = work_ref[:, rank:]
    start = pl.multiple_of(me * rows, SUBLANES)
    here_ref[...] = dot(whole_ref[pl.ds(start, rows), :], inverse, ((1,), (1,))).astype(BF16)
    for n in range(0, total, chunk):
        ortho_t_ref[:, n : n + chunk] = dot(
            inverse, whole_ref[n : n + chunk, :], ((1,), (1,))
        ).astype(BF16)


def factor_call(owner, base, stacked):
    _, rows, rank = stacked[0].shape
    total = rows * sum(stack.shape[0] for stack in stacked)
    vmem = pl.BlockSpec(memory_space=pltpu.VMEM)
    return pl.pallas_call(
        functools.partial(factor_kernel, len(stacked), owner),
        in_specs=[vmem] * (1 + len(stacked)),
        out_specs=[vmem, vmem],
        out_shape=[
            jax.ShapeDtypeStruct((rank, total), BF16),
            jax.ShapeDtypeStruct((rows, rank), BF16),
        ],
        scratch_shapes=[
            pltpu.VMEM((total, rank), F32),
            pltpu.VMEM((rank, 2 * rank), F32),
            pltpu.VMEM((SUBLANES, LANES), F32),
        ],
        compiler_params=params(24),
        cost_estimate=cost(40 * total * rank * rank, total * rank * 6),
        name="factor",
    )(base, *stacked)


def back_kernel(base_ref, ortho_t_ref, *refs):
    *columns, colsq_ref, back_ref, whole_ref, corner_ref = refs
    corner_ref[...] = base_ref[:SUBLANES, :LANES]
    me = lax.axis_index("fsdp") if len(columns) > 1 else 0
    rows = columns[0].shape[0]
    for n, piece in enumerate(columns):
        whole_ref[pl.ds(pl.multiple_of((me ^ n) * rows, 16), rows), :] = piece[...]
    back_t = jnp.dot(ortho_t_ref[...], whole_ref[...], preferred_element_type=F32)
    back = back_t.T.astype(BF16)
    back_ref[...] = back
    wide = back.astype(F32)
    colsq_ref[...] = jnp.sum(wide * wide, axis=0, keepdims=True)


def back_call(base, ortho_t, columns):
    rank, total = ortho_t.shape
    share = columns[0].shape[1]
    vmem = pl.BlockSpec(memory_space=pltpu.VMEM)
    return pl.pallas_call(
        back_kernel,
        in_specs=[vmem] * (2 + len(columns)),
        out_specs=[vmem] * 2,
        out_shape=[
            jax.ShapeDtypeStruct((1, rank), F32),
            jax.ShapeDtypeStruct((share, rank), BF16),
        ],
        scratch_shapes=[pltpu.VMEM((total, share), BF16), pltpu.VMEM((SUBLANES, LANES), F32)],
        compiler_params=params(24),
        cost_estimate=cost(2 * rank * total * share, total * share * 2),
        name="back",
    )(base, ortho_t, *columns)


def output_kernel(owner, factor, base_ref, ortho_ref, colsq_ref, *refs):
    me = lax.axis_index("fsdp")
    *pieces, nm_ref, nb_ref, up_ref, nm_tile, nb_tile, up_tile, sems = refs
    count, share, cols = nm_tile.shape[0], nm_tile.shape[2], nm_ref.shape[1]
    scale = lax.rsqrt(colsq_ref[...] + 1e-06)
    ortho = ortho_ref[...]
    over = (((1,), (1,)), ((), ()))

    def copies(n, width):
        there = pl.ds(pl.multiple_of(owner(me, n) * share, LANES), width)
        sides = (
            (nm_tile.at[n, :, :width], nm_ref.at[:, there]),
            (nb_tile.at[n, :width, :], nb_ref.at[there, :]),
            (up_tile.at[n, :, :width], up_ref.at[:, there]),
        )
        return [
            pltpu.make_async_copy(source, target, sems.at[n, which])
            for which, (source, target) in enumerate(sides)
        ]

    for n in range(count):

        def compute(width):
            there = pl.ds(pl.multiple_of(owner(me, n) * share, LANES), width)
            back = pieces[n][:width, :]
            unit = (back.astype(F32) * scale).astype(BF16)
            nb_tile[n, :width, :] = unit
            nm_tile[n, :, :width] = base_ref[:, there] - 0.05 * lax.dot_general(
                ortho, back, over, preferred_element_type=F32
            )
            up_tile[n, :, :width] = (
                factor * lax.dot_general(ortho, unit, over, preferred_element_type=F32)
            ).astype(BF16)
            for copy in copies(n, width):
                copy.start()

        by_width(owner(me, n), cols, share, 0, share, compute)

    for n in range(count):

        def wait(width):
            for copy in copies(n, width):
                copy.wait()

        by_width(owner(me, n), cols, share, 0, share, wait)


def output_call(owner, blocks, colsq, previous, base, ortho, factor):
    rows, cols = base.shape
    share, rank = blocks[0].shape
    count = len(blocks)
    previous = previous or ()
    vmem, hbm = pl.BlockSpec(memory_space=pltpu.VMEM), pl.BlockSpec(memory_space=pltpu.HBM)
    return pl.pallas_call(
        functools.partial(output_kernel, owner, factor),
        in_specs=[vmem] * (3 + count) + [hbm] * len(previous),
        out_specs=[hbm] * 3,
        out_shape=[
            jax.ShapeDtypeStruct((rows, cols), F32),
            jax.ShapeDtypeStruct((cols, rank), BF16),
            jax.ShapeDtypeStruct((rows, cols), BF16),
        ],
        scratch_shapes=[
            pltpu.VMEM((count, rows, share), F32),
            pltpu.VMEM((count, share, rank), BF16),
            pltpu.VMEM((count, rows, share), BF16),
            pltpu.SemaphoreType.DMA((count, 3)),
        ],
        input_output_aliases={3 + count + n: n for n in range(len(previous))},
        compiler_params=params(16),
        cost_estimate=cost(
            4 * rows * share * rank * count, count * share * (rows * 10 + rank * 4)
        ),
        name="outputs",
    )(base, ortho, colsq, *blocks, *previous)


def ring_order(chips):
    half = chips // 2
    return [2 * q for q in range(half)] + [2 * (chips - 1 - q) + 1 for q in range(half, chips)]


def ring_steps(count):
    order = ring_order(count // 2)
    after = dict(zip(order, order[1:] + order[:1]))
    up = [(2 * c + k, 2 * after[c] + k) for c in order for k in (0, 1)]
    down = [(b, a) for a, b in up]
    first = [p for p in up if p[0] % 2 == 0] + [p for p in down if p[0] % 2 == 1]
    second = [p for p in down if p[0] % 2 == 0] + [p for p in up if p[0] % 2 == 1]
    return first, second


def ring_owner(count, hops, other, me):
    chips = count // 2
    half = chips // 2
    core, chip = me & 1, me >> 1
    place = jnp.where((chip & 1) == 0, chip >> 1, chips - 1 - (chip >> 1))
    forward = hops * (2 * core - 1)
    place = lax.rem(place + chips + (-forward if other else forward), chips)
    chip = jnp.where(place < half, 2 * place, 2 * (chips - 1 - place) + 1)
    return 2 * chip + (1 - core if other else core)


def owner_of(ways):
    return lambda me, n: ways[n](me)


def swap_pairs(count):
    return [(n, n ^ 1) for n in range(count)]


def tie(x, *work):
    return lax.optimization_barrier((x, *work))[0] if work else x


def exchange_windows(count):
    chips, steps = count // 2, count // 4
    far, near = list(range(chips, count)), list(range(1, chips))
    each = -(-len(near) // (steps + 1))
    windows = [far[w : w + 1] + near[w * each : (w + 1) * each] for w in range(steps + 1)]
    return windows + [far[steps + 1 :]]


def gather_and_exchange(sketch, outgoing, count):
    chips = count // 2
    first, second = ring_steps(count)
    windows = exchange_windows(count)
    columns = {0: outgoing[0]}

    def exchange(window, *after):
        for k in window:
            pairs = [(n, n ^ k) for n in range(count)]
            columns[k] = lax.ppermute(tie(outgoing[k], *after), "fsdp", pairs)

    exchange(windows[0], sketch)
    sketch = sketch + lax.ppermute(sketch, "tp", [(0, 1), (1, 0)])
    hops, held = [0], [sketch]
    ahead = behind = sketch
    for step in range(1, chips // 2 + 1):
        work = [columns[k] for k in windows[step - 2]] if step > 1 else []
        ahead, behind, *_ = lax.optimization_barrier((ahead, behind, *work))
        exchange(windows[step], ahead, behind)
        ahead = lax.ppermute(ahead, "fsdp", first)
        held.append(ahead)
        hops.append(step)
        if 2 * step < chips:
            behind = lax.ppermute(behind, "fsdp", second)
            held.append(behind)
            hops.append(-step)
    exchange(windows[-1], ahead, behind)
    held = tie(jnp.stack(held), *[columns[k] for k in windows[-3]])
    other = lax.ppermute(held, "fsdp", swap_pairs(count))
    ways = [(h, far) for far in (False, True) for h in hops]
    return [held, other], ways, [columns[k] for k in range(count)]


def sum_rounds(count):
    rounds, bit = [("tp", [1])], 1
    while bit < count:
        rounds.append(("fsdp", [bit, 2 * bit, 3 * bit] if 2 * bit < count else [bit]))
        bit *= 4
    return rounds


def sum_round(x, axis, distances):
    size = lax.axis_size(axis)
    terms = [x]
    for d in distances:
        terms.append(lax.ppermute(x, axis, [(n, n ^ d) for n in range(size)]))
    if len(terms) == 2:
        return terms[0] + terms[1]
    return (terms[0] + terms[1]) + (terms[2] + terms[3])


def local(momentum, gradient, basis):
    rows, cols = momentum.shape
    rank = basis.shape[1]
    count = lax.axis_size("fsdp")
    tp_count = lax.axis_size("tp")
    chips = count // 2
    share = -(-cols // (count * LANES)) * LANES
    factor = math.sqrt(rows * count * cols * tp_count / rank)
    ring = tp_count == 2 and count in (16, 32) and (count - 1) * share < cols

    base = momentum + gradient.astype(F32)
    base_b = base.astype(BF16)
    sketch = jnp.dot(base_b, basis, preferred_element_type=F32)
    base = pltpu.with_memory_space_constraint(base, pltpu.VMEM)
    if ring:
        outgoing = pack_call(base, share, count)
        pieces, ways, columns = gather_and_exchange(sketch, outgoing, count)
        owner = owner_of([functools.partial(ring_owner, count, *way) for way in ways])
    else:
        padded = jnp.pad(base_b, ((0, 0), (0, share * count - cols)))
        columns = jnp.swapaxes(padded.reshape(rows, count, share), 0, 1)
        columns = lax.all_to_all(columns, "fsdp", 0, 0, tiled=True)
        columns = [columns.reshape(count * rows, share)]
        pieces = [lax.all_gather(lax.psum(sketch, "tp"), "fsdp", axis=0)]
        owner = lambda me, n: n
    ortho_t, ortho_here = factor_call(owner, base, pieces)
    part, back = back_call(base, ortho_t, columns)
    write = functools.partial(output_call, base=base, ortho=ortho_here, factor=factor)
    if not ring:
        whole = lax.all_gather(back, "fsdp", axis=0)
        blocks = [whole[n] for n in range(-(-cols // share))]
        colsq = lax.psum(part, ("fsdp", "tp"))
        return tuple(write(lambda me, n: n, blocks, colsq, None))

    turns, swap = ring_steps(count), swap_pairs(count)
    rounds = sum_rounds(count)
    colsq, result, waiting = part, None, {}
    arrived, blocks, owners, written = {0: back}, [], [], 0
    ready = {chips - 3: 2 * chips - 8, chips - 2: 2 * chips - 4, chips - 1: 2 * chips - 1}
    for n in range(chips):
        if n < 2:
            for _ in range(2 - n):
                colsq = sum_round(tie(colsq, arrived[n]), *rounds.pop(0))
        if n == 1:
            waiting[1] = (colsq,)
        block = tie(arrived[n], *waiting.get(n, ()))
        for later in (1, 2) if n == 0 else (n + 2,):
            if later < chips:
                arrived[later] = lax.ppermute(block, "fsdp", turns[(later + 1) % 2])
        blocks += [block, lax.ppermute(block, "fsdp", swap)]
        hops = (n + 1) // 2 if n % 2 else -(n // 2)
        owners += [functools.partial(ring_owner, count, hops, far) for far in (False, True)]
        if n in ready:
            upto = ready[n]
            result = write(owner_of(owners[written:upto]), blocks[written:upto], colsq, result)
            written, waiting[n + 1] = upto, tuple(result) + waiting.get(n + 1, ())
    return tuple(write(owner_of(owners[written:]), blocks[written:], colsq, result))


def solution(mesh):
    return jax.shard_map(
        local,
        mesh=mesh,
        in_specs=(P("fsdp", "tp"), P("fsdp", "tp"), P("tp", None)),
        out_specs=(P("fsdp", "tp"), P("tp", None), P("fsdp", "tp")),
        check_vma=False,
    )
```

```python
import functools
import math

import jax
import jax.numpy as jnp
from jax import lax
from jax.experimental import pallas as pl
from jax.experimental.pallas import tpu as pltpu
from jax.sharding import PartitionSpec as P

LANES = 128
SUBLANES = 8
PANEL = 64
MIB = 1024 * 1024
FULL = lax.Precision.HIGHEST
F32 = jnp.float32
BF16 = jnp.bfloat16


def cost(flops, nbytes):
    return pl.CostEstimate(flops=flops, bytes_accessed=nbytes, transcendentals=0)


def params(mib):
    return pltpu.CompilerParams(vmem_limit_bytes=mib * MIB)


def by_width(block, cols, share, start, stop, act):
    last = (cols - 1) // share
    width, short = stop - start, max(0, min(cols - last * share, stop) - start)
    if short == width:
        act(width)
        return

    @pl.when(block < last)
    def _():
        act(width)

    if short:

        @pl.when(block == last)
        def _():
            act(short)


def pack_kernel(base_ref, *out_refs):
    cols = base_ref.shape[1]
    share = out_refs[0].shape[1]
    me = lax.axis_index("fsdp")
    for n, out_ref in enumerate(out_refs):
        owner = me ^ n

        def fill(width):
            start = pl.multiple_of(owner * share, LANES)
            out_ref[:, :width] = base_ref[:, pl.ds(start, width)].astype(BF16)
            if width < share:
                out_ref[:, width:] = jnp.zeros((out_ref.shape[0], share - width), BF16)

        by_width(owner, cols, share, 0, share, fill)


def pack_call(base, share, count):
    rows = base.shape[0]
    vmem = pl.BlockSpec(memory_space=pltpu.VMEM)
    return pl.pallas_call(
        pack_kernel,
        in_specs=[vmem],
        out_specs=[vmem] * count,
        out_shape=[jax.ShapeDtypeStruct((rows, share), BF16)] * count,
        compiler_params=params(16),
        cost_estimate=cost(0, 6 * rows * share * count),
        name="pack",
    )(base)


def spread(x, lane):
    return jnp.broadcast_to(x[:, lane : lane + 1], (x.shape[0], LANES))


def row_of(x, row):
    return jnp.broadcast_to(x[row : row + 1, :], (SUBLANES, LANES))


def eliminate(block):
    sub = lax.broadcasted_iota(jnp.int32, (SUBLANES, LANES), 0)
    groups = PANEL // SUBLANES
    top = [block[SUBLANES * g : SUBLANES * (g + 1)] for g in range(groups)]
    for g in range(groups):
        first = PANEL + SUBLANES * g
        t = top[g]
        cols = [spread(t, first + j) for j in range(SUBLANES)]
        below = [[spread(top[i], first + j) for j in range(SUBLANES)] for i in range(g + 1, groups)]
        pivots = jnp.zeros((SUBLANES, LANES), F32)
        inverse, corner = [], {}
        for j in range(SUBLANES):
            pivot = row_of(cols[j], j)
            pivots = jnp.where(sub == j, pivot, pivots)
            inverse.append(1.0 / pivot)
            factor = jnp.where(sub > j, cols[j] * inverse[j], 0.0)
            t = t - factor * row_of(t, j)
            for k in range(j + 1, SUBLANES):
                corner[j, k] = row_of(cols[k], j)
                cols[k] = cols[k] - factor * corner[j, k]
        lines = [row_of(t, j) for j in range(SUBLANES)]
        for i in range(g + 1, groups):
            entries = below[i - g - 1]
            acc = top[i]
            for j in range(SUBLANES):
                factor = entries[j] * inverse[j]
                acc = acc - factor * lines[j]
                for k in range(j + 1, SUBLANES):
                    entries[k] = entries[k] - factor * corner[j, k]
            top[i] = acc
        top[g] = t * lax.rsqrt(pivots)
    return jnp.concatenate(top, axis=0)[:, :PANEL]


def dot(a, b, dims):
    return lax.dot_general(a, b, (dims, ((), ())), precision=FULL, preferred_element_type=F32)


def factor_kernel(stacks, owner, base_ref, *refs):
    me = lax.axis_index("fsdp")
    stacked, (ortho_t_ref, here_ref, whole_ref, work_ref, corner_ref) = refs[:stacks], refs[stacks:]
    corner_ref[...] = base_ref[:SUBLANES, :LANES]
    rows, rank = here_ref.shape
    total = whole_ref.shape[0]
    pieces = [stack.at[n] for stack in stacked for n in range(stack.shape[0])]
    for n, piece in enumerate(pieces):
        start = pl.multiple_of(owner(me, n) * rows, SUBLANES)
        whole_ref[pl.ds(start, rows), :] = piece[...]

    work_ref[:, :rank] = jnp.zeros((rank, rank), F32)
    chunk = 4 * rows

    @pl.loop(0, total // chunk)
    def _(n):
        part = whole_ref[pl.ds(pl.multiple_of(n * chunk, SUBLANES), chunk), :]
        work_ref[:, :rank] += dot(part, part, ((0,), (0,)))

    line = lax.broadcasted_iota(jnp.int32, (rank, rank), 0)
    column = lax.broadcasted_iota(jnp.int32, (rank, rank), 1)
    work_ref[:, rank:] = jnp.where(line == column, 1.0, 0.0).astype(F32)
    eye = jnp.where(line == column, 1.0, 0.0).astype(F32)[:PANEL, :PANEL]
    for start in range(0, rank, PANEL):
        stop = start + PANEL
        diagonal = work_ref[start:stop, start:stop]
        small = eliminate(jnp.concatenate([eye, diagonal], axis=1))
        panel = dot(small, work_ref[start:stop, :], ((1,), (0,)))
        work_ref[start:stop, :] = panel
        if stop < rank:
            work_ref[stop:, :] -= dot(panel[:, stop:rank], panel, ((0,), (0,)))
    inverse = work_ref[:, rank:]
    start = pl.multiple_of(me * rows, SUBLANES)
    here_ref[...] = dot(whole_ref[pl.ds(start, rows), :], inverse, ((1,), (1,))).astype(BF16)
    for n in range(0, total, chunk):
        ortho_t_ref[:, n : n + chunk] = dot(
            inverse, whole_ref[n : n + chunk, :], ((1,), (1,))
        ).astype(BF16)


def factor_call(owner, base, stacked):
    _, rows, rank = stacked[0].shape
    total = rows * sum(stack.shape[0] for stack in stacked)
    vmem = pl.BlockSpec(memory_space=pltpu.VMEM)
    return pl.pallas_call(
        functools.partial(factor_kernel, len(stacked), owner),
        in_specs=[vmem] * (1 + len(stacked)),
        out_specs=[vmem, vmem],
        out_shape=[
            jax.ShapeDtypeStruct((rank, total), BF16),
            jax.ShapeDtypeStruct((rows, rank), BF16),
        ],
        scratch_shapes=[
            pltpu.VMEM((total, rank), F32),
            pltpu.VMEM((rank, 2 * rank), F32),
            pltpu.VMEM((SUBLANES, LANES), F32),
        ],
        compiler_params=params(24),
        cost_estimate=cost(40 * total * rank * rank, total * rank * 6),
        name="factor",
    )(base, *stacked)


def back_kernel(base_ref, ortho_t_ref, *refs):
    *columns, colsq_ref, back_ref, whole_ref, corner_ref = refs
    corner_ref[...] = base_ref[:SUBLANES, :LANES]
    me = lax.axis_index("fsdp") if len(columns) > 1 else 0
    rows = columns[0].shape[0]
    for n, piece in enumerate(columns):
        whole_ref[pl.ds(pl.multiple_of((me ^ n) * rows, 16), rows), :] = piece[...]
    back_t = jnp.dot(ortho_t_ref[...], whole_ref[...], preferred_element_type=F32)
    back = back_t.T.astype(BF16)
    back_ref[...] = back
    wide = back.astype(F32)
    colsq_ref[...] = jnp.sum(wide * wide, axis=0, keepdims=True)


def back_call(base, ortho_t, columns):
    rank, total = ortho_t.shape
    share = columns[0].shape[1]
    vmem = pl.BlockSpec(memory_space=pltpu.VMEM)
    return pl.pallas_call(
        back_kernel,
        in_specs=[vmem] * (2 + len(columns)),
        out_specs=[vmem] * 2,
        out_shape=[
            jax.ShapeDtypeStruct((1, rank), F32),
            jax.ShapeDtypeStruct((share, rank), BF16),
        ],
        scratch_shapes=[pltpu.VMEM((total, share), BF16), pltpu.VMEM((SUBLANES, LANES), F32)],
        compiler_params=params(24),
        cost_estimate=cost(2 * rank * total * share, total * share * 2),
        name="back",
    )(base, ortho_t, *columns)


def output_kernel(owner, factor, base_ref, ortho_ref, colsq_ref, *refs):
    me = lax.axis_index("fsdp")
    *pieces, nm_ref, nb_ref, up_ref, nm_tile, nb_tile, up_tile, sems = refs
    count, share, cols = nm_tile.shape[0], nm_tile.shape[2], nm_ref.shape[1]
    scale = lax.rsqrt(colsq_ref[...] + 1e-06)
    ortho = ortho_ref[...]
    over = (((1,), (1,)), ((), ()))

    def copies(n, width):
        there = pl.ds(pl.multiple_of(owner(me, n) * share, LANES), width)
        sides = (
            (nm_tile.at[n, :, :width], nm_ref.at[:, there]),
            (nb_tile.at[n, :width, :], nb_ref.at[there, :]),
            (up_tile.at[n, :, :width], up_ref.at[:, there]),
        )
        return [
            pltpu.make_async_copy(source, target, sems.at[n, which])
            for which, (source, target) in enumerate(sides)
        ]

    for n in range(count):

        def compute(width):
            there = pl.ds(pl.multiple_of(owner(me, n) * share, LANES), width)
            back = pieces[n][:width, :]
            unit = (back.astype(F32) * scale).astype(BF16)
            nb_tile[n, :width, :] = unit
            nm_tile[n, :, :width] = base_ref[:, there] - 0.05 * lax.dot_general(
                ortho, back, over, preferred_element_type=F32
            )
            up_tile[n, :, :width] = (
                factor * lax.dot_general(ortho, unit, over, preferred_element_type=F32)
            ).astype(BF16)
            for copy in copies(n, width):
                copy.start()

        by_width(owner(me, n), cols, share, 0, share, compute)

    for n in range(count):

        def wait(width):
            for copy in copies(n, width):
                copy.wait()

        by_width(owner(me, n), cols, share, 0, share, wait)


def output_call(owner, blocks, colsq, previous, base, ortho, factor):
    rows, cols = base.shape
    share, rank = blocks[0].shape
    count = len(blocks)
    previous = previous or ()
    vmem, hbm = pl.BlockSpec(memory_space=pltpu.VMEM), pl.BlockSpec(memory_space=pltpu.HBM)
    return pl.pallas_call(
        functools.partial(output_kernel, owner, factor),
        in_specs=[vmem] * (3 + count) + [hbm] * len(previous),
        out_specs=[hbm] * 3,
        out_shape=[
            jax.ShapeDtypeStruct((rows, cols), F32),
            jax.ShapeDtypeStruct((cols, rank), BF16),
            jax.ShapeDtypeStruct((rows, cols), BF16),
        ],
        scratch_shapes=[
            pltpu.VMEM((count, rows, share), F32),
            pltpu.VMEM((count, share, rank), BF16),
            pltpu.VMEM((count, rows, share), BF16),
            pltpu.SemaphoreType.DMA((count, 3)),
        ],
        input_output_aliases={3 + count + n: n for n in range(len(previous))},
        compiler_params=params(16),
        cost_estimate=cost(
            4 * rows * share * rank * count, count * share * (rows * 10 + rank * 4)
        ),
        name="outputs",
    )(base, ortho, colsq, *blocks, *previous)


def ring_order(chips):
    half = chips // 2
    return [2 * q for q in range(half)] + [2 * (chips - 1 - q) + 1 for q in range(half, chips)]


def ring_steps(count):
    order = ring_order(count // 2)
    after = dict(zip(order, order[1:] + order[:1]))
    up = [(2 * c + k, 2 * after[c] + k) for c in order for k in (0, 1)]
    down = [(b, a) for a, b in up]
    first = [p for p in up if p[0] % 2 == 0] + [p for p in down if p[0] % 2 == 1]
    second = [p for p in down if p[0] % 2 == 0] + [p for p in up if p[0] % 2 == 1]
    return first, second


def ring_owner(count, hops, other, me):
    chips = count // 2
    half = chips // 2
    core, chip = me & 1, me >> 1
    place = jnp.where((chip & 1) == 0, chip >> 1, chips - 1 - (chip >> 1))
    forward = hops * (2 * core - 1)
    place = lax.rem(place + chips + (-forward if other else forward), chips)
    chip = jnp.where(place < half, 2 * place, 2 * (chips - 1 - place) + 1)
    return 2 * chip + (1 - core if other else core)


def owner_of(ways):
    return lambda me, n: ways[n](me)


def swap_pairs(count):
    return [(n, n ^ 1) for n in range(count)]


def tie(x, *work):
    return lax.optimization_barrier((x, *work))[0] if work else x


def exchange_windows(count):
    chips, steps = count // 2, count // 4
    far, near = list(range(chips, count)), list(range(1, chips))
    each = -(-len(near) // (steps + 1))
    windows = [far[w : w + 1] + near[w * each : (w + 1) * each] for w in range(steps + 1)]
    return windows + [far[steps + 1 :]]


def gather_and_exchange(sketch, outgoing, count):
    chips = count // 2
    first, second = ring_steps(count)
    windows = exchange_windows(count)
    columns = {0: outgoing[0]}

    def exchange(window, *after):
        for k in window:
            pairs = [(n, n ^ k) for n in range(count)]
            columns[k] = lax.ppermute(tie(outgoing[k], *after), "fsdp", pairs)

    exchange(windows[0], sketch)
    sketch = sketch + lax.ppermute(sketch, "tp", [(0, 1), (1, 0)])
    hops, held = [0], [sketch]
    ahead = behind = sketch
    for step in range(1, chips // 2 + 1):
        work = [columns[k] for k in windows[step - 2]] if step > 1 else []
        ahead, behind, *_ = lax.optimization_barrier((ahead, behind, *work))
        exchange(windows[step], ahead, behind)
        ahead = lax.ppermute(ahead, "fsdp", first)
        held.append(ahead)
        hops.append(step)
        if 2 * step < chips:
            behind = lax.ppermute(behind, "fsdp", second)
            held.append(behind)
            hops.append(-step)
    exchange(windows[-1], ahead, behind)
    held = tie(jnp.stack(held), *[columns[k] for k in windows[-3]])
    other = lax.ppermute(held, "fsdp", swap_pairs(count))
    ways = [(h, far) for far in (False, True) for h in hops]
    return [held, other], ways, [columns[k] for k in range(count)]


def sum_rounds(count):
    rounds, bit = [("tp", [1])], 1
    while bit < count:
        rounds.append(("fsdp", [bit, 2 * bit, 3 * bit] if 2 * bit < count else [bit]))
        bit *= 4
    return rounds


def sum_round(x, axis, distances):
    size = lax.axis_size(axis)
    terms = [x]
    for d in distances:
        terms.append(lax.ppermute(x, axis, [(n, n ^ d) for n in range(size)]))
    if len(terms) == 2:
        return terms[0] + terms[1]
    return (terms[0] + terms[1]) + (terms[2] + terms[3])


def local(momentum, gradient, basis):
    rows, cols = momentum.shape
    rank = basis.shape[1]
    count = lax.axis_size("fsdp")
    tp_count = lax.axis_size("tp")
    chips = count // 2
    share = -(-cols // (count * LANES)) * LANES
    factor = math.sqrt(rows * count * cols * tp_count / rank)
    ring = tp_count == 2 and count in (16, 32) and (count - 1) * share < cols

    base = momentum + gradient.astype(F32)
    base_b = base.astype(BF16)
    sketch = jnp.dot(base_b, basis, preferred_element_type=F32)
    base = pltpu.with_memory_space_constraint(base, pltpu.VMEM)
    if ring:
        outgoing = pack_call(base, share, count)
        pieces, ways, columns = gather_and_exchange(sketch, outgoing, count)
        owner = owner_of([functools.partial(ring_owner, count, *way) for way in ways])
    else:
        padded = jnp.pad(base_b, ((0, 0), (0, share * count - cols)))
        columns = jnp.swapaxes(padded.reshape(rows, count, share), 0, 1)
        columns = lax.all_to_all(columns, "fsdp", 0, 0, tiled=True)
        columns = [columns.reshape(count * rows, share)]
        pieces = [lax.all_gather(lax.psum(sketch, "tp"), "fsdp", axis=0)]
        owner = lambda me, n: n
    ortho_t, ortho_here = factor_call(owner, base, pieces)
    part, back = back_call(base, ortho_t, columns)
    write = functools.partial(output_call, base=base, ortho=ortho_here, factor=factor)
    if not ring:
        whole = lax.all_gather(back, "fsdp", axis=0)
        blocks = [whole[n] for n in range(-(-cols // share))]
        colsq = lax.psum(part, ("fsdp", "tp"))
        return tuple(write(lambda me, n: n, blocks, colsq, None))

    turns, swap = ring_steps(count), swap_pairs(count)
    colsq, result = part, None
    for axis, distances in sum_rounds(count):
        colsq = sum_round(colsq, axis, distances)
    arrived, blocks, owners, written = {0: back}, [], [], 0
    waiting = ()
    for n in range(chips):
        block = tie(arrived[n], *waiting)
        for later in (1, 2) if n == 0 else (n + 2,):
            if later < chips:
                arrived[later] = lax.ppermute(block, "fsdp", turns[(later + 1) % 2])
        blocks += [block, lax.ppermute(block, "fsdp", swap)]
        hops = (n + 1) // 2 if n % 2 else -(n // 2)
        owners += [functools.partial(ring_owner, count, hops, far) for far in (False, True)]
        if n == 0:
            waiting = (arrived[2], colsq)
            continue
        if n == 2:
            waiting = ()
            continue
        upto = 2 * n + (2 if n == 1 else 1 if n + 1 == chips else 0)
        upto = min(upto, written + 4) if n + 1 < chips else upto
        result = write(owner_of(owners[written:upto]), blocks[written:upto], colsq, result)
        written, waiting = upto, tuple(result)
    return tuple(write(owner_of(owners[written:]), blocks[written:], colsq, result))


def solution(mesh):
    return jax.shard_map(
        local,
        mesh=mesh,
        in_specs=(P("fsdp", "tp"), P("fsdp", "tp"), P("tp", None)),
        out_specs=(P("fsdp", "tp"), P("tp", None), P("fsdp", "tp")),
        check_vma=False,
    )
```

```python
import functools
import math

import jax
import jax.numpy as jnp
from jax import lax
from jax.experimental import pallas as pl
from jax.experimental.pallas import tpu as pltpu
from jax.sharding import PartitionSpec as P

LANES = 128
SUBLANES = 8
PANEL = 64
SPLIT = 3 * LANES
MIB = 1024 * 1024
FULL = lax.Precision.HIGHEST
F32 = jnp.float32
BF16 = jnp.bfloat16


def cost(flops, nbytes):
    return pl.CostEstimate(flops=flops, bytes_accessed=nbytes, transcendentals=0)


def params(mib):
    return pltpu.CompilerParams(vmem_limit_bytes=mib * MIB)


def by_width(block, cols, share, start, stop, act):
    last = (cols - 1) // share
    width, short = stop - start, max(0, min(cols - last * share, stop) - start)
    if short == width:
        act(width)
        return

    @pl.when(block < last)
    def _():
        act(width)

    if short:

        @pl.when(block == last)
        def _():
            act(short)


def pack_kernel(share, base_ref, *out_refs):
    cols = base_ref.shape[1]
    half, whole = len(out_refs) // 2, share - SPLIT
    last = (cols - 1) // share
    me = lax.axis_index("fsdp")

    def fill(out_ref, offset, owner, start, stop):
        short = max(0, min(cols - last * share, stop) - start)

        def put(width):
            if width:
                there = pl.ds(pl.multiple_of(owner * share + start, LANES), width)
                out_ref[:, offset : offset + width] = base_ref[:, there].astype(BF16)
            if width < stop - start:
                empty = jnp.zeros((out_ref.shape[0], stop - start - width), BF16)
                out_ref[:, offset + width : offset + stop - start] = empty

        if short == stop - start:
            put(short)
        else:
            pl.when(owner < last)(lambda: put(stop - start))
            pl.when(owner == last)(lambda: put(short))

    for n, out_ref in enumerate(out_refs):
        owner = me ^ n
        if n < half:
            fill(out_ref, 0, owner, 0, share)
            fill(out_ref, share, owner ^ half, whole, share)
        else:
            fill(out_ref, 0, owner, 0, whole)


def pack_call(base, share, count):
    rows, half = base.shape[0], count // 2
    widths = [share + SPLIT] * half + [share - SPLIT] * half
    vmem = pl.BlockSpec(memory_space=pltpu.VMEM)
    return pl.pallas_call(
        functools.partial(pack_kernel, share),
        in_specs=[vmem],
        out_specs=[vmem] * count,
        out_shape=[jax.ShapeDtypeStruct((rows, width), BF16) for width in widths],
        compiler_params=params(16),
        cost_estimate=cost(0, 6 * rows * share * count),
        name="pack",
    )(base)


def spread(x, lane):
    return jnp.broadcast_to(x[:, lane : lane + 1], (x.shape[0], LANES))


def row_of(x, row):
    return jnp.broadcast_to(x[row : row + 1, :], (SUBLANES, LANES))


def eliminate(block):
    sub = lax.broadcasted_iota(jnp.int32, (SUBLANES, LANES), 0)
    groups = PANEL // SUBLANES
    top = [block[SUBLANES * g : SUBLANES * (g + 1)] for g in range(groups)]
    for g in range(groups):
        first = PANEL + SUBLANES * g
        t = top[g]
        cols = [spread(t, first + j) for j in range(SUBLANES)]
        below = [[spread(top[i], first + j) for j in range(SUBLANES)] for i in range(g + 1, groups)]
        pivots = jnp.zeros((SUBLANES, LANES), F32)
        inverse, corner = [], {}
        for j in range(SUBLANES):
            pivot = row_of(cols[j], j)
            pivots = jnp.where(sub == j, pivot, pivots)
            inverse.append(1.0 / pivot)
            factor = jnp.where(sub > j, cols[j] * inverse[j], 0.0)
            t = t - factor * row_of(t, j)
            for k in range(j + 1, SUBLANES):
                corner[j, k] = row_of(cols[k], j)
                cols[k] = cols[k] - factor * corner[j, k]
        lines = [row_of(t, j) for j in range(SUBLANES)]
        for i in range(g + 1, groups):
            entries = below[i - g - 1]
            acc = top[i]
            for j in range(SUBLANES):
                factor = entries[j] * inverse[j]
                acc = acc - factor * lines[j]
                for k in range(j + 1, SUBLANES):
                    entries[k] = entries[k] - factor * corner[j, k]
            top[i] = acc
        top[g] = t * lax.rsqrt(pivots)
    return jnp.concatenate(top, axis=0)[:, :PANEL]


def dot(a, b, dims):
    return lax.dot_general(a, b, (dims, ((), ())), precision=FULL, preferred_element_type=F32)


def factor_kernel(stacks, owner, base_ref, *refs):
    me = lax.axis_index("fsdp")
    stacked, (ortho_t_ref, here_ref, whole_ref, work_ref, corner_ref) = refs[:stacks], refs[stacks:]
    corner_ref[...] = base_ref[:SUBLANES, :LANES]
    rows, rank = here_ref.shape
    total = whole_ref.shape[0]
    pieces = [stack.at[n] for stack in stacked for n in range(stack.shape[0])]
    for n, piece in enumerate(pieces):
        start = pl.multiple_of(owner(me, n) * rows, SUBLANES)
        whole_ref[pl.ds(start, rows), :] = piece[...]

    work_ref[:, :rank] = jnp.zeros((rank, rank), F32)
    chunk = 4 * rows

    @pl.loop(0, total // chunk)
    def _(n):
        part = whole_ref[pl.ds(pl.multiple_of(n * chunk, SUBLANES), chunk), :]
        work_ref[:, :rank] += dot(part, part, ((0,), (0,)))

    line = lax.broadcasted_iota(jnp.int32, (rank, rank), 0)
    column = lax.broadcasted_iota(jnp.int32, (rank, rank), 1)
    work_ref[:, rank:] = jnp.where(line == column, 1.0, 0.0).astype(F32)
    eye = jnp.where(line == column, 1.0, 0.0).astype(F32)[:PANEL, :PANEL]
    for start in range(0, rank, PANEL):
        stop = start + PANEL
        diagonal = work_ref[start:stop, start:stop]
        small = eliminate(jnp.concatenate([eye, diagonal], axis=1))
        panel = dot(small, work_ref[start:stop, :], ((1,), (0,)))
        work_ref[start:stop, :] = panel
        if stop < rank:
            work_ref[stop:, :] -= dot(panel[:, stop:rank], panel, ((0,), (0,)))
    inverse = work_ref[:, rank:]
    start = pl.multiple_of(me * rows, SUBLANES)
    here_ref[...] = dot(whole_ref[pl.ds(start, rows), :], inverse, ((1,), (1,))).astype(BF16)
    for n in range(0, total, chunk):
        ortho_t_ref[:, n : n + chunk] = dot(
            inverse, whole_ref[n : n + chunk, :], ((1,), (1,))
        ).astype(BF16)


def factor_call(owner, base, stacked):
    _, rows, rank = stacked[0].shape
    total = rows * sum(stack.shape[0] for stack in stacked)
    vmem = pl.BlockSpec(memory_space=pltpu.VMEM)
    return pl.pallas_call(
        functools.partial(factor_kernel, len(stacked), owner),
        in_specs=[vmem] * (1 + len(stacked)),
        out_specs=[vmem, vmem],
        out_shape=[
            jax.ShapeDtypeStruct((rank, total), BF16),
            jax.ShapeDtypeStruct((rows, rank), BF16),
        ],
        scratch_shapes=[
            pltpu.VMEM((total, rank), F32),
            pltpu.VMEM((rank, 2 * rank), F32),
            pltpu.VMEM((SUBLANES, LANES), F32),
        ],
        compiler_params=params(24),
        cost_estimate=cost(40 * total * rank * rank, total * rank * 6),
        name="factor",
    )(base, *stacked)


def half_kernel(share, ortho_t_ref, *refs):
    *near, mine_ref, theirs_ref, rows_ref = refs
    me = lax.axis_index("fsdp")
    rows, half = near[0].shape[0], len(near)
    for n, piece in enumerate(near):
        at = pl.ds(pl.multiple_of(((me ^ n) & (half - 1)) * rows, 16), rows)
        rows_ref[at, :] = piece[:, share - SPLIT :]
    first = pl.multiple_of((me & half) * rows, LANES)
    ortho_t = ortho_t_ref[:, pl.ds(first, half * rows)]
    back = jnp.dot(ortho_t, rows_ref[...], preferred_element_type=F32).T
    mine_ref[...] = back[:SPLIT]
    theirs_ref[...] = back[SPLIT:].astype(BF16)


def half_call(ortho_t, near, share):
    rank = ortho_t.shape[0]
    rows = near[0].shape[0] * len(near)
    vmem = pl.BlockSpec(memory_space=pltpu.VMEM)
    return pl.pallas_call(
        functools.partial(half_kernel, share),
        in_specs=[vmem] * (1 + len(near)),
        out_specs=[vmem] * 2,
        out_shape=[
            jax.ShapeDtypeStruct((SPLIT, rank), F32),
            jax.ShapeDtypeStruct((SPLIT, rank), BF16),
        ],
        scratch_shapes=[pltpu.VMEM((rows, 2 * SPLIT), BF16)],
        compiler_params=params(16),
        cost_estimate=cost(4 * rank * rows * SPLIT, rows * SPLIT * 4),
        name="half_back",
    )(ortho_t, *near)


def back_kernel(pieces, base_ref, ortho_t_ref, *refs):
    columns, (*sums, colsq_ref, back_ref, whole_ref, corner_ref) = refs[:pieces], refs[pieces:]
    corner_ref[...] = base_ref[:SUBLANES, :LANES]
    me = lax.axis_index("fsdp") if pieces > 1 else 0
    rows, width = columns[0].shape[0], whole_ref.shape[1]
    for n, piece in enumerate(columns):
        at = pl.ds(pl.multiple_of((me ^ n) * rows, 16), rows)
        whole_ref[at, :] = piece[:, :width]
    back_t = jnp.dot(ortho_t_ref[...], whole_ref[...], preferred_element_type=F32)
    back_ref[:width, :] = back_t.T.astype(BF16)
    if sums:
        mine_ref, other_ref = sums
        back_ref[width:, :] = (mine_ref[...] + other_ref[...].astype(F32)).astype(BF16)
    wide = back_ref[...].astype(F32)
    colsq_ref[...] = jnp.sum(wide * wide, axis=0, keepdims=True)


def back_call(base, ortho_t, columns, share, sums=()):
    rank, total = ortho_t.shape
    width = share - (SPLIT if sums else 0)
    vmem = pl.BlockSpec(memory_space=pltpu.VMEM)
    return pl.pallas_call(
        functools.partial(back_kernel, len(columns)),
        in_specs=[vmem] * (2 + len(columns) + len(sums)),
        out_specs=[vmem] * 2,
        out_shape=[
            jax.ShapeDtypeStruct((1, rank), F32),
            jax.ShapeDtypeStruct((share, rank), BF16),
        ],
        scratch_shapes=[pltpu.VMEM((total, width), BF16), pltpu.VMEM((SUBLANES, LANES), F32)],
        compiler_params=params(24),
        cost_estimate=cost(2 * rank * total * width, total * width * 2),
        name="back",
    )(base, ortho_t, *columns, *sums)


def output_kernel(owner, factor, base_ref, ortho_ref, colsq_ref, *refs):
    me = lax.axis_index("fsdp")
    *pieces, nm_ref, nb_ref, up_ref, nm_tile, nb_tile, up_tile, sems = refs
    count, share, cols = nm_tile.shape[0], nm_tile.shape[2], nm_ref.shape[1]
    scale = lax.rsqrt(colsq_ref[...] + 1e-06)
    ortho = ortho_ref[...]
    over = (((1,), (1,)), ((), ()))

    def copies(n, width):
        there = pl.ds(pl.multiple_of(owner(me, n) * share, LANES), width)
        sides = (
            (nm_tile.at[n, :, :width], nm_ref.at[:, there]),
            (nb_tile.at[n, :width, :], nb_ref.at[there, :]),
            (up_tile.at[n, :, :width], up_ref.at[:, there]),
        )
        return [
            pltpu.make_async_copy(source, target, sems.at[n, which])
            for which, (source, target) in enumerate(sides)
        ]

    for n in range(count):

        def compute(width):
            there = pl.ds(pl.multiple_of(owner(me, n) * share, LANES), width)
            back = pieces[n][:width, :]
            unit = (back.astype(F32) * scale).astype(BF16)
            nb_tile[n, :width, :] = unit
            nm_tile[n, :, :width] = base_ref[:, there] - 0.05 * lax.dot_general(
                ortho, back, over, preferred_element_type=F32
            )
            up_tile[n, :, :width] = (
                factor * lax.dot_general(ortho, unit, over, preferred_element_type=F32)
            ).astype(BF16)
            for copy in copies(n, width):
                copy.start()

        by_width(owner(me, n), cols, share, 0, share, compute)

    for n in range(count):

        def wait(width):
            for copy in copies(n, width):
                copy.wait()

        by_width(owner(me, n), cols, share, 0, share, wait)


def output_call(owner, blocks, colsq, previous, base, ortho, factor):
    rows, cols = base.shape
    share, rank = blocks[0].shape
    count = len(blocks)
    previous = previous or ()
    vmem, hbm = pl.BlockSpec(memory_space=pltpu.VMEM), pl.BlockSpec(memory_space=pltpu.HBM)
    return pl.pallas_call(
        functools.partial(output_kernel, owner, factor),
        in_specs=[vmem] * (3 + count) + [hbm] * len(previous),
        out_specs=[hbm] * 3,
        out_shape=[
            jax.ShapeDtypeStruct((rows, cols), F32),
            jax.ShapeDtypeStruct((cols, rank), BF16),
            jax.ShapeDtypeStruct((rows, cols), BF16),
        ],
        scratch_shapes=[
            pltpu.VMEM((count, rows, share), F32),
            pltpu.VMEM((count, share, rank), BF16),
            pltpu.VMEM((count, rows, share), BF16),
            pltpu.SemaphoreType.DMA((count, 3)),
        ],
        input_output_aliases={3 + count + n: n for n in range(len(previous))},
        compiler_params=params(16),
        cost_estimate=cost(
            4 * rows * share * rank * count, count * share * (rows * 10 + rank * 4)
        ),
        name="outputs",
    )(base, ortho, colsq, *blocks, *previous)


def ring_order(chips):
    half = chips // 2
    return [2 * q for q in range(half)] + [2 * (chips - 1 - q) + 1 for q in range(half, chips)]


def ring_steps(count):
    order = ring_order(count // 2)
    after = dict(zip(order, order[1:] + order[:1]))
    up = [(2 * c + k, 2 * after[c] + k) for c in order for k in (0, 1)]
    down = [(b, a) for a, b in up]
    first = [p for p in up if p[0] % 2 == 0] + [p for p in down if p[0] % 2 == 1]
    second = [p for p in down if p[0] % 2 == 0] + [p for p in up if p[0] % 2 == 1]
    return first, second


def ring_owner(count, hops, other, me):
    chips = count // 2
    half = chips // 2
    core, chip = me & 1, me >> 1
    place = jnp.where((chip & 1) == 0, chip >> 1, chips - 1 - (chip >> 1))
    forward = hops * (2 * core - 1)
    place = lax.rem(place + chips + (-forward if other else forward), chips)
    chip = jnp.where(place < half, 2 * place, 2 * (chips - 1 - place) + 1)
    return 2 * chip + (1 - core if other else core)


def owner_of(ways):
    return lambda me, n: ways[n](me)


def swap_pairs(count):
    return [(n, n ^ 1) for n in range(count)]


def tie(x, *work):
    return lax.optimization_barrier((x, *work))[0] if work else x


def exchange_windows(count):
    chips, steps = count // 2, count // 4
    far, near = list(range(chips, count)), list(range(1, chips))
    each = -(-len(near) // (steps + 1))
    windows = [far[w : w + 1] + near[w * each : (w + 1) * each] for w in range(steps + 1)]
    return windows + [far[steps + 1 :]]


def gather_and_exchange(sketch, outgoing, count):
    chips = count // 2
    first, second = ring_steps(count)
    windows = exchange_windows(count)
    columns = {0: outgoing[0]}

    def exchange(window, *after):
        for k in window:
            pairs = [(n, n ^ k) for n in range(count)]
            columns[k] = lax.ppermute(tie(outgoing[k], *after), "fsdp", pairs)

    exchange(windows[0], sketch)
    sketch = sketch + lax.ppermute(sketch, "tp", [(0, 1), (1, 0)])
    hops, held = [0], [sketch]
    ahead = behind = sketch
    for step in range(1, chips // 2 + 1):
        work = [columns[k] for k in windows[step - 2]] if step > 1 else []
        ahead, behind, *_ = lax.optimization_barrier((ahead, behind, *work))
        exchange(windows[step], ahead, behind)
        ahead = lax.ppermute(ahead, "fsdp", first)
        held.append(ahead)
        hops.append(step)
        if 2 * step < chips:
            behind = lax.ppermute(behind, "fsdp", second)
            held.append(behind)
            hops.append(-step)
    exchange(windows[-1], ahead, behind)
    held = tie(jnp.stack(held), *[columns[k] for k in windows[-3]])
    other = lax.ppermute(held, "fsdp", swap_pairs(count))
    ways = [(h, far) for far in (False, True) for h in hops]
    return [held, other], ways, [columns[k] for k in range(count)]


def sum_rounds(count):
    rounds, bit = [("tp", [1])], 1
    while bit < count:
        rounds.append(("fsdp", [bit, 2 * bit, 3 * bit] if 2 * bit < count else [bit]))
        bit *= 4
    return rounds


def sum_round(x, axis, distances):
    size = lax.axis_size(axis)
    terms = [x]
    for d in distances:
        terms.append(lax.ppermute(x, axis, [(n, n ^ d) for n in range(size)]))
    if len(terms) == 2:
        return terms[0] + terms[1]
    return (terms[0] + terms[1]) + (terms[2] + terms[3])


def local(momentum, gradient, basis):
    rows, cols = momentum.shape
    rank = basis.shape[1]
    count = lax.axis_size("fsdp")
    tp_count = lax.axis_size("tp")
    chips = count // 2
    share = -(-cols // (count * LANES)) * LANES
    factor = math.sqrt(rows * count * cols * tp_count / rank)
    ring = tp_count == 2 and count in (16, 32) and share > SPLIT and (count - 1) * share < cols

    base = momentum + gradient.astype(F32)
    base_b = base.astype(BF16)
    sketch = jnp.dot(base_b, basis, preferred_element_type=F32)
    base = pltpu.with_memory_space_constraint(base, pltpu.VMEM)
    if ring:
        outgoing = pack_call(base, share, count)
        pieces, ways, columns = gather_and_exchange(sketch, outgoing, count)
        owner = owner_of([functools.partial(ring_owner, count, *way) for way in ways])
    else:
        padded = jnp.pad(base_b, ((0, 0), (0, share * count - cols)))
        columns = jnp.swapaxes(padded.reshape(rows, count, share), 0, 1)
        columns = lax.all_to_all(columns, "fsdp", 0, 0, tiled=True)
        columns = [columns.reshape(count * rows, share)]
        pieces = [lax.all_gather(lax.psum(sketch, "tp"), "fsdp", axis=0)]
        owner = lambda me, n: n
    ortho_t, ortho_here = factor_call(owner, base, pieces)
    sums = ()
    if ring:
        mine, theirs = half_call(ortho_t, columns[:chips], share)
        theirs = tie(theirs, *columns[chips:])
        sums = (mine, lax.ppermute(theirs, "fsdp", [(n, n ^ chips) for n in range(count)]))
    part, back = back_call(base, ortho_t, columns, share, sums)
    write = functools.partial(output_call, base=base, ortho=ortho_here, factor=factor)
    if not ring:
        whole = lax.all_gather(back, "fsdp", axis=0)
        blocks = [whole[n] for n in range(-(-cols // share))]
        colsq = lax.psum(part, ("fsdp", "tp"))
        return tuple(write(lambda me, n: n, blocks, colsq, None))

    turns, swap = ring_steps(count), swap_pairs(count)
    result = None
    partial = [part]
    for axis, distances in sum_rounds(count):
        partial.append(sum_round(partial[-1], axis, distances))
    colsq = partial[-1]
    arrived, blocks, owners, written = {0: back}, [], [], 0
    waiting = ()
    for n in range(chips):
        block = tie(arrived[n], *waiting)
        for later in (1, 2) if n == 0 else (n + 2,):
            if later < chips:
                arrived[later] = lax.ppermute(block, "fsdp", turns[(later + 1) % 2])
        blocks += [block, lax.ppermute(block, "fsdp", swap)]
        hops = (n + 1) // 2 if n % 2 else -(n // 2)
        owners += [functools.partial(ring_owner, count, hops, far) for far in (False, True)]
        if n == 0:
            waiting = (arrived[2], partial[-2])
            continue
        if n == 2:
            waiting = ()
            continue
        upto = 2 * n + (2 if n == 1 else 1 if n + 1 == chips else 0)
        upto = min(upto, written + 4) if n + 1 < chips else upto
        result = write(owner_of(owners[written:upto]), blocks[written:upto], colsq, result)
        written, waiting = upto, tuple(result)
    return tuple(write(owner_of(owners[written:]), blocks[written:], colsq, result))


def solution(mesh):
    return jax.shard_map(
        local,
        mesh=mesh,
        in_specs=(P("fsdp", "tp"), P("fsdp", "tp"), P("tp", None)),
        out_specs=(P("fsdp", "tp"), P("tp", None), P("fsdp", "tp")),
        check_vma=False,
    )
```

```python
import functools
import math

import jax
import jax.numpy as jnp
from jax import lax
from jax.experimental import pallas as pl
from jax.experimental.pallas import tpu as pltpu
from jax.sharding import PartitionSpec as P

LANES = 128
SUBLANES = 8
PANEL = 64
SPLIT = LANES
MIB = 1024 * 1024
FULL = lax.Precision.HIGHEST
F32 = jnp.float32
BF16 = jnp.bfloat16


def cost(flops, nbytes):
    return pl.CostEstimate(flops=flops, bytes_accessed=nbytes, transcendentals=0)


def params(mib):
    return pltpu.CompilerParams(vmem_limit_bytes=mib * MIB)


def by_width(block, cols, share, start, stop, act):
    last = (cols - 1) // share
    width, short = stop - start, max(0, min(cols - last * share, stop) - start)
    if short == width:
        act(width)
        return

    @pl.when(block < last)
    def _():
        act(width)

    if short:

        @pl.when(block == last)
        def _():
            act(short)


def pack_kernel(share, base_ref, *out_refs):
    cols = base_ref.shape[1]
    half, whole = len(out_refs) // 2, share - SPLIT
    last = (cols - 1) // share
    me = lax.axis_index("fsdp")

    def fill(out_ref, offset, owner, start, stop):
        short = max(0, min(cols - last * share, stop) - start)

        def put(width):
            if width:
                there = pl.ds(pl.multiple_of(owner * share + start, LANES), width)
                out_ref[:, offset : offset + width] = base_ref[:, there].astype(BF16)
            if width < stop - start:
                empty = jnp.zeros((out_ref.shape[0], stop - start - width), BF16)
                out_ref[:, offset + width : offset + stop - start] = empty

        if short == stop - start:
            put(short)
        else:
            pl.when(owner < last)(lambda: put(stop - start))
            pl.when(owner == last)(lambda: put(short))

    for n, out_ref in enumerate(out_refs):
        owner = me ^ n
        if n < half:
            fill(out_ref, 0, owner, 0, share)
            fill(out_ref, share, owner ^ half, whole, share)
        else:
            fill(out_ref, 0, owner, 0, whole)


def pack_call(base, share, count):
    rows, half = base.shape[0], count // 2
    widths = [share + SPLIT] * half + [share - SPLIT] * half
    vmem = pl.BlockSpec(memory_space=pltpu.VMEM)
    return pl.pallas_call(
        functools.partial(pack_kernel, share),
        in_specs=[vmem],
        out_specs=[vmem] * count,
        out_shape=[jax.ShapeDtypeStruct((rows, width), BF16) for width in widths],
        compiler_params=params(16),
        cost_estimate=cost(0, 6 * rows * share * count),
        name="pack",
    )(base)


def spread(x, lane):
    return jnp.broadcast_to(x[:, lane : lane + 1], (x.shape[0], LANES))


def row_of(x, row):
    return jnp.broadcast_to(x[row : row + 1, :], (SUBLANES, LANES))


def eliminate(block):
    sub = lax.broadcasted_iota(jnp.int32, (SUBLANES, LANES), 0)
    groups = PANEL // SUBLANES
    top = [block[SUBLANES * g : SUBLANES * (g + 1)] for g in range(groups)]
    for g in range(groups):
        first = PANEL + SUBLANES * g
        t = top[g]
        cols = [spread(t, first + j) for j in range(SUBLANES)]
        below = [[spread(top[i], first + j) for j in range(SUBLANES)] for i in range(g + 1, groups)]
        pivots = jnp.zeros((SUBLANES, LANES), F32)
        inverse, corner = [], {}
        for j in range(SUBLANES):
            pivot = row_of(cols[j], j)
            pivots = jnp.where(sub == j, pivot, pivots)
            inverse.append(1.0 / pivot)
            factor = jnp.where(sub > j, cols[j] * inverse[j], 0.0)
            t = t - factor * row_of(t, j)
            for k in range(j + 1, SUBLANES):
                corner[j, k] = row_of(cols[k], j)
                cols[k] = cols[k] - factor * corner[j, k]
        lines = [row_of(t, j) for j in range(SUBLANES)]
        for i in range(g + 1, groups):
            entries = below[i - g - 1]
            acc = top[i]
            for j in range(SUBLANES):
                factor = entries[j] * inverse[j]
                acc = acc - factor * lines[j]
                for k in range(j + 1, SUBLANES):
                    entries[k] = entries[k] - factor * corner[j, k]
            top[i] = acc
        top[g] = t * lax.rsqrt(pivots)
    return jnp.concatenate(top, axis=0)[:, :PANEL]


def dot(a, b, dims):
    return lax.dot_general(a, b, (dims, ((), ())), precision=FULL, preferred_element_type=F32)


def factor_kernel(stacks, owner, base_ref, *refs):
    me = lax.axis_index("fsdp")
    stacked, (ortho_t_ref, here_ref, whole_ref, work_ref, corner_ref) = refs[:stacks], refs[stacks:]
    corner_ref[...] = base_ref[:SUBLANES, :LANES]
    rows, rank = here_ref.shape
    total = whole_ref.shape[0]
    pieces = [stack.at[n] for stack in stacked for n in range(stack.shape[0])]
    for n, piece in enumerate(pieces):
        start = pl.multiple_of(owner(me, n) * rows, SUBLANES)
        whole_ref[pl.ds(start, rows), :] = piece[...]

    work_ref[:, :rank] = jnp.zeros((rank, rank), F32)
    chunk = 4 * rows

    @pl.loop(0, total // chunk)
    def _(n):
        part = whole_ref[pl.ds(pl.multiple_of(n * chunk, SUBLANES), chunk), :]
        work_ref[:, :rank] += dot(part, part, ((0,), (0,)))

    line = lax.broadcasted_iota(jnp.int32, (rank, rank), 0)
    column = lax.broadcasted_iota(jnp.int32, (rank, rank), 1)
    work_ref[:, rank:] = jnp.where(line == column, 1.0, 0.0).astype(F32)
    eye = jnp.where(line == column, 1.0, 0.0).astype(F32)[:PANEL, :PANEL]
    for start in range(0, rank, PANEL):
        stop = start + PANEL
        diagonal = work_ref[start:stop, start:stop]
        small = eliminate(jnp.concatenate([eye, diagonal], axis=1))
        panel = dot(small, work_ref[start:stop, :], ((1,), (0,)))
        work_ref[start:stop, :] = panel
        if stop < rank:
            work_ref[stop:, :] -= dot(panel[:, stop:rank], panel, ((0,), (0,)))
    inverse = work_ref[:, rank:]
    start = pl.multiple_of(me * rows, SUBLANES)
    here_ref[...] = dot(whole_ref[pl.ds(start, rows), :], inverse, ((1,), (1,))).astype(BF16)
    for n in range(0, total, chunk):
        ortho_t_ref[:, n : n + chunk] = dot(
            inverse, whole_ref[n : n + chunk, :], ((1,), (1,))
        ).astype(BF16)


def factor_call(owner, base, stacked):
    _, rows, rank = stacked[0].shape
    total = rows * sum(stack.shape[0] for stack in stacked)
    vmem = pl.BlockSpec(memory_space=pltpu.VMEM)
    return pl.pallas_call(
        functools.partial(factor_kernel, len(stacked), owner),
        in_specs=[vmem] * (1 + len(stacked)),
        out_specs=[vmem, vmem],
        out_shape=[
            jax.ShapeDtypeStruct((rank, total), BF16),
            jax.ShapeDtypeStruct((rows, rank), BF16),
        ],
        scratch_shapes=[
            pltpu.VMEM((total, rank), F32),
            pltpu.VMEM((rank, 2 * rank), F32),
            pltpu.VMEM((SUBLANES, LANES), F32),
        ],
        compiler_params=params(24),
        cost_estimate=cost(40 * total * rank * rank, total * rank * 6),
        name="factor",
    )(base, *stacked)


def half_kernel(share, ortho_t_ref, *refs):
    *near, mine_ref, theirs_ref, rows_ref = refs
    me = lax.axis_index("fsdp")
    rows, half = near[0].shape[0], len(near)
    for n, piece in enumerate(near):
        at = pl.ds(pl.multiple_of(((me ^ n) & (half - 1)) * rows, 16), rows)
        rows_ref[at, :] = piece[:, share - SPLIT :]
    first = pl.multiple_of((me & half) * rows, LANES)
    ortho_t = ortho_t_ref[:, pl.ds(first, half * rows)]
    back = jnp.dot(ortho_t, rows_ref[...], preferred_element_type=F32).T
    mine_ref[...] = back[:SPLIT]
    theirs_ref[...] = back[SPLIT:].astype(BF16)


def half_call(ortho_t, near, share):
    rank = ortho_t.shape[0]
    rows = near[0].shape[0] * len(near)
    vmem = pl.BlockSpec(memory_space=pltpu.VMEM)
    return pl.pallas_call(
        functools.partial(half_kernel, share),
        in_specs=[vmem] * (1 + len(near)),
        out_specs=[vmem] * 2,
        out_shape=[
            jax.ShapeDtypeStruct((SPLIT, rank), F32),
            jax.ShapeDtypeStruct((SPLIT, rank), BF16),
        ],
        scratch_shapes=[pltpu.VMEM((rows, 2 * SPLIT), BF16)],
        compiler_params=params(16),
        cost_estimate=cost(4 * rank * rows * SPLIT, rows * SPLIT * 4),
        name="half_back",
    )(ortho_t, *near)


def back_kernel(pieces, base_ref, ortho_t_ref, *refs):
    columns, (*sums, colsq_ref, back_ref, whole_ref, corner_ref) = refs[:pieces], refs[pieces:]
    corner_ref[...] = base_ref[:SUBLANES, :LANES]
    me = lax.axis_index("fsdp") if pieces > 1 else 0
    rows, width = columns[0].shape[0], whole_ref.shape[1]
    for n, piece in enumerate(columns):
        at = pl.ds(pl.multiple_of((me ^ n) * rows, 16), rows)
        whole_ref[at, :] = piece[:, :width]
    back_t = jnp.dot(ortho_t_ref[...], whole_ref[...], preferred_element_type=F32)
    back_ref[:width, :] = back_t.T.astype(BF16)
    if sums:
        mine_ref, other_ref = sums
        back_ref[width:, :] = (mine_ref[...] + other_ref[...].astype(F32)).astype(BF16)
    wide = back_ref[...].astype(F32)
    colsq_ref[...] = jnp.sum(wide * wide, axis=0, keepdims=True)


def back_call(base, ortho_t, columns, share, sums=()):
    rank, total = ortho_t.shape
    width = share - (SPLIT if sums else 0)
    vmem = pl.BlockSpec(memory_space=pltpu.VMEM)
    return pl.pallas_call(
        functools.partial(back_kernel, len(columns)),
        in_specs=[vmem] * (2 + len(columns) + len(sums)),
        out_specs=[vmem] * 2,
        out_shape=[
            jax.ShapeDtypeStruct((1, rank), F32),
            jax.ShapeDtypeStruct((share, rank), BF16),
        ],
        scratch_shapes=[pltpu.VMEM((total, width), BF16), pltpu.VMEM((SUBLANES, LANES), F32)],
        compiler_params=params(24),
        cost_estimate=cost(2 * rank * total * width, total * width * 2),
        name="back",
    )(base, ortho_t, *columns, *sums)


def output_kernel(owner, factor, base_ref, ortho_ref, colsq_ref, *refs):
    me = lax.axis_index("fsdp")
    *pieces, nm_ref, nb_ref, up_ref, nm_tile, nb_tile, up_tile, sems = refs
    count, share, cols = nm_tile.shape[0], nm_tile.shape[2], nm_ref.shape[1]
    scale = lax.rsqrt(colsq_ref[...] + 1e-06)
    ortho = ortho_ref[...]
    over = (((1,), (1,)), ((), ()))

    def copies(n, width):
        there = pl.ds(pl.multiple_of(owner(me, n) * share, LANES), width)
        sides = (
            (nm_tile.at[n, :, :width], nm_ref.at[:, there]),
            (nb_tile.at[n, :width, :], nb_ref.at[there, :]),
            (up_tile.at[n, :, :width], up_ref.at[:, there]),
        )
        return [
            pltpu.make_async_copy(source, target, sems.at[n, which])
            for which, (source, target) in enumerate(sides)
        ]

    for n in range(count):

        def compute(width):
            there = pl.ds(pl.multiple_of(owner(me, n) * share, LANES), width)
            back = pieces[n][:width, :]
            unit = (back.astype(F32) * scale).astype(BF16)
            nb_tile[n, :width, :] = unit
            nm_tile[n, :, :width] = base_ref[:, there] - 0.05 * lax.dot_general(
                ortho, back, over, preferred_element_type=F32
            )
            up_tile[n, :, :width] = (
                factor * lax.dot_general(ortho, unit, over, preferred_element_type=F32)
            ).astype(BF16)
            for copy in copies(n, width):
                copy.start()

        by_width(owner(me, n), cols, share, 0, share, compute)

    for n in range(count):

        def wait(width):
            for copy in copies(n, width):
                copy.wait()

        by_width(owner(me, n), cols, share, 0, share, wait)


def output_call(owner, blocks, colsq, previous, base, ortho, factor):
    rows, cols = base.shape
    share, rank = blocks[0].shape
    count = len(blocks)
    previous = previous or ()
    vmem, hbm = pl.BlockSpec(memory_space=pltpu.VMEM), pl.BlockSpec(memory_space=pltpu.HBM)
    return pl.pallas_call(
        functools.partial(output_kernel, owner, factor),
        in_specs=[vmem] * (3 + count) + [hbm] * len(previous),
        out_specs=[hbm] * 3,
        out_shape=[
            jax.ShapeDtypeStruct((rows, cols), F32),
            jax.ShapeDtypeStruct((cols, rank), BF16),
            jax.ShapeDtypeStruct((rows, cols), BF16),
        ],
        scratch_shapes=[
            pltpu.VMEM((count, rows, share), F32),
            pltpu.VMEM((count, share, rank), BF16),
            pltpu.VMEM((count, rows, share), BF16),
            pltpu.SemaphoreType.DMA((count, 3)),
        ],
        input_output_aliases={3 + count + n: n for n in range(len(previous))},
        compiler_params=params(16),
        cost_estimate=cost(
            4 * rows * share * rank * count, count * share * (rows * 10 + rank * 4)
        ),
        name="outputs",
    )(base, ortho, colsq, *blocks, *previous)


def ring_order(chips):
    half = chips // 2
    return [2 * q for q in range(half)] + [2 * (chips - 1 - q) + 1 for q in range(half, chips)]


def ring_steps(count):
    order = ring_order(count // 2)
    after = dict(zip(order, order[1:] + order[:1]))
    up = [(2 * c + k, 2 * after[c] + k) for c in order for k in (0, 1)]
    down = [(b, a) for a, b in up]
    first = [p for p in up if p[0] % 2 == 0] + [p for p in down if p[0] % 2 == 1]
    second = [p for p in down if p[0] % 2 == 0] + [p for p in up if p[0] % 2 == 1]
    return first, second


def ring_owner(count, hops, other, me):
    chips = count // 2
    half = chips // 2
    core, chip = me & 1, me >> 1
    place = jnp.where((chip & 1) == 0, chip >> 1, chips - 1 - (chip >> 1))
    forward = hops * (2 * core - 1)
    place = lax.rem(place + chips + (-forward if other else forward), chips)
    chip = jnp.where(place < half, 2 * place, 2 * (chips - 1 - place) + 1)
    return 2 * chip + (1 - core if other else core)


def owner_of(ways):
    return lambda me, n: ways[n](me)


def swap_pairs(count):
    return [(n, n ^ 1) for n in range(count)]


def tie(x, *work):
    return lax.optimization_barrier((x, *work))[0] if work else x


def exchange_windows(count):
    chips, steps = count // 2, count // 4
    far, near = list(range(chips, count)), list(range(1, chips))
    each = -(-len(near) // (steps + 1))
    windows = [far[w : w + 1] + near[w * each : (w + 1) * each] for w in range(steps + 1)]
    return windows + [far[steps + 1 :]]


def gather_and_exchange(sketch, outgoing, count):
    chips = count // 2
    first, second = ring_steps(count)
    windows = exchange_windows(count)
    columns = {0: outgoing[0]}

    def exchange(window, *after):
        for k in window:
            pairs = [(n, n ^ k) for n in range(count)]
            columns[k] = lax.ppermute(tie(outgoing[k], *after), "fsdp", pairs)

    exchange(windows[0], sketch)
    sketch = sketch + lax.ppermute(sketch, "tp", [(0, 1), (1, 0)])
    hops, held = [0], [sketch]
    ahead = behind = sketch
    for step in range(1, chips // 2 + 1):
        work = [columns[k] for k in windows[step - 2]] if step > 1 else []
        ahead, behind, *_ = lax.optimization_barrier((ahead, behind, *work))
        exchange(windows[step], ahead, behind)
        ahead = lax.ppermute(ahead, "fsdp", first)
        held.append(ahead)
        hops.append(step)
        if 2 * step < chips:
            behind = lax.ppermute(behind, "fsdp", second)
            held.append(behind)
            hops.append(-step)
    exchange(windows[-1], ahead, behind)
    held = tie(jnp.stack(held), *[columns[k] for k in windows[-3]])
    other = lax.ppermute(held, "fsdp", swap_pairs(count))
    ways = [(h, far) for far in (False, True) for h in hops]
    return [held, other], ways, [columns[k] for k in range(count)]


def sum_rounds(count):
    rounds, bit = [("tp", [1])], 1
    while bit < count:
        rounds.append(("fsdp", [bit, 2 * bit, 3 * bit] if 2 * bit < count else [bit]))
        bit *= 4
    return rounds


def sum_round(x, axis, distances):
    size = lax.axis_size(axis)
    terms = [x]
    for d in distances:
        terms.append(lax.ppermute(x, axis, [(n, n ^ d) for n in range(size)]))
    if len(terms) == 2:
        return terms[0] + terms[1]
    return (terms[0] + terms[1]) + (terms[2] + terms[3])


def local(momentum, gradient, basis):
    rows, cols = momentum.shape
    rank = basis.shape[1]
    count = lax.axis_size("fsdp")
    tp_count = lax.axis_size("tp")
    chips = count // 2
    share = -(-cols // (count * LANES)) * LANES
    factor = math.sqrt(rows * count * cols * tp_count / rank)
    ring = tp_count == 2 and count in (16, 32) and share > SPLIT and (count - 1) * share < cols

    base = momentum + gradient.astype(F32)
    base_b = base.astype(BF16)
    sketch = jnp.dot(base_b, basis, preferred_element_type=F32)
    base = pltpu.with_memory_space_constraint(base, pltpu.VMEM)
    if ring:
        outgoing = pack_call(base, share, count)
        pieces, ways, columns = gather_and_exchange(sketch, outgoing, count)
        owner = owner_of([functools.partial(ring_owner, count, *way) for way in ways])
    else:
        padded = jnp.pad(base_b, ((0, 0), (0, share * count - cols)))
        columns = jnp.swapaxes(padded.reshape(rows, count, share), 0, 1)
        columns = lax.all_to_all(columns, "fsdp", 0, 0, tiled=True)
        columns = [columns.reshape(count * rows, share)]
        pieces = [lax.all_gather(lax.psum(sketch, "tp"), "fsdp", axis=0)]
        owner = lambda me, n: n
    ortho_t, ortho_here = factor_call(owner, base, pieces)
    sums = ()
    if ring:
        mine, theirs = half_call(ortho_t, columns[:chips], share)
        theirs = tie(theirs, *columns[chips:])
        sums = (mine, lax.ppermute(theirs, "fsdp", [(n, n ^ chips) for n in range(count)]))
    part, back = back_call(base, ortho_t, columns, share, sums)
    write = functools.partial(output_call, base=base, ortho=ortho_here, factor=factor)
    if not ring:
        whole = lax.all_gather(back, "fsdp", axis=0)
        blocks = [whole[n] for n in range(-(-cols // share))]
        colsq = lax.psum(part, ("fsdp", "tp"))
        return tuple(write(lambda me, n: n, blocks, colsq, None))

    turns, swap = ring_steps(count), swap_pairs(count)
    result = None
    colsq = part
    for axis, distances in sum_rounds(count):
        colsq = sum_round(colsq, axis, distances)
    arrived, blocks, owners, written = {0: back}, [], [], 0
    waiting = ()
    for n in range(chips):
        block = tie(arrived[n], *waiting)
        for later in (1, 2) if n == 0 else (n + 2,):
            if later < chips:
                arrived[later] = lax.ppermute(block, "fsdp", turns[(later + 1) % 2])
        blocks += [block, lax.ppermute(block, "fsdp", swap)]
        hops = (n + 1) // 2 if n % 2 else -(n // 2)
        owners += [functools.partial(ring_owner, count, hops, far) for far in (False, True)]
        if n == 0:
            waiting = (arrived[2], colsq)
            continue
        if n == 2:
            waiting = ()
            continue
        upto = 2 * n + (2 if n == 1 else 1 if n + 1 == chips else 0)
        upto = min(upto, written + 4) if n + 1 < chips else upto
        result = write(owner_of(owners[written:upto]), blocks[written:upto], colsq, result)
        written, waiting = upto, tuple(result)
    return tuple(write(owner_of(owners[written:]), blocks[written:], colsq, result))


def solution(mesh):
    return jax.shard_map(
        local,
        mesh=mesh,
        in_specs=(P("fsdp", "tp"), P("fsdp", "tp"), P("tp", None)),
        out_specs=(P("fsdp", "tp"), P("tp", None), P("fsdp", "tp")),
        check_vma=False,
    )
```

```python
import functools
import math

import jax
import jax.numpy as jnp
from jax import lax
from jax.experimental import pallas as pl
from jax.experimental.pallas import tpu as pltpu
from jax.sharding import PartitionSpec as P

LANES = 128
SUBLANES = 8
PANEL = 64
MIB = 1024 * 1024
FULL = lax.Precision.HIGHEST
F32 = jnp.float32
BF16 = jnp.bfloat16


def cost(flops, nbytes):
    return pl.CostEstimate(flops=flops, bytes_accessed=nbytes, transcendentals=0)


def params(mib):
    return pltpu.CompilerParams(vmem_limit_bytes=mib * MIB)


def by_width(block, cols, share, start, stop, act):
    last = (cols - 1) // share
    width, short = stop - start, max(0, min(cols - last * share, stop) - start)
    if short == width:
        act(width)
        return

    @pl.when(block < last)
    def _():
        act(width)

    if short:

        @pl.when(block == last)
        def _():
            act(short)


def pack_kernel(base_ref, *out_refs):
    cols = base_ref.shape[1]
    share = out_refs[0].shape[1]
    me = lax.axis_index("fsdp")
    for n, out_ref in enumerate(out_refs):
        owner = me ^ n

        def fill(width):
            start = pl.multiple_of(owner * share, LANES)
            out_ref[:, :width] = base_ref[:, pl.ds(start, width)].astype(BF16)
            if width < share:
                out_ref[:, width:] = jnp.zeros((out_ref.shape[0], share - width), BF16)

        by_width(owner, cols, share, 0, share, fill)


def pack_call(base, share, count):
    rows = base.shape[0]
    vmem = pl.BlockSpec(memory_space=pltpu.VMEM)
    return pl.pallas_call(
        pack_kernel,
        in_specs=[vmem],
        out_specs=[vmem] * count,
        out_shape=[jax.ShapeDtypeStruct((rows, share), BF16)] * count,
        compiler_params=params(16),
        cost_estimate=cost(0, 6 * rows * share * count),
        name="pack",
    )(base)


def spread(x, lane):
    return jnp.broadcast_to(x[:, lane : lane + 1], (x.shape[0], LANES))


def row_of(x, row):
    return jnp.broadcast_to(x[row : row + 1, :], (SUBLANES, LANES))


def eliminate(block):
    sub = lax.broadcasted_iota(jnp.int32, (SUBLANES, LANES), 0)
    groups = PANEL // SUBLANES
    top = [block[SUBLANES * g : SUBLANES * (g + 1)] for g in range(groups)]
    for g in range(groups):
        first = PANEL + SUBLANES * g
        t = top[g]
        cols = [spread(t, first + j) for j in range(SUBLANES)]
        below = [[spread(top[i], first + j) for j in range(SUBLANES)] for i in range(g + 1, groups)]
        pivots = jnp.zeros((SUBLANES, LANES), F32)
        inverse, corner = [], {}
        for j in range(SUBLANES):
            pivot = row_of(cols[j], j)
            pivots = jnp.where(sub == j, pivot, pivots)
            inverse.append(1.0 / pivot)
            factor = jnp.where(sub > j, cols[j] * inverse[j], 0.0)
            t = t - factor * row_of(t, j)
            for k in range(j + 1, SUBLANES):
                corner[j, k] = row_of(cols[k], j)
                cols[k] = cols[k] - factor * corner[j, k]
        lines = [row_of(t, j) for j in range(SUBLANES)]
        for i in range(g + 1, groups):
            entries = below[i - g - 1]
            acc = top[i]
            for j in range(SUBLANES):
                factor = entries[j] * inverse[j]
                acc = acc - factor * lines[j]
                for k in range(j + 1, SUBLANES):
                    entries[k] = entries[k] - factor * corner[j, k]
            top[i] = acc
        top[g] = t * lax.rsqrt(pivots)
    return jnp.concatenate(top, axis=0)[:, :PANEL]


def dot(a, b, dims):
    return lax.dot_general(a, b, (dims, ((), ())), precision=FULL, preferred_element_type=F32)


def factor_kernel(stacks, owner, base_ref, *refs):
    me = lax.axis_index("fsdp")
    stacked, (ortho_t_ref, here_ref, whole_ref, work_ref, corner_ref) = refs[:stacks], refs[stacks:]
    corner_ref[...] = base_ref[:SUBLANES, :LANES]
    rows, rank = here_ref.shape
    total = whole_ref.shape[0]
    pieces = [stack.at[n] for stack in stacked for n in range(stack.shape[0])]
    for n, piece in enumerate(pieces):
        start = pl.multiple_of(owner(me, n) * rows, SUBLANES)
        whole_ref[pl.ds(start, rows), :] = piece[...]

    work_ref[:, :rank] = jnp.zeros((rank, rank), F32)
    chunk = 4 * rows

    @pl.loop(0, total // chunk)
    def _(n):
        part = whole_ref[pl.ds(pl.multiple_of(n * chunk, SUBLANES), chunk), :]
        work_ref[:, :rank] += dot(part, part, ((0,), (0,)))

    line = lax.broadcasted_iota(jnp.int32, (rank, rank), 0)
    column = lax.broadcasted_iota(jnp.int32, (rank, rank), 1)
    work_ref[:, rank:] = jnp.where(line == column, 1.0, 0.0).astype(F32)
    eye = jnp.where(line == column, 1.0, 0.0).astype(F32)[:PANEL, :PANEL]
    for start in range(0, rank, PANEL):
        stop = start + PANEL
        diagonal = work_ref[start:stop, start:stop]
        small = eliminate(jnp.concatenate([eye, diagonal], axis=1))
        panel = dot(small, work_ref[start:stop, :], ((1,), (0,)))
        work_ref[start:stop, :] = panel
        if stop < rank:
            work_ref[stop:, :] -= dot(panel[:, stop:rank], panel, ((0,), (0,)))
    inverse = work_ref[:, rank:]
    start = pl.multiple_of(me * rows, SUBLANES)
    here_ref[...] = dot(whole_ref[pl.ds(start, rows), :], inverse, ((1,), (1,))).astype(BF16)
    for n in range(0, total, chunk):
        ortho_t_ref[:, n : n + chunk] = dot(
            inverse, whole_ref[n : n + chunk, :], ((1,), (1,))
        ).astype(BF16)


def factor_call(owner, base, stacked):
    _, rows, rank = stacked[0].shape
    total = rows * sum(stack.shape[0] for stack in stacked)
    vmem = pl.BlockSpec(memory_space=pltpu.VMEM)
    return pl.pallas_call(
        functools.partial(factor_kernel, len(stacked), owner),
        in_specs=[vmem] * (1 + len(stacked)),
        out_specs=[vmem, vmem],
        out_shape=[
            jax.ShapeDtypeStruct((rank, total), BF16),
            jax.ShapeDtypeStruct((rows, rank), BF16),
        ],
        scratch_shapes=[
            pltpu.VMEM((total, rank), F32),
            pltpu.VMEM((rank, 2 * rank), F32),
            pltpu.VMEM((SUBLANES, LANES), F32),
        ],
        compiler_params=params(24),
        cost_estimate=cost(40 * total * rank * rank, total * rank * 6),
        name="factor",
    )(base, *stacked)


def back_kernel(base_ref, ortho_t_ref, *refs):
    *columns, colsq_ref, back_ref, whole_ref, corner_ref = refs
    corner_ref[...] = base_ref[:SUBLANES, :LANES]
    me = lax.axis_index("fsdp") if len(columns) > 1 else 0
    rows = columns[0].shape[0]
    for n, piece in enumerate(columns):
        whole_ref[pl.ds(pl.multiple_of((me ^ n) * rows, 16), rows), :] = piece[...]
    back_t = jnp.dot(ortho_t_ref[...], whole_ref[...], preferred_element_type=F32)
    back = back_t.T.astype(BF16)
    back_ref[...] = back
    wide = back.astype(F32)
    colsq_ref[...] = jnp.sum(wide * wide, axis=0, keepdims=True)


def back_call(base, ortho_t, columns):
    rank, total = ortho_t.shape
    share = columns[0].shape[1]
    vmem = pl.BlockSpec(memory_space=pltpu.VMEM)
    return pl.pallas_call(
        back_kernel,
        in_specs=[vmem] * (2 + len(columns)),
        out_specs=[vmem] * 2,
        out_shape=[
            jax.ShapeDtypeStruct((1, rank), F32),
            jax.ShapeDtypeStruct((share, rank), BF16),
        ],
        scratch_shapes=[pltpu.VMEM((total, share), BF16), pltpu.VMEM((SUBLANES, LANES), F32)],
        compiler_params=params(24),
        cost_estimate=cost(2 * rank * total * share, total * share * 2),
        name="back",
    )(base, ortho_t, *columns)


def output_kernel(owner, factor, base_ref, ortho_ref, colsq_ref, *refs):
    me = lax.axis_index("fsdp")
    *pieces, nm_ref, nb_ref, up_ref, nm_tile, nb_tile, up_tile, sems = refs
    count, share, cols = nm_tile.shape[0], nm_tile.shape[2], nm_ref.shape[1]
    scale = lax.rsqrt(colsq_ref[...] + 1e-06)
    ortho = ortho_ref[...]
    over = (((1,), (1,)), ((), ()))

    def copies(n, width):
        there = pl.ds(pl.multiple_of(owner(me, n) * share, LANES), width)
        sides = (
            (nm_tile.at[n, :, :width], nm_ref.at[:, there]),
            (nb_tile.at[n, :width, :], nb_ref.at[there, :]),
            (up_tile.at[n, :, :width], up_ref.at[:, there]),
        )
        return [
            pltpu.make_async_copy(source, target, sems.at[n, which])
            for which, (source, target) in enumerate(sides)
        ]

    for n in range(count):

        def compute(width):
            there = pl.ds(pl.multiple_of(owner(me, n) * share, LANES), width)
            back = pieces[n][:width, :]
            unit = (back.astype(F32) * scale).astype(BF16)
            nb_tile[n, :width, :] = unit
            nm_tile[n, :, :width] = base_ref[:, there] - 0.05 * lax.dot_general(
                ortho, back, over, preferred_element_type=F32
            )
            up_tile[n, :, :width] = (
                factor * lax.dot_general(ortho, unit, over, preferred_element_type=F32)
            ).astype(BF16)
            for copy in copies(n, width):
                copy.start()

        by_width(owner(me, n), cols, share, 0, share, compute)

    for n in range(count):

        def wait(width):
            for copy in copies(n, width):
                copy.wait()

        by_width(owner(me, n), cols, share, 0, share, wait)


def output_call(owner, blocks, colsq, previous, base, ortho, factor):
    rows, cols = base.shape
    share, rank = blocks[0].shape
    count = len(blocks)
    previous = previous or ()
    vmem, hbm = pl.BlockSpec(memory_space=pltpu.VMEM), pl.BlockSpec(memory_space=pltpu.HBM)
    return pl.pallas_call(
        functools.partial(output_kernel, owner, factor),
        in_specs=[vmem] * (3 + count) + [hbm] * len(previous),
        out_specs=[hbm] * 3,
        out_shape=[
            jax.ShapeDtypeStruct((rows, cols), F32),
            jax.ShapeDtypeStruct((cols, rank), BF16),
            jax.ShapeDtypeStruct((rows, cols), BF16),
        ],
        scratch_shapes=[
            pltpu.VMEM((count, rows, share), F32),
            pltpu.VMEM((count, share, rank), BF16),
            pltpu.VMEM((count, rows, share), BF16),
            pltpu.SemaphoreType.DMA((count, 3)),
        ],
        input_output_aliases={3 + count + n: n for n in range(len(previous))},
        compiler_params=params(16),
        cost_estimate=cost(
            4 * rows * share * rank * count, count * share * (rows * 10 + rank * 4)
        ),
        name="outputs",
    )(base, ortho, colsq, *blocks, *previous)


def ring_order(chips):
    half = chips // 2
    return [2 * q for q in range(half)] + [2 * (chips - 1 - q) + 1 for q in range(half, chips)]


def ring_steps(count):
    order = ring_order(count // 2)
    after = dict(zip(order, order[1:] + order[:1]))
    up = [(2 * c + k, 2 * after[c] + k) for c in order for k in (0, 1)]
    down = [(b, a) for a, b in up]
    first = [p for p in up if p[0] % 2 == 0] + [p for p in down if p[0] % 2 == 1]
    second = [p for p in down if p[0] % 2 == 0] + [p for p in up if p[0] % 2 == 1]
    return first, second


def ring_owner(count, hops, other, me):
    chips = count // 2
    half = chips // 2
    core, chip = me & 1, me >> 1
    place = jnp.where((chip & 1) == 0, chip >> 1, chips - 1 - (chip >> 1))
    forward = hops * (2 * core - 1)
    place = lax.rem(place + chips + (-forward if other else forward), chips)
    chip = jnp.where(place < half, 2 * place, 2 * (chips - 1 - place) + 1)
    return 2 * chip + (1 - core if other else core)


def owner_of(ways):
    return lambda me, n: ways[n](me)


def swap_pairs(count):
    return [(n, n ^ 1) for n in range(count)]


def tie(x, *work):
    return lax.optimization_barrier((x, *work))[0] if work else x


def exchange_windows(count):
    chips, steps = count // 2, count // 4
    far, near = list(range(chips, count)), list(range(1, chips))
    each = -(-len(near) // steps)
    windows = [far[w + 1 : w + 2] + near[(w - 1) * each : w * each] for w in range(1, steps + 1)]
    return [far[:2]] + windows + [far[steps + 2 :]]


def gather_and_exchange(sketch, outgoing, count):
    chips = count // 2
    first, second = ring_steps(count)
    windows = exchange_windows(count)
    columns = {0: outgoing[0]}

    def exchange(window, *after):
        for k in window:
            pairs = [(n, n ^ k) for n in range(count)]
            columns[k] = lax.ppermute(tie(outgoing[k], *after), "fsdp", pairs)

    exchange(windows[0], sketch)
    sketch = sketch + lax.ppermute(sketch, "tp", [(0, 1), (1, 0)])
    hops, held = [0], [sketch]
    ahead = behind = sketch
    for step in range(1, chips // 2 + 1):
        work = [columns[k] for k in windows[step - 2]] if step > 1 else []
        ahead, behind, *_ = lax.optimization_barrier((ahead, behind, *work))
        exchange(windows[step], ahead, behind)
        ahead = lax.ppermute(ahead, "fsdp", first)
        held.append(ahead)
        hops.append(step)
        if 2 * step < chips:
            behind = lax.ppermute(behind, "fsdp", second)
            held.append(behind)
            hops.append(-step)
    exchange(windows[-1], ahead, behind)
    held = tie(jnp.stack(held), *[columns[k] for k in windows[-3]])
    other = lax.ppermute(held, "fsdp", swap_pairs(count))
    ways = [(h, far) for far in (False, True) for h in hops]
    return [held, other], ways, [columns[k] for k in range(count)]


def sum_rounds(count):
    rounds, bit = [("tp", [1])], 1
    while bit < count:
        rounds.append(("fsdp", [bit, 2 * bit, 3 * bit] if 2 * bit < count else [bit]))
        bit *= 4
    return rounds


def sum_round(x, axis, distances):
    size = lax.axis_size(axis)
    terms = [x]
    for d in distances:
        terms.append(lax.ppermute(x, axis, [(n, n ^ d) for n in range(size)]))
    if len(terms) == 2:
        return terms[0] + terms[1]
    return (terms[0] + terms[1]) + (terms[2] + terms[3])


def local(momentum, gradient, basis):
    rows, cols = momentum.shape
    rank = basis.shape[1]
    count = lax.axis_size("fsdp")
    tp_count = lax.axis_size("tp")
    chips = count // 2
    share = -(-cols // (count * LANES)) * LANES
    factor = math.sqrt(rows * count * cols * tp_count / rank)
    ring = tp_count == 2 and count in (16, 32) and (count - 1) * share < cols

    base = momentum + gradient.astype(F32)
    base_b = base.astype(BF16)
    sketch = jnp.dot(base_b, basis, preferred_element_type=F32)
    base = pltpu.with_memory_space_constraint(base, pltpu.VMEM)
    if ring:
        outgoing = pack_call(base, share, count)
        pieces, ways, columns = gather_and_exchange(sketch, outgoing, count)
        owner = owner_of([functools.partial(ring_owner, count, *way) for way in ways])
    else:
        padded = jnp.pad(base_b, ((0, 0), (0, share * count - cols)))
        columns = jnp.swapaxes(padded.reshape(rows, count, share), 0, 1)
        columns = lax.all_to_all(columns, "fsdp", 0, 0, tiled=True)
        columns = [columns.reshape(count * rows, share)]
        pieces = [lax.all_gather(lax.psum(sketch, "tp"), "fsdp", axis=0)]
        owner = lambda me, n: n
    ortho_t, ortho_here = factor_call(owner, base, pieces)
    part, back = back_call(base, ortho_t, columns)
    write = functools.partial(output_call, base=base, ortho=ortho_here, factor=factor)
    if not ring:
        whole = lax.all_gather(back, "fsdp", axis=0)
        blocks = [whole[n] for n in range(-(-cols // share))]
        colsq = lax.psum(part, ("fsdp", "tp"))
        return tuple(write(lambda me, n: n, blocks, colsq, None))

    turns, swap = ring_steps(count), swap_pairs(count)
    colsq, result = part, None
    for axis, distances in sum_rounds(count):
        colsq = sum_round(colsq, axis, distances)
    arrived, blocks, owners, written = {0: back}, [], [], 0
    waiting = ()
    for n in range(chips):
        block = tie(arrived[n], *waiting)
        for later in (1, 2) if n == 0 else (n + 2,):
            if later < chips:
                arrived[later] = lax.ppermute(block, "fsdp", turns[(later + 1) % 2])
        blocks += [block, lax.ppermute(block, "fsdp", swap)]
        hops = (n + 1) // 2 if n % 2 else -(n // 2)
        owners += [functools.partial(ring_owner, count, hops, far) for far in (False, True)]
        if n == 0:
            waiting = (arrived[2], colsq)
            continue
        if n == 2:
            waiting = ()
            continue
        upto = 2 * n + (2 if n == 1 else 1 if n + 1 == chips else 0)
        upto = min(upto, written + 4) if n + 1 < chips else upto
        result = write(owner_of(owners[written:upto]), blocks[written:upto], colsq, result)
        written, waiting = upto, tuple(result)
    return tuple(write(owner_of(owners[written:]), blocks[written:], colsq, result))


def solution(mesh):
    return jax.shard_map(
        local,
        mesh=mesh,
        in_specs=(P("fsdp", "tp"), P("fsdp", "tp"), P("tp", None)),
        out_specs=(P("fsdp", "tp"), P("tp", None), P("fsdp", "tp")),
        check_vma=False,
    )
```

```python
import functools
import math

import jax
import jax.numpy as jnp
from jax import lax
from jax.experimental import pallas as pl
from jax.experimental.pallas import tpu as pltpu
from jax.sharding import PartitionSpec as P

LANES = 128
SUBLANES = 8
PANEL = 64
MIB = 1024 * 1024
FULL = lax.Precision.HIGHEST
F32 = jnp.float32
BF16 = jnp.bfloat16


def cost(flops, nbytes):
    return pl.CostEstimate(flops=flops, bytes_accessed=nbytes, transcendentals=0)


def params(mib):
    return pltpu.CompilerParams(vmem_limit_bytes=mib * MIB)


def by_width(block, cols, share, start, stop, act):
    last = (cols - 1) // share
    width, short = stop - start, max(0, min(cols - last * share, stop) - start)
    if short == width:
        act(width)
        return

    @pl.when(block < last)
    def _():
        act(width)

    if short:

        @pl.when(block == last)
        def _():
            act(short)


def pack_kernel(base_ref, *out_refs):
    cols = base_ref.shape[1]
    share = out_refs[0].shape[1]
    me = lax.axis_index("fsdp")
    for n, out_ref in enumerate(out_refs):
        owner = me ^ n

        def fill(width):
            start = pl.multiple_of(owner * share, LANES)
            out_ref[:, :width] = base_ref[:, pl.ds(start, width)].astype(BF16)
            if width < share:
                out_ref[:, width:] = jnp.zeros((out_ref.shape[0], share - width), BF16)

        by_width(owner, cols, share, 0, share, fill)


def pack_call(base, share, count):
    rows = base.shape[0]
    vmem = pl.BlockSpec(memory_space=pltpu.VMEM)
    return pl.pallas_call(
        pack_kernel,
        in_specs=[vmem],
        out_specs=[vmem] * count,
        out_shape=[jax.ShapeDtypeStruct((rows, share), BF16)] * count,
        compiler_params=params(16),
        cost_estimate=cost(0, 6 * rows * share * count),
        name="pack",
    )(base)


def spread(x, lane):
    return jnp.broadcast_to(x[:, lane : lane + 1], (x.shape[0], LANES))


def row_of(x, row):
    return jnp.broadcast_to(x[row : row + 1, :], (SUBLANES, LANES))


def eliminate(block):
    sub = lax.broadcasted_iota(jnp.int32, (SUBLANES, LANES), 0)
    groups = PANEL // SUBLANES
    top = [block[SUBLANES * g : SUBLANES * (g + 1)] for g in range(groups)]
    for g in range(groups):
        first = PANEL + SUBLANES * g
        t = top[g]
        cols = [spread(t, first + j) for j in range(SUBLANES)]
        below = [[spread(top[i], first + j) for j in range(SUBLANES)] for i in range(g + 1, groups)]
        pivots = jnp.zeros((SUBLANES, LANES), F32)
        inverse, corner = [], {}
        for j in range(SUBLANES):
            pivot = row_of(cols[j], j)
            pivots = jnp.where(sub == j, pivot, pivots)
            inverse.append(1.0 / pivot)
            factor = jnp.where(sub > j, cols[j] * inverse[j], 0.0)
            t = t - factor * row_of(t, j)
            for k in range(j + 1, SUBLANES):
                corner[j, k] = row_of(cols[k], j)
                cols[k] = cols[k] - factor * corner[j, k]
        lines = [row_of(t, j) for j in range(SUBLANES)]
        for i in range(g + 1, groups):
            entries = below[i - g - 1]
            acc = top[i]
            for j in range(SUBLANES):
                factor = entries[j] * inverse[j]
                acc = acc - factor * lines[j]
                for k in range(j + 1, SUBLANES):
                    entries[k] = entries[k] - factor * corner[j, k]
            top[i] = acc
        top[g] = t * lax.rsqrt(pivots)
    return jnp.concatenate(top, axis=0)[:, :PANEL]


def dot(a, b, dims):
    return lax.dot_general(a, b, (dims, ((), ())), precision=FULL, preferred_element_type=F32)


def factor_kernel(stacks, owner, base_ref, *refs):
    me = lax.axis_index("fsdp")
    stacked, (ortho_t_ref, here_ref, whole_ref, work_ref, corner_ref) = refs[:stacks], refs[stacks:]
    corner_ref[...] = base_ref[:SUBLANES, :LANES]
    rows, rank = here_ref.shape
    total = whole_ref.shape[0]
    pieces = [stack.at[n] for stack in stacked for n in range(stack.shape[0])]
    for n, piece in enumerate(pieces):
        start = pl.multiple_of(owner(me, n) * rows, SUBLANES)
        whole_ref[pl.ds(start, rows), :] = piece[...]

    work_ref[:, :rank] = jnp.zeros((rank, rank), F32)
    chunk = 4 * rows

    @pl.loop(0, total // chunk)
    def _(n):
        part = whole_ref[pl.ds(pl.multiple_of(n * chunk, SUBLANES), chunk), :]
        work_ref[:, :rank] += dot(part, part, ((0,), (0,)))

    line = lax.broadcasted_iota(jnp.int32, (rank, rank), 0)
    column = lax.broadcasted_iota(jnp.int32, (rank, rank), 1)
    work_ref[:, rank:] = jnp.where(line == column, 1.0, 0.0).astype(F32)
    eye = jnp.where(line == column, 1.0, 0.0).astype(F32)[:PANEL, :PANEL]
    for start in range(0, rank, PANEL):
        stop = start + PANEL
        diagonal = work_ref[start:stop, start:stop]
        small = eliminate(jnp.concatenate([eye, diagonal], axis=1))
        panel = dot(small, work_ref[start:stop, :], ((1,), (0,)))
        work_ref[start:stop, :] = panel
        if stop < rank:
            work_ref[stop:, :] -= dot(panel[:, stop:rank], panel, ((0,), (0,)))
    inverse = work_ref[:, rank:]
    start = pl.multiple_of(me * rows, SUBLANES)
    here_ref[...] = dot(whole_ref[pl.ds(start, rows), :], inverse, ((1,), (1,))).astype(BF16)
    for n in range(0, total, chunk):
        ortho_t_ref[:, n : n + chunk] = dot(
            inverse, whole_ref[n : n + chunk, :], ((1,), (1,))
        ).astype(BF16)


def factor_call(owner, base, stacked):
    _, rows, rank = stacked[0].shape
    total = rows * sum(stack.shape[0] for stack in stacked)
    vmem = pl.BlockSpec(memory_space=pltpu.VMEM)
    return pl.pallas_call(
        functools.partial(factor_kernel, len(stacked), owner),
        in_specs=[vmem] * (1 + len(stacked)),
        out_specs=[vmem, vmem],
        out_shape=[
            jax.ShapeDtypeStruct((rank, total), BF16),
            jax.ShapeDtypeStruct((rows, rank), BF16),
        ],
        scratch_shapes=[
            pltpu.VMEM((total, rank), F32),
            pltpu.VMEM((rank, 2 * rank), F32),
            pltpu.VMEM((SUBLANES, LANES), F32),
        ],
        compiler_params=params(24),
        cost_estimate=cost(40 * total * rank * rank, total * rank * 6),
        name="factor",
    )(base, *stacked)


def back_kernel(base_ref, ortho_t_ref, *refs):
    *columns, colsq_ref, back_ref, whole_ref, corner_ref = refs
    corner_ref[...] = base_ref[:SUBLANES, :LANES]
    me = lax.axis_index("fsdp") if len(columns) > 1 else 0
    rows = columns[0].shape[0]
    for n, piece in enumerate(columns):
        whole_ref[pl.ds(pl.multiple_of((me ^ n) * rows, 16), rows), :] = piece[...]
    back_t = jnp.dot(ortho_t_ref[...], whole_ref[...], preferred_element_type=F32)
    back = back_t.T.astype(BF16)
    back_ref[...] = back
    wide = back.astype(F32)
    colsq_ref[...] = jnp.sum(wide * wide, axis=0, keepdims=True)


def back_call(base, ortho_t, columns):
    rank, total = ortho_t.shape
    share = columns[0].shape[1]
    vmem = pl.BlockSpec(memory_space=pltpu.VMEM)
    return pl.pallas_call(
        back_kernel,
        in_specs=[vmem] * (2 + len(columns)),
        out_specs=[vmem] * 2,
        out_shape=[
            jax.ShapeDtypeStruct((1, rank), F32),
            jax.ShapeDtypeStruct((share, rank), BF16),
        ],
        scratch_shapes=[pltpu.VMEM((total, share), BF16), pltpu.VMEM((SUBLANES, LANES), F32)],
        compiler_params=params(24),
        cost_estimate=cost(2 * rank * total * share, total * share * 2),
        name="back",
    )(base, ortho_t, *columns)


def output_kernel(owner, factor, base_ref, ortho_ref, colsq_ref, *refs):
    me = lax.axis_index("fsdp")
    *pieces, nm_ref, nb_ref, up_ref, nm_tile, nb_tile, up_tile, sems = refs
    count, share, cols = nm_tile.shape[0], nm_tile.shape[2], nm_ref.shape[1]
    scale = lax.rsqrt(colsq_ref[...] + 1e-06)
    ortho = ortho_ref[...]
    over = (((1,), (1,)), ((), ()))

    def copies(n, width):
        there = pl.ds(pl.multiple_of(owner(me, n) * share, LANES), width)
        sides = (
            (nm_tile.at[n, :, :width], nm_ref.at[:, there]),
            (nb_tile.at[n, :width, :], nb_ref.at[there, :]),
            (up_tile.at[n, :, :width], up_ref.at[:, there]),
        )
        return [
            pltpu.make_async_copy(source, target, sems.at[n, which])
            for which, (source, target) in enumerate(sides)
        ]

    for n in range(count):

        def compute(width):
            there = pl.ds(pl.multiple_of(owner(me, n) * share, LANES), width)
            back = pieces[n][:width, :]
            unit = (back.astype(F32) * scale).astype(BF16)
            nb_tile[n, :width, :] = unit
            nm_tile[n, :, :width] = base_ref[:, there] - 0.05 * lax.dot_general(
                ortho, back, over, preferred_element_type=F32
            )
            up_tile[n, :, :width] = (
                factor * lax.dot_general(ortho, unit, over, preferred_element_type=F32)
            ).astype(BF16)
            for copy in copies(n, width):
                copy.start()

        by_width(owner(me, n), cols, share, 0, share, compute)

    for n in range(count):

        def wait(width):
            for copy in copies(n, width):
                copy.wait()

        by_width(owner(me, n), cols, share, 0, share, wait)


def output_call(owner, blocks, colsq, previous, base, ortho, factor):
    rows, cols = base.shape
    share, rank = blocks[0].shape
    count = len(blocks)
    previous = previous or ()
    vmem, hbm = pl.BlockSpec(memory_space=pltpu.VMEM), pl.BlockSpec(memory_space=pltpu.HBM)
    return pl.pallas_call(
        functools.partial(output_kernel, owner, factor),
        in_specs=[vmem] * (3 + count) + [hbm] * len(previous),
        out_specs=[hbm] * 3,
        out_shape=[
            jax.ShapeDtypeStruct((rows, cols), F32),
            jax.ShapeDtypeStruct((cols, rank), BF16),
            jax.ShapeDtypeStruct((rows, cols), BF16),
        ],
        scratch_shapes=[
            pltpu.VMEM((count, rows, share), F32),
            pltpu.VMEM((count, share, rank), BF16),
            pltpu.VMEM((count, rows, share), BF16),
            pltpu.SemaphoreType.DMA((count, 3)),
        ],
        input_output_aliases={3 + count + n: n for n in range(len(previous))},
        compiler_params=params(16),
        cost_estimate=cost(
            4 * rows * share * rank * count, count * share * (rows * 10 + rank * 4)
        ),
        name="outputs",
    )(base, ortho, colsq, *blocks, *previous)


def ring_order(chips):
    half = chips // 2
    return [2 * q for q in range(half)] + [2 * (chips - 1 - q) + 1 for q in range(half, chips)]


def ring_steps(count):
    order = ring_order(count // 2)
    after = dict(zip(order, order[1:] + order[:1]))
    up = [(2 * c + k, 2 * after[c] + k) for c in order for k in (0, 1)]
    down = [(b, a) for a, b in up]
    first = [p for p in up if p[0] % 2 == 0] + [p for p in down if p[0] % 2 == 1]
    second = [p for p in down if p[0] % 2 == 0] + [p for p in up if p[0] % 2 == 1]
    return first, second


def ring_owner(count, hops, other, me, sign=1):
    chips = count // 2
    half = chips // 2
    core, chip = me & 1, me >> 1
    place = jnp.where((chip & 1) == 0, chip >> 1, chips - 1 - (chip >> 1))
    forward = hops * sign * (2 * core - 1)
    place = lax.rem(place + chips + (-forward if other else forward), chips)
    chip = jnp.where(place < half, 2 * place, 2 * (chips - 1 - place) + 1)
    return 2 * chip + (1 - core if other else core)


def owner_of(ways):
    return lambda me, n: ways[n](me)


def swap_pairs(count):
    return [(n, n ^ 1) for n in range(count)]


def tie(x, *work):
    return lax.optimization_barrier((x, *work))[0] if work else x


def exchange_windows(count):
    chips, steps = count // 2, count // 4
    far, near = list(range(chips, count)), list(range(1, chips))
    each = -(-len(near) // (steps + 1))
    windows = [far[w : w + 1] + near[w * each : (w + 1) * each] for w in range(steps + 1)]
    return windows + [far[steps + 1 :]]


def gather_and_exchange(sketch, outgoing, count):
    chips = count // 2
    first, second = ring_steps(count)
    windows = exchange_windows(count)
    columns = {0: outgoing[0]}

    def exchange(window, *after):
        for k in window:
            pairs = [(n, n ^ k) for n in range(count)]
            columns[k] = lax.ppermute(tie(outgoing[k], *after), "fsdp", pairs)

    exchange(windows[0], sketch)
    across = [(0, 1), (1, 0)]
    sketch = sketch + lax.ppermute(sketch, "tp", across)
    turns = [(2 * a + half, 2 * b + half) for half in (0, 1) for a, b in (first, second)[half]]
    hops, held, block = [0], [sketch], sketch
    for step in range(1, chips // 2 + 1):
        work = [columns[k] for k in windows[step - 2]] if step > 1 else []
        block = tie(block, *work)
        exchange(windows[step], block)
        block = lax.ppermute(block, ("fsdp", "tp"), turns)
        held.append(block)
        hops.append(step)
        if 2 * step < chips:
            held.append(lax.ppermute(block, "tp", across))
            hops.append(-step)
    exchange(windows[-1], block)
    held = tie(jnp.stack(held), *[columns[k] for k in windows[-3]])
    other = lax.ppermute(held, "fsdp", swap_pairs(count))
    ways = [(h, far) for far in (False, True) for h in hops]
    return [held, other], ways, [columns[k] for k in range(count)]


def sum_rounds(count):
    rounds, bit = [("tp", [1])], 1
    while bit < count:
        rounds.append(("fsdp", [bit, 2 * bit, 3 * bit] if 2 * bit < count else [bit]))
        bit *= 4
    return rounds


def sum_round(x, axis, distances):
    size = lax.axis_size(axis)
    terms = [x]
    for d in distances:
        terms.append(lax.ppermute(x, axis, [(n, n ^ d) for n in range(size)]))
    if len(terms) == 2:
        return terms[0] + terms[1]
    return (terms[0] + terms[1]) + (terms[2] + terms[3])


def local(momentum, gradient, basis):
    rows, cols = momentum.shape
    rank = basis.shape[1]
    count = lax.axis_size("fsdp")
    tp_count = lax.axis_size("tp")
    chips = count // 2
    share = -(-cols // (count * LANES)) * LANES
    factor = math.sqrt(rows * count * cols * tp_count / rank)
    ring = tp_count == 2 and count in (16, 32) and (count - 1) * share < cols

    base = momentum + gradient.astype(F32)
    base_b = base.astype(BF16)
    sketch = jnp.dot(base_b, basis, preferred_element_type=F32)
    base = pltpu.with_memory_space_constraint(base, pltpu.VMEM)
    if ring:
        outgoing = pack_call(base, share, count)
        pieces, ways, columns = gather_and_exchange(sketch, outgoing, count)
        ways = [functools.partial(ring_owner, count, *way) for way in ways]
        owner = lambda me, n: ways[n](me, 1 - 2 * lax.axis_index("tp"))
    else:
        padded = jnp.pad(base_b, ((0, 0), (0, share * count - cols)))
        columns = jnp.swapaxes(padded.reshape(rows, count, share), 0, 1)
        columns = lax.all_to_all(columns, "fsdp", 0, 0, tiled=True)
        columns = [columns.reshape(count * rows, share)]
        pieces = [lax.all_gather(lax.psum(sketch, "tp"), "fsdp", axis=0)]
        owner = lambda me, n: n
    ortho_t, ortho_here = factor_call(owner, base, pieces)
    part, back = back_call(base, ortho_t, columns)
    write = functools.partial(output_call, base=base, ortho=ortho_here, factor=factor)
    if not ring:
        whole = lax.all_gather(back, "fsdp", axis=0)
        blocks = [whole[n] for n in range(-(-cols // share))]
        colsq = lax.psum(part, ("fsdp", "tp"))
        return tuple(write(lambda me, n: n, blocks, colsq, None))

    turns, swap = ring_steps(count), swap_pairs(count)
    colsq, result = part, None
    for axis, distances in sum_rounds(count):
        colsq = sum_round(colsq, axis, distances)
    arrived, blocks, owners, written = {0: back}, [], [], 0
    waiting = ()
    for n in range(chips):
        block = tie(arrived[n], *waiting)
        for later in (1, 2) if n == 0 else (n + 2,):
            if later < chips:
                arrived[later] = lax.ppermute(block, "fsdp", turns[(later + 1) % 2])
        blocks += [block, lax.ppermute(block, "fsdp", swap)]
        hops = (n + 1) // 2 if n % 2 else -(n // 2)
        owners += [functools.partial(ring_owner, count, hops, far) for far in (False, True)]
        if n == 0:
            waiting = (arrived[2], colsq)
            continue
        if n == 2:
            waiting = ()
            continue
        upto = 2 * n + (2 if n == 1 else 1 if n + 1 == chips else 0)
        upto = min(upto, written + 4) if n + 1 < chips else upto
        result = write(owner_of(owners[written:upto]), blocks[written:upto], colsq, result)
        written, waiting = upto, tuple(result)
    return tuple(write(owner_of(owners[written:]), blocks[written:], colsq, result))


def solution(mesh):
    return jax.shard_map(
        local,
        mesh=mesh,
        in_specs=(P("fsdp", "tp"), P("fsdp", "tp"), P("tp", None)),
        out_specs=(P("fsdp", "tp"), P("tp", None), P("fsdp", "tp")),
        check_vma=False,
    )
```

```python
import functools
import math

import jax
import jax.numpy as jnp
from jax import lax
from jax.experimental import pallas as pl
from jax.experimental.pallas import tpu as pltpu
from jax.sharding import PartitionSpec as P

LANES = 128
SUBLANES = 8
PANEL = 64
MIB = 1024 * 1024
FULL = lax.Precision.HIGHEST
F32 = jnp.float32
BF16 = jnp.bfloat16


def cost(flops, nbytes):
    return pl.CostEstimate(flops=flops, bytes_accessed=nbytes, transcendentals=0)


def params(mib):
    return pltpu.CompilerParams(vmem_limit_bytes=mib * MIB)


def by_width(block, cols, share, start, stop, act):
    last = (cols - 1) // share
    width, short = stop - start, max(0, min(cols - last * share, stop) - start)
    if short == width:
        act(width)
        return

    @pl.when(block < last)
    def _():
        act(width)

    if short:

        @pl.when(block == last)
        def _():
            act(short)


def pack_kernel(base_ref, *out_refs):
    cols = base_ref.shape[1]
    share = out_refs[0].shape[1]
    me = lax.axis_index("fsdp")
    for n, out_ref in enumerate(out_refs):
        owner = me ^ n

        def fill(width):
            start = pl.multiple_of(owner * share, LANES)
            out_ref[:, :width] = base_ref[:, pl.ds(start, width)].astype(BF16)
            if width < share:
                out_ref[:, width:] = jnp.zeros((out_ref.shape[0], share - width), BF16)

        by_width(owner, cols, share, 0, share, fill)


def pack_call(base, share, count):
    rows = base.shape[0]
    vmem = pl.BlockSpec(memory_space=pltpu.VMEM)
    return pl.pallas_call(
        pack_kernel,
        in_specs=[vmem],
        out_specs=[vmem] * count,
        out_shape=[jax.ShapeDtypeStruct((rows, share), BF16)] * count,
        compiler_params=params(16),
        cost_estimate=cost(0, 6 * rows * share * count),
        name="pack",
    )(base)


def spread(x, lane):
    return jnp.broadcast_to(x[:, lane : lane + 1], (x.shape[0], LANES))


def row_of(x, row):
    return jnp.broadcast_to(x[row : row + 1, :], (SUBLANES, LANES))


def eliminate(block):
    sub = lax.broadcasted_iota(jnp.int32, (SUBLANES, LANES), 0)
    groups = PANEL // SUBLANES
    top = [block[SUBLANES * g : SUBLANES * (g + 1)] for g in range(groups)]
    for g in range(groups):
        first = PANEL + SUBLANES * g
        t = top[g]
        cols = [spread(t, first + j) for j in range(SUBLANES)]
        below = [[spread(top[i], first + j) for j in range(SUBLANES)] for i in range(g + 1, groups)]
        pivots = jnp.zeros((SUBLANES, LANES), F32)
        inverse, corner = [], {}
        for j in range(SUBLANES):
            pivot = row_of(cols[j], j)
            pivots = jnp.where(sub == j, pivot, pivots)
            inverse.append(1.0 / pivot)
            factor = jnp.where(sub > j, cols[j] * inverse[j], 0.0)
            t = t - factor * row_of(t, j)
            for k in range(j + 1, SUBLANES):
                corner[j, k] = row_of(cols[k], j)
                cols[k] = cols[k] - factor * corner[j, k]
        lines = [row_of(t, j) for j in range(SUBLANES)]
        for i in range(g + 1, groups):
            entries = below[i - g - 1]
            acc = top[i]
            for j in range(SUBLANES):
                factor = entries[j] * inverse[j]
                acc = acc - factor * lines[j]
                for k in range(j + 1, SUBLANES):
                    entries[k] = entries[k] - factor * corner[j, k]
            top[i] = acc
        top[g] = t * lax.rsqrt(pivots)
    return jnp.concatenate(top, axis=0)[:, :PANEL]


def dot(a, b, dims):
    return lax.dot_general(a, b, (dims, ((), ())), precision=FULL, preferred_element_type=F32)


def factor_kernel(stacks, owner, base_ref, *refs):
    me = lax.axis_index("fsdp")
    stacked, (ortho_t_ref, here_ref, whole_ref, work_ref, corner_ref) = refs[:stacks], refs[stacks:]
    corner_ref[...] = base_ref[:SUBLANES, :LANES]
    rows, rank = here_ref.shape
    total = whole_ref.shape[0]
    pieces = [stack.at[n] for stack in stacked for n in range(stack.shape[0])]
    for n, piece in enumerate(pieces):
        start = pl.multiple_of(owner(me, n) * rows, SUBLANES)
        whole_ref[pl.ds(start, rows), :] = piece[...]

    work_ref[:, :rank] = jnp.zeros((rank, rank), F32)
    chunk = 4 * rows

    @pl.loop(0, total // chunk)
    def _(n):
        part = whole_ref[pl.ds(pl.multiple_of(n * chunk, SUBLANES), chunk), :]
        work_ref[:, :rank] += dot(part, part, ((0,), (0,)))

    line = lax.broadcasted_iota(jnp.int32, (rank, rank), 0)
    column = lax.broadcasted_iota(jnp.int32, (rank, rank), 1)
    work_ref[:, rank:] = jnp.where(line == column, 1.0, 0.0).astype(F32)
    eye = jnp.where(line == column, 1.0, 0.0).astype(F32)[:PANEL, :PANEL]
    for start in range(0, rank, PANEL):
        stop = start + PANEL
        diagonal = work_ref[start:stop, start:stop]
        small = eliminate(jnp.concatenate([eye, diagonal], axis=1))
        panel = dot(small, work_ref[start:stop, :], ((1,), (0,)))
        work_ref[start:stop, :] = panel
        if stop < rank:
            work_ref[stop:, :] -= dot(panel[:, stop:rank], panel, ((0,), (0,)))
    inverse = work_ref[:, rank:]
    start = pl.multiple_of(me * rows, SUBLANES)
    here_ref[...] = dot(whole_ref[pl.ds(start, rows), :], inverse, ((1,), (1,))).astype(BF16)
    for n in range(0, total, chunk):
        ortho_t_ref[:, n : n + chunk] = dot(
            inverse, whole_ref[n : n + chunk, :], ((1,), (1,))
        ).astype(BF16)


def factor_call(owner, base, stacked):
    _, rows, rank = stacked[0].shape
    total = rows * sum(stack.shape[0] for stack in stacked)
    vmem = pl.BlockSpec(memory_space=pltpu.VMEM)
    return pl.pallas_call(
        functools.partial(factor_kernel, len(stacked), owner),
        in_specs=[vmem] * (1 + len(stacked)),
        out_specs=[vmem, vmem],
        out_shape=[
            jax.ShapeDtypeStruct((rank, total), BF16),
            jax.ShapeDtypeStruct((rows, rank), BF16),
        ],
        scratch_shapes=[
            pltpu.VMEM((total, rank), F32),
            pltpu.VMEM((rank, 2 * rank), F32),
            pltpu.VMEM((SUBLANES, LANES), F32),
        ],
        compiler_params=params(24),
        cost_estimate=cost(40 * total * rank * rank, total * rank * 6),
        name="factor",
    )(base, *stacked)


def back_kernel(base_ref, ortho_t_ref, *refs):
    *columns, colsq_ref, back_ref, whole_ref, corner_ref = refs
    corner_ref[...] = base_ref[:SUBLANES, :LANES]
    me = lax.axis_index("fsdp") if len(columns) > 1 else 0
    rows = columns[0].shape[0]
    for n, piece in enumerate(columns):
        whole_ref[pl.ds(pl.multiple_of((me ^ n) * rows, 16), rows), :] = piece[...]
    back_t = jnp.dot(ortho_t_ref[...], whole_ref[...], preferred_element_type=F32)
    back = back_t.T.astype(BF16)
    back_ref[...] = back
    wide = back.astype(F32)
    colsq_ref[...] = jnp.sum(wide * wide, axis=0, keepdims=True)


def back_call(base, ortho_t, columns):
    rank, total = ortho_t.shape
    share = columns[0].shape[1]
    vmem = pl.BlockSpec(memory_space=pltpu.VMEM)
    return pl.pallas_call(
        back_kernel,
        in_specs=[vmem] * (2 + len(columns)),
        out_specs=[vmem] * 2,
        out_shape=[
            jax.ShapeDtypeStruct((1, rank), F32),
            jax.ShapeDtypeStruct((share, rank), BF16),
        ],
        scratch_shapes=[pltpu.VMEM((total, share), BF16), pltpu.VMEM((SUBLANES, LANES), F32)],
        compiler_params=params(24),
        cost_estimate=cost(2 * rank * total * share, total * share * 2),
        name="back",
    )(base, ortho_t, *columns)


def output_kernel(owner, factor, base_ref, ortho_ref, colsq_ref, *refs):
    me = lax.axis_index("fsdp")
    *pieces, nm_ref, nb_ref, up_ref, nm_tile, nb_tile, up_tile, sems = refs
    count, share, cols = nm_tile.shape[0], nm_tile.shape[2], nm_ref.shape[1]
    scale = lax.rsqrt(colsq_ref[...] + 1e-06)
    ortho = ortho_ref[...]
    over = (((1,), (1,)), ((), ()))

    def copies(n, width):
        there = pl.ds(pl.multiple_of(owner(me, n) * share, LANES), width)
        sides = (
            (nm_tile.at[n, :, :width], nm_ref.at[:, there]),
            (nb_tile.at[n, :width, :], nb_ref.at[there, :]),
            (up_tile.at[n, :, :width], up_ref.at[:, there]),
        )
        return [
            pltpu.make_async_copy(source, target, sems.at[n, which])
            for which, (source, target) in enumerate(sides)
        ]

    for n in range(count):

        def compute(width):
            there = pl.ds(pl.multiple_of(owner(me, n) * share, LANES), width)
            back = pieces[n][:width, :]
            unit = (back.astype(F32) * scale).astype(BF16)
            nb_tile[n, :width, :] = unit
            nm_tile[n, :, :width] = base_ref[:, there] - 0.05 * lax.dot_general(
                ortho, back, over, preferred_element_type=F32
            )
            up_tile[n, :, :width] = (
                factor * lax.dot_general(ortho, unit, over, preferred_element_type=F32)
            ).astype(BF16)
            for copy in copies(n, width):
                copy.start()

        by_width(owner(me, n), cols, share, 0, share, compute)

    for n in range(count):

        def wait(width):
            for copy in copies(n, width):
                copy.wait()

        by_width(owner(me, n), cols, share, 0, share, wait)


def output_call(owner, blocks, colsq, previous, base, ortho, factor):
    rows, cols = base.shape
    share, rank = blocks[0].shape
    count = len(blocks)
    previous = previous or ()
    vmem, hbm = pl.BlockSpec(memory_space=pltpu.VMEM), pl.BlockSpec(memory_space=pltpu.HBM)
    return pl.pallas_call(
        functools.partial(output_kernel, owner, factor),
        in_specs=[vmem] * (3 + count) + [hbm] * len(previous),
        out_specs=[hbm] * 3,
        out_shape=[
            jax.ShapeDtypeStruct((rows, cols), F32),
            jax.ShapeDtypeStruct((cols, rank), BF16),
            jax.ShapeDtypeStruct((rows, cols), BF16),
        ],
        scratch_shapes=[
            pltpu.VMEM((count, rows, share), F32),
            pltpu.VMEM((count, share, rank), BF16),
            pltpu.VMEM((count, rows, share), BF16),
            pltpu.SemaphoreType.DMA((count, 3)),
        ],
        input_output_aliases={3 + count + n: n for n in range(len(previous))},
        compiler_params=params(16),
        cost_estimate=cost(
            4 * rows * share * rank * count, count * share * (rows * 10 + rank * 4)
        ),
        name="outputs",
    )(base, ortho, colsq, *blocks, *previous)


def ring_order(chips):
    half = chips // 2
    return [2 * q for q in range(half)] + [2 * (chips - 1 - q) + 1 for q in range(half, chips)]


def ring_steps(count):
    order = ring_order(count // 2)
    after = dict(zip(order, order[1:] + order[:1]))
    up = [(2 * c + k, 2 * after[c] + k) for c in order for k in (0, 1)]
    down = [(b, a) for a, b in up]
    first = [p for p in up if p[0] % 2 == 0] + [p for p in down if p[0] % 2 == 1]
    second = [p for p in down if p[0] % 2 == 0] + [p for p in up if p[0] % 2 == 1]
    return first, second


def ring_owner(count, hops, other, me, sign=1):
    chips = count // 2
    half = chips // 2
    core, chip = me & 1, me >> 1
    place = jnp.where((chip & 1) == 0, chip >> 1, chips - 1 - (chip >> 1))
    forward = hops * sign * (2 * core - 1)
    place = lax.rem(place + chips + (-forward if other else forward), chips)
    chip = jnp.where(place < half, 2 * place, 2 * (chips - 1 - place) + 1)
    return 2 * chip + (1 - core if other else core)


def owner_of(ways):
    return lambda me, n: ways[n](me)


def swap_pairs(count):
    return [(n, n ^ 1) for n in range(count)]


def tie(x, *work):
    return lax.optimization_barrier((x, *work))[0] if work else x


def exchange_windows(count):
    chips, steps = count // 2, count // 4
    far, near = list(range(chips, count)), list(range(1, chips))
    each = -(-len(near) // steps)
    windows = [far[w + 1 : w + 2] + near[(w - 1) * each : w * each] for w in range(1, steps + 1)]
    return [far[:2]] + windows + [far[steps + 2 :]]


def gather_and_exchange(sketch, outgoing, count):
    chips = count // 2
    first, second = ring_steps(count)
    windows = exchange_windows(count)
    columns = {0: outgoing[0]}

    def exchange(window, *after):
        for k in window:
            pairs = [(n, n ^ k) for n in range(count)]
            columns[k] = lax.ppermute(tie(outgoing[k], *after), "fsdp", pairs)

    exchange(windows[0], sketch)
    across = [(0, 1), (1, 0)]
    sketch = sketch + lax.ppermute(sketch, "tp", across)
    turns = [(2 * a + half, 2 * b + half) for half in (0, 1) for a, b in (first, second)[half]]
    hops, held, block = [0], [sketch], sketch
    for step in range(1, chips // 2 + 1):
        work = [columns[k] for k in windows[step - 2]] if step > 1 else []
        block = tie(block, *work)
        exchange(windows[step], block)
        block = lax.ppermute(block, ("fsdp", "tp"), turns)
        held.append(block)
        hops.append(step)
        if 2 * step < chips:
            held.append(lax.ppermute(block, "tp", across))
            hops.append(-step)
    exchange(windows[-1], block)
    held = tie(jnp.stack(held), *[columns[k] for k in windows[-3]])
    other = lax.ppermute(held, "fsdp", swap_pairs(count))
    ways = [(h, far) for far in (False, True) for h in hops]
    return [held, other], ways, [columns[k] for k in range(count)]


def sum_rounds(count):
    rounds, bit = [("tp", [1])], 1
    while bit < count:
        rounds.append(("fsdp", [bit, 2 * bit, 3 * bit] if 2 * bit < count else [bit]))
        bit *= 4
    return rounds


def sum_round(x, axis, distances):
    size = lax.axis_size(axis)
    terms = [x]
    for d in distances:
        terms.append(lax.ppermute(x, axis, [(n, n ^ d) for n in range(size)]))
    if len(terms) == 2:
        return terms[0] + terms[1]
    return (terms[0] + terms[1]) + (terms[2] + terms[3])


def local(momentum, gradient, basis):
    rows, cols = momentum.shape
    rank = basis.shape[1]
    count = lax.axis_size("fsdp")
    tp_count = lax.axis_size("tp")
    chips = count // 2
    share = -(-cols // (count * LANES)) * LANES
    factor = math.sqrt(rows * count * cols * tp_count / rank)
    ring = tp_count == 2 and count in (16, 32) and (count - 1) * share < cols

    base = momentum + gradient.astype(F32)
    base_b = base.astype(BF16)
    sketch = jnp.dot(base_b, basis, preferred_element_type=F32)
    base = pltpu.with_memory_space_constraint(base, pltpu.VMEM)
    if ring:
        outgoing = pack_call(base, share, count)
        pieces, ways, columns = gather_and_exchange(sketch, outgoing, count)
        ways = [functools.partial(ring_owner, count, *way) for way in ways]
        owner = lambda me, n: ways[n](me, 1 - 2 * lax.axis_index("tp"))
    else:
        padded = jnp.pad(base_b, ((0, 0), (0, share * count - cols)))
        columns = jnp.swapaxes(padded.reshape(rows, count, share), 0, 1)
        columns = lax.all_to_all(columns, "fsdp", 0, 0, tiled=True)
        columns = [columns.reshape(count * rows, share)]
        pieces = [lax.all_gather(lax.psum(sketch, "tp"), "fsdp", axis=0)]
        owner = lambda me, n: n
    ortho_t, ortho_here = factor_call(owner, base, pieces)
    part, back = back_call(base, ortho_t, columns)
    write = functools.partial(output_call, base=base, ortho=ortho_here, factor=factor)
    if not ring:
        whole = lax.all_gather(back, "fsdp", axis=0)
        blocks = [whole[n] for n in range(-(-cols // share))]
        colsq = lax.psum(part, ("fsdp", "tp"))
        return tuple(write(lambda me, n: n, blocks, colsq, None))

    turns, swap = ring_steps(count), swap_pairs(count)
    colsq, result = part, None
    for axis, distances in sum_rounds(count):
        colsq = sum_round(colsq, axis, distances)
    arrived, blocks, owners, written = {0: back}, [], [], 0
    waiting = ()
    for n in range(chips):
        block = tie(arrived[n], *waiting)
        for later in (1, 2) if n == 0 else (n + 2,):
            if later < chips:
                arrived[later] = lax.ppermute(block, "fsdp", turns[(later + 1) % 2])
        blocks += [block, lax.ppermute(block, "fsdp", swap)]
        hops = (n + 1) // 2 if n % 2 else -(n // 2)
        owners += [functools.partial(ring_owner, count, hops, far) for far in (False, True)]
        if n == 0:
            waiting = (arrived[2], colsq)
            continue
        if n == 2:
            waiting = ()
            continue
        upto = 2 * n + (2 if n == 1 else 1 if n + 1 == chips else 0)
        upto = min(upto, written + 4) if n + 1 < chips else upto
        result = write(owner_of(owners[written:upto]), blocks[written:upto], colsq, result)
        written, waiting = upto, tuple(result)
    return tuple(write(owner_of(owners[written:]), blocks[written:], colsq, result))


def solution(mesh):
    return jax.shard_map(
        local,
        mesh=mesh,
        in_specs=(P("fsdp", "tp"), P("fsdp", "tp"), P("tp", None)),
        out_specs=(P("fsdp", "tp"), P("tp", None), P("fsdp", "tp")),
        check_vma=False,
    )
```

```python
import functools
import math

import jax
import jax.numpy as jnp
from jax import lax
from jax.experimental import pallas as pl
from jax.experimental.pallas import tpu as pltpu
from jax.sharding import PartitionSpec as P

LANES = 128
SUBLANES = 8
PANEL = 64
MIB = 1024 * 1024
FULL = lax.Precision.HIGHEST
F32 = jnp.float32
BF16 = jnp.bfloat16


def cost(flops, nbytes):
    return pl.CostEstimate(flops=flops, bytes_accessed=nbytes, transcendentals=0)


def params(mib):
    return pltpu.CompilerParams(vmem_limit_bytes=mib * MIB)


def by_width(block, cols, share, start, stop, act):
    last = (cols - 1) // share
    width, short = stop - start, max(0, min(cols - last * share, stop) - start)
    if short == width:
        act(width)
        return

    @pl.when(block < last)
    def _():
        act(width)

    if short:

        @pl.when(block == last)
        def _():
            act(short)


def pack_kernel(base_ref, *out_refs):
    cols = base_ref.shape[1]
    share = out_refs[0].shape[1]
    me = lax.axis_index("fsdp")
    for n, out_ref in enumerate(out_refs):
        owner = me ^ n

        def fill(width):
            start = pl.multiple_of(owner * share, LANES)
            out_ref[:, :width] = base_ref[:, pl.ds(start, width)].astype(BF16)
            if width < share:
                out_ref[:, width:] = jnp.zeros((out_ref.shape[0], share - width), BF16)

        by_width(owner, cols, share, 0, share, fill)


def pack_call(base, share, count):
    rows = base.shape[0]
    vmem = pl.BlockSpec(memory_space=pltpu.VMEM)
    return pl.pallas_call(
        pack_kernel,
        in_specs=[vmem],
        out_specs=[vmem] * count,
        out_shape=[jax.ShapeDtypeStruct((rows, share), BF16)] * count,
        compiler_params=params(16),
        cost_estimate=cost(0, 6 * rows * share * count),
        name="pack",
    )(base)


def spread(x, lane):
    return jnp.broadcast_to(x[:, lane : lane + 1], (x.shape[0], LANES))


def row_of(x, row):
    return jnp.broadcast_to(x[row : row + 1, :], (SUBLANES, LANES))


def eliminate(block):
    sub = lax.broadcasted_iota(jnp.int32, (SUBLANES, LANES), 0)
    groups = PANEL // SUBLANES
    top = [block[SUBLANES * g : SUBLANES * (g + 1)] for g in range(groups)]
    for g in range(groups):
        first = PANEL + SUBLANES * g
        t = top[g]
        cols = [spread(t, first + j) for j in range(SUBLANES)]
        below = [[spread(top[i], first + j) for j in range(SUBLANES)] for i in range(g + 1, groups)]
        pivots = jnp.zeros((SUBLANES, LANES), F32)
        inverse, corner = [], {}
        for j in range(SUBLANES):
            pivot = row_of(cols[j], j)
            pivots = jnp.where(sub == j, pivot, pivots)
            inverse.append(1.0 / pivot)
            factor = jnp.where(sub > j, cols[j] * inverse[j], 0.0)
            t = t - factor * row_of(t, j)
            for k in range(j + 1, SUBLANES):
                corner[j, k] = row_of(cols[k], j)
                cols[k] = cols[k] - factor * corner[j, k]
        lines = [row_of(t, j) for j in range(SUBLANES)]
        for i in range(g + 1, groups):
            entries = below[i - g - 1]
            acc = top[i]
            for j in range(SUBLANES):
                factor = entries[j] * inverse[j]
                acc = acc - factor * lines[j]
                for k in range(j + 1, SUBLANES):
                    entries[k] = entries[k] - factor * corner[j, k]
            top[i] = acc
        top[g] = t * lax.rsqrt(pivots)
    return jnp.concatenate(top, axis=0)[:, :PANEL]


def dot(a, b, dims):
    return lax.dot_general(a, b, (dims, ((), ())), precision=FULL, preferred_element_type=F32)


def factor_kernel(stacks, owner, base_ref, *refs):
    me = lax.axis_index("fsdp")
    stacked, (ortho_t_ref, here_ref, whole_ref, work_ref, corner_ref) = refs[:stacks], refs[stacks:]
    corner_ref[...] = base_ref[:SUBLANES, :LANES]
    rows, rank = here_ref.shape
    total = whole_ref.shape[0]
    pieces = [stack.at[n] for stack in stacked for n in range(stack.shape[0])]
    for n, piece in enumerate(pieces):
        start = pl.multiple_of(owner(me, n) * rows, SUBLANES)
        whole_ref[pl.ds(start, rows), :] = piece[...]

    work_ref[:, :rank] = jnp.zeros((rank, rank), F32)
    chunk = 4 * rows

    @pl.loop(0, total // chunk)
    def _(n):
        part = whole_ref[pl.ds(pl.multiple_of(n * chunk, SUBLANES), chunk), :]
        work_ref[:, :rank] += dot(part, part, ((0,), (0,)))

    line = lax.broadcasted_iota(jnp.int32, (rank, rank), 0)
    column = lax.broadcasted_iota(jnp.int32, (rank, rank), 1)
    work_ref[:, rank:] = jnp.where(line == column, 1.0, 0.0).astype(F32)
    eye = jnp.where(line == column, 1.0, 0.0).astype(F32)[:PANEL, :PANEL]
    for start in range(0, rank, PANEL):
        stop = start + PANEL
        diagonal = work_ref[start:stop, start:stop]
        small = eliminate(jnp.concatenate([eye, diagonal], axis=1))
        panel = dot(small, work_ref[start:stop, :], ((1,), (0,)))
        work_ref[start:stop, :] = panel
        if stop < rank:
            work_ref[stop:, :] -= dot(panel[:, stop:rank], panel, ((0,), (0,)))
    inverse = work_ref[:, rank:]
    start = pl.multiple_of(me * rows, SUBLANES)
    here_ref[...] = dot(whole_ref[pl.ds(start, rows), :], inverse, ((1,), (1,))).astype(BF16)
    for n in range(0, total, chunk):
        ortho_t_ref[:, n : n + chunk] = dot(
            inverse, whole_ref[n : n + chunk, :], ((1,), (1,))
        ).astype(BF16)


def factor_call(owner, base, stacked):
    _, rows, rank = stacked[0].shape
    total = rows * sum(stack.shape[0] for stack in stacked)
    vmem = pl.BlockSpec(memory_space=pltpu.VMEM)
    return pl.pallas_call(
        functools.partial(factor_kernel, len(stacked), owner),
        in_specs=[vmem] * (1 + len(stacked)),
        out_specs=[vmem, vmem],
        out_shape=[
            jax.ShapeDtypeStruct((rank, total), BF16),
            jax.ShapeDtypeStruct((rows, rank), BF16),
        ],
        scratch_shapes=[
            pltpu.VMEM((total, rank), F32),
            pltpu.VMEM((rank, 2 * rank), F32),
            pltpu.VMEM((SUBLANES, LANES), F32),
        ],
        compiler_params=params(24),
        cost_estimate=cost(40 * total * rank * rank, total * rank * 6),
        name="factor",
    )(base, *stacked)


def back_kernel(base_ref, ortho_t_ref, *refs):
    *columns, colsq_ref, back_ref, whole_ref, corner_ref = refs
    corner_ref[...] = base_ref[:SUBLANES, :LANES]
    me = lax.axis_index("fsdp") if len(columns) > 1 else 0
    rows = columns[0].shape[0]
    for n, piece in enumerate(columns):
        whole_ref[pl.ds(pl.multiple_of((me ^ n) * rows, 16), rows), :] = piece[...]
    back_t = jnp.dot(ortho_t_ref[...], whole_ref[...], preferred_element_type=F32)
    back = back_t.T.astype(BF16)
    back_ref[...] = back
    wide = back.astype(F32)
    colsq_ref[...] = jnp.sum(wide * wide, axis=0, keepdims=True)


def back_call(base, ortho_t, columns):
    rank, total = ortho_t.shape
    share = columns[0].shape[1]
    vmem = pl.BlockSpec(memory_space=pltpu.VMEM)
    return pl.pallas_call(
        back_kernel,
        in_specs=[vmem] * (2 + len(columns)),
        out_specs=[vmem] * 2,
        out_shape=[
            jax.ShapeDtypeStruct((1, rank), F32),
            jax.ShapeDtypeStruct((share, rank), BF16),
        ],
        scratch_shapes=[pltpu.VMEM((total, share), BF16), pltpu.VMEM((SUBLANES, LANES), F32)],
        compiler_params=params(24),
        cost_estimate=cost(2 * rank * total * share, total * share * 2),
        name="back",
    )(base, ortho_t, *columns)


def output_kernel(owner, factor, base_ref, ortho_ref, colsq_ref, *refs):
    me = lax.axis_index("fsdp")
    *pieces, nm_ref, nb_ref, up_ref, nm_tile, nb_tile, up_tile, sems = refs
    count, share, cols = nm_tile.shape[0], nm_tile.shape[2], nm_ref.shape[1]
    scale = lax.rsqrt(colsq_ref[...] + 1e-06)
    ortho = ortho_ref[...]
    over = (((1,), (1,)), ((), ()))

    def copies(n, width):
        there = pl.ds(pl.multiple_of(owner(me, n) * share, LANES), width)
        sides = (
            (nm_tile.at[n, :, :width], nm_ref.at[:, there]),
            (nb_tile.at[n, :width, :], nb_ref.at[there, :]),
            (up_tile.at[n, :, :width], up_ref.at[:, there]),
        )
        return [
            pltpu.make_async_copy(source, target, sems.at[n, which])
            for which, (source, target) in enumerate(sides)
        ]

    for n in range(count):

        def compute(width):
            there = pl.ds(pl.multiple_of(owner(me, n) * share, LANES), width)
            back = pieces[n][:width, :]
            unit = (back.astype(F32) * scale).astype(BF16)
            nb_tile[n, :width, :] = unit
            nm_tile[n, :, :width] = base_ref[:, there] - 0.05 * lax.dot_general(
                ortho, back, over, preferred_element_type=F32
            )
            up_tile[n, :, :width] = (
                factor * lax.dot_general(ortho, unit, over, preferred_element_type=F32)
            ).astype(BF16)
            for copy in copies(n, width):
                copy.start()

        by_width(owner(me, n), cols, share, 0, share, compute)

    for n in range(count):

        def wait(width):
            for copy in copies(n, width):
                copy.wait()

        by_width(owner(me, n), cols, share, 0, share, wait)


def output_call(owner, blocks, colsq, previous, base, ortho, factor):
    rows, cols = base.shape
    share, rank = blocks[0].shape
    count = len(blocks)
    previous = previous or ()
    vmem, hbm = pl.BlockSpec(memory_space=pltpu.VMEM), pl.BlockSpec(memory_space=pltpu.HBM)
    return pl.pallas_call(
        functools.partial(output_kernel, owner, factor),
        in_specs=[vmem] * (3 + count) + [hbm] * len(previous),
        out_specs=[hbm] * 3,
        out_shape=[
            jax.ShapeDtypeStruct((rows, cols), F32),
            jax.ShapeDtypeStruct((cols, rank), BF16),
            jax.ShapeDtypeStruct((rows, cols), BF16),
        ],
        scratch_shapes=[
            pltpu.VMEM((count, rows, share), F32),
            pltpu.VMEM((count, share, rank), BF16),
            pltpu.VMEM((count, rows, share), BF16),
            pltpu.SemaphoreType.DMA((count, 3)),
        ],
        input_output_aliases={3 + count + n: n for n in range(len(previous))},
        compiler_params=params(16),
        cost_estimate=cost(
            4 * rows * share * rank * count, count * share * (rows * 10 + rank * 4)
        ),
        name="outputs",
    )(base, ortho, colsq, *blocks, *previous)


def ring_order(chips):
    half = chips // 2
    return [2 * q for q in range(half)] + [2 * (chips - 1 - q) + 1 for q in range(half, chips)]


def ring_steps(count):
    order = ring_order(count // 2)
    after = dict(zip(order, order[1:] + order[:1]))
    up = [(2 * c + k, 2 * after[c] + k) for c in order for k in (0, 1)]
    down = [(b, a) for a, b in up]
    first = [p for p in up if p[0] % 2 == 0] + [p for p in down if p[0] % 2 == 1]
    second = [p for p in down if p[0] % 2 == 0] + [p for p in up if p[0] % 2 == 1]
    return first, second


def ring_owner(count, hops, other, me, sign=1):
    chips = count // 2
    half = chips // 2
    core, chip = me & 1, me >> 1
    place = jnp.where((chip & 1) == 0, chip >> 1, chips - 1 - (chip >> 1))
    forward = hops * sign * (2 * core - 1)
    place = lax.rem(place + chips + (-forward if other else forward), chips)
    chip = jnp.where(place < half, 2 * place, 2 * (chips - 1 - place) + 1)
    return 2 * chip + (1 - core if other else core)


def owner_of(ways):
    return lambda me, n: ways[n](me)


def swap_pairs(count):
    return [(n, n ^ 1) for n in range(count)]


def tie(x, *work):
    return lax.optimization_barrier((x, *work))[0] if work else x


def exchange_windows(count):
    chips, steps = count // 2, count // 4
    far, near = list(range(chips, count)), list(range(1, chips))
    each = -(-len(near) // steps)
    windows = [far[w + 1 : w + 2] + near[(w - 1) * each : w * each] for w in range(1, steps + 1)]
    return [far[:2]] + windows + [far[steps + 2 :]]


def gather_and_exchange(sketch, outgoing, count):
    chips = count // 2
    first, second = ring_steps(count)
    windows = exchange_windows(count)
    columns = {0: outgoing[0]}

    def exchange(window, *after):
        for k in window:
            pairs = [(n, n ^ k) for n in range(count)]
            columns[k] = lax.ppermute(tie(outgoing[k], *after), "fsdp", pairs)

    exchange(windows[0], sketch)
    across = [(0, 1), (1, 0)]
    sketch = sketch + lax.ppermute(sketch, "tp", across)
    turns = [(2 * a + half, 2 * b + half) for half in (0, 1) for a, b in (first, second)[half]]
    hops, held, block = [0], [sketch], sketch
    for step in range(1, chips // 2 + 1):
        work = [columns[k] for k in windows[step - 2]] if step > 1 else []
        block = tie(block, *work)
        exchange(windows[step], block)
        block = lax.ppermute(block, ("fsdp", "tp"), turns)
        held.append(block)
        hops.append(step)
        if 2 * step < chips:
            held.append(lax.ppermute(block, "tp", across))
            hops.append(-step)
    exchange(windows[-1], block)
    held = tie(jnp.stack(held), *[columns[k] for k in windows[-3]])
    other = lax.ppermute(held, "fsdp", swap_pairs(count))
    ways = [(h, far) for far in (False, True) for h in hops]
    return [held, other], ways, [columns[k] for k in range(count)]


def sum_rounds(count):
    rounds, bit = [], 1
    while bit < count:
        rounds.append(("fsdp", [bit, 2 * bit, 3 * bit] if 2 * bit < count else [bit]))
        bit *= 4
    return rounds[::-1]


def sum_round(x, axis, distances):
    size = lax.axis_size(axis)
    terms = [x]
    for d in distances:
        terms.append(lax.ppermute(x, axis, [(n, n ^ d) for n in range(size)]))
    if len(terms) == 2:
        return terms[0] + terms[1]
    return (terms[0] + terms[1]) + (terms[2] + terms[3])


def local(momentum, gradient, basis):
    rows, cols = momentum.shape
    rank = basis.shape[1]
    count = lax.axis_size("fsdp")
    tp_count = lax.axis_size("tp")
    chips = count // 2
    share = -(-cols // (count * LANES)) * LANES
    factor = math.sqrt(rows * count * cols * tp_count / rank)
    ring = tp_count == 2 and count in (16, 32) and (count - 1) * share < cols

    base = momentum + gradient.astype(F32)
    base_b = base.astype(BF16)
    sketch = jnp.dot(base_b, basis, preferred_element_type=F32)
    base = pltpu.with_memory_space_constraint(base, pltpu.VMEM)
    if ring:
        outgoing = pack_call(base, share, count)
        pieces, ways, columns = gather_and_exchange(sketch, outgoing, count)
        ways = [functools.partial(ring_owner, count, *way) for way in ways]
        owner = lambda me, n: ways[n](me, 1 - 2 * lax.axis_index("tp"))
    else:
        padded = jnp.pad(base_b, ((0, 0), (0, share * count - cols)))
        columns = jnp.swapaxes(padded.reshape(rows, count, share), 0, 1)
        columns = lax.all_to_all(columns, "fsdp", 0, 0, tiled=True)
        columns = [columns.reshape(count * rows, share)]
        pieces = [lax.all_gather(lax.psum(sketch, "tp"), "fsdp", axis=0)]
        owner = lambda me, n: n
    ortho_t, ortho_here = factor_call(owner, base, pieces)
    part, back = back_call(base, ortho_t, columns)
    write = functools.partial(output_call, base=base, ortho=ortho_here, factor=factor)
    if not ring:
        whole = lax.all_gather(back, "fsdp", axis=0)
        blocks = [whole[n] for n in range(-(-cols // share))]
        colsq = lax.psum(part, ("fsdp", "tp"))
        return tuple(write(lambda me, n: n, blocks, colsq, None))

    turns, swap = ring_steps(count), swap_pairs(count)
    colsq, result = part, None
    for axis, distances in sum_rounds(count):
        colsq = sum_round(colsq, axis, distances)
    arrived, blocks, owners, written = {0: back}, [], [], 0
    waiting = ()
    for n in range(chips):
        block = tie(arrived[n], *waiting)
        for later in (1, 2) if n == 0 else (n + 2,):
            if later < chips:
                arrived[later] = lax.ppermute(block, "fsdp", turns[(later + 1) % 2])
        blocks += [block, lax.ppermute(block, "fsdp", swap)]
        hops = (n + 1) // 2 if n % 2 else -(n // 2)
        owners += [functools.partial(ring_owner, count, hops, far) for far in (False, True)]
        if n == 0:
            waiting = (arrived[2], colsq)
            continue
        if n == 1:
            colsq = sum_round(tie(colsq, blocks[-1]), "tp", [1])
        if n == 2:
            waiting = ()
            continue
        upto = {1: 4, 3: 6, chips - 1: 2 * n + 1}.get(n, 2 * n)
        result = write(owner_of(owners[written:upto]), blocks[written:upto], colsq, result)
        written, waiting = upto, tuple(result)
    return tuple(write(owner_of(owners[written:]), blocks[written:], colsq, result))


def solution(mesh):
    return jax.shard_map(
        local,
        mesh=mesh,
        in_specs=(P("fsdp", "tp"), P("fsdp", "tp"), P("tp", None)),
        out_specs=(P("fsdp", "tp"), P("tp", None), P("fsdp", "tp")),
        check_vma=False,
    )
```

```python
import functools
import math

import jax
import jax.numpy as jnp
from jax import lax
from jax.experimental import pallas as pl
from jax.experimental.pallas import tpu as pltpu
from jax.sharding import PartitionSpec as P

LANES = 128
SUBLANES = 8
PANEL = 64
MIB = 1024 * 1024
FULL = lax.Precision.HIGHEST
F32 = jnp.float32
BF16 = jnp.bfloat16


def cost(flops, nbytes):
    return pl.CostEstimate(flops=flops, bytes_accessed=nbytes, transcendentals=0)


def params(mib):
    return pltpu.CompilerParams(vmem_limit_bytes=mib * MIB)


def by_width(block, cols, share, start, stop, act):
    last = (cols - 1) // share
    width, short = stop - start, max(0, min(cols - last * share, stop) - start)
    if short == width:
        act(width)
        return

    @pl.when(block < last)
    def _():
        act(width)

    if short:

        @pl.when(block == last)
        def _():
            act(short)


def pack_kernel(base_ref, *out_refs):
    cols = base_ref.shape[1]
    share = out_refs[0].shape[1]
    me = lax.axis_index("fsdp")
    for n, out_ref in enumerate(out_refs):
        owner = me ^ n

        def fill(width):
            start = pl.multiple_of(owner * share, LANES)
            out_ref[:, :width] = base_ref[:, pl.ds(start, width)].astype(BF16)
            if width < share:
                out_ref[:, width:] = jnp.zeros((out_ref.shape[0], share - width), BF16)

        by_width(owner, cols, share, 0, share, fill)


def pack_call(base, share, count):
    rows = base.shape[0]
    vmem = pl.BlockSpec(memory_space=pltpu.VMEM)
    return pl.pallas_call(
        pack_kernel,
        in_specs=[vmem],
        out_specs=[vmem] * count,
        out_shape=[jax.ShapeDtypeStruct((rows, share), BF16)] * count,
        compiler_params=params(16),
        cost_estimate=cost(0, 6 * rows * share * count),
        name="pack",
    )(base)


def spread(x, lane):
    return jnp.broadcast_to(x[:, lane : lane + 1], (x.shape[0], LANES))


def row_of(x, row):
    return jnp.broadcast_to(x[row : row + 1, :], (SUBLANES, LANES))


def eliminate(block):
    sub = lax.broadcasted_iota(jnp.int32, (SUBLANES, LANES), 0)
    groups = PANEL // SUBLANES
    top = [block[SUBLANES * g : SUBLANES * (g + 1)] for g in range(groups)]
    for g in range(groups):
        first = PANEL + SUBLANES * g
        t = top[g]
        cols = [spread(t, first + j) for j in range(SUBLANES)]
        below = [[spread(top[i], first + j) for j in range(SUBLANES)] for i in range(g + 1, groups)]
        pivots = jnp.zeros((SUBLANES, LANES), F32)
        inverse, corner = [], {}
        for j in range(SUBLANES):
            pivot = row_of(cols[j], j)
            pivots = jnp.where(sub == j, pivot, pivots)
            inverse.append(1.0 / pivot)
            factor = jnp.where(sub > j, cols[j] * inverse[j], 0.0)
            t = t - factor * row_of(t, j)
            for k in range(j + 1, SUBLANES):
                corner[j, k] = row_of(cols[k], j)
                cols[k] = cols[k] - factor * corner[j, k]
        lines = [row_of(t, j) for j in range(SUBLANES)]
        for i in range(g + 1, groups):
            entries = below[i - g - 1]
            acc = top[i]
            for j in range(SUBLANES):
                factor = entries[j] * inverse[j]
                acc = acc - factor * lines[j]
                for k in range(j + 1, SUBLANES):
                    entries[k] = entries[k] - factor * corner[j, k]
            top[i] = acc
        top[g] = t * lax.rsqrt(pivots)
    return jnp.concatenate(top, axis=0)[:, :PANEL]


def dot(a, b, dims):
    return lax.dot_general(a, b, (dims, ((), ())), precision=FULL, preferred_element_type=F32)


def factor_kernel(stacks, owner, base_ref, *refs):
    me = lax.axis_index("fsdp")
    stacked, (ortho_t_ref, here_ref, whole_ref, work_ref, corner_ref) = refs[:stacks], refs[stacks:]
    corner_ref[...] = base_ref[:SUBLANES, :LANES]
    rows, rank = here_ref.shape
    total = whole_ref.shape[0]
    pieces = [stack.at[n] for stack in stacked for n in range(stack.shape[0])]
    for n, piece in enumerate(pieces):
        start = pl.multiple_of(owner(me, n) * rows, SUBLANES)
        whole_ref[pl.ds(start, rows), :] = piece[...]

    work_ref[:, :rank] = jnp.zeros((rank, rank), F32)
    chunk = 4 * rows

    @pl.loop(0, total // chunk)
    def _(n):
        part = whole_ref[pl.ds(pl.multiple_of(n * chunk, SUBLANES), chunk), :]
        work_ref[:, :rank] += dot(part, part, ((0,), (0,)))

    line = lax.broadcasted_iota(jnp.int32, (rank, rank), 0)
    column = lax.broadcasted_iota(jnp.int32, (rank, rank), 1)
    work_ref[:, rank:] = jnp.where(line == column, 1.0, 0.0).astype(F32)
    eye = jnp.where(line == column, 1.0, 0.0).astype(F32)[:PANEL, :PANEL]
    for start in range(0, rank, PANEL):
        stop = start + PANEL
        diagonal = work_ref[start:stop, start:stop]
        small = eliminate(jnp.concatenate([eye, diagonal], axis=1))
        panel = dot(small, work_ref[start:stop, :], ((1,), (0,)))
        work_ref[start:stop, :] = panel
        if stop < rank:
            work_ref[stop:, :] -= dot(panel[:, stop:rank], panel, ((0,), (0,)))
    inverse = work_ref[:, rank:]
    start = pl.multiple_of(me * rows, SUBLANES)
    here_ref[...] = dot(whole_ref[pl.ds(start, rows), :], inverse, ((1,), (1,))).astype(BF16)
    for n in range(0, total, chunk):
        ortho_t_ref[:, n : n + chunk] = dot(
            inverse, whole_ref[n : n + chunk, :], ((1,), (1,))
        ).astype(BF16)


def factor_call(owner, base, stacked):
    _, rows, rank = stacked[0].shape
    total = rows * sum(stack.shape[0] for stack in stacked)
    vmem = pl.BlockSpec(memory_space=pltpu.VMEM)
    return pl.pallas_call(
        functools.partial(factor_kernel, len(stacked), owner),
        in_specs=[vmem] * (1 + len(stacked)),
        out_specs=[vmem, vmem],
        out_shape=[
            jax.ShapeDtypeStruct((rank, total), BF16),
            jax.ShapeDtypeStruct((rows, rank), BF16),
        ],
        scratch_shapes=[
            pltpu.VMEM((total, rank), F32),
            pltpu.VMEM((rank, 2 * rank), F32),
            pltpu.VMEM((SUBLANES, LANES), F32),
        ],
        compiler_params=params(24),
        cost_estimate=cost(40 * total * rank * rank, total * rank * 6),
        name="factor",
    )(base, *stacked)


def back_kernel(base_ref, ortho_t_ref, *refs):
    *columns, colsq_ref, back_ref, whole_ref, corner_ref = refs
    corner_ref[...] = base_ref[:SUBLANES, :LANES]
    me = lax.axis_index("fsdp") if len(columns) > 1 else 0
    rows = columns[0].shape[0]
    for n, piece in enumerate(columns):
        whole_ref[pl.ds(pl.multiple_of((me ^ n) * rows, 16), rows), :] = piece[...]
    back_t = jnp.dot(ortho_t_ref[...], whole_ref[...], preferred_element_type=F32)
    back = back_t.T.astype(BF16)
    back_ref[...] = back
    wide = back.astype(F32)
    colsq_ref[...] = jnp.sum(wide * wide, axis=0, keepdims=True)


def back_call(base, ortho_t, columns):
    rank, total = ortho_t.shape
    share = columns[0].shape[1]
    vmem = pl.BlockSpec(memory_space=pltpu.VMEM)
    return pl.pallas_call(
        back_kernel,
        in_specs=[vmem] * (2 + len(columns)),
        out_specs=[vmem] * 2,
        out_shape=[
            jax.ShapeDtypeStruct((1, rank), F32),
            jax.ShapeDtypeStruct((share, rank), BF16),
        ],
        scratch_shapes=[pltpu.VMEM((total, share), BF16), pltpu.VMEM((SUBLANES, LANES), F32)],
        compiler_params=params(24),
        cost_estimate=cost(2 * rank * total * share, total * share * 2),
        name="back",
    )(base, ortho_t, *columns)


def output_kernel(owner, factor, base_ref, ortho_ref, colsq_ref, *refs):
    me = lax.axis_index("fsdp")
    *pieces, nm_ref, nb_ref, up_ref, nm_tile, nb_tile, up_tile, sems = refs
    count, share, cols = nm_tile.shape[0], nm_tile.shape[2], nm_ref.shape[1]
    scale = lax.rsqrt(colsq_ref[...] + 1e-06)
    ortho = ortho_ref[...]
    over = (((1,), (1,)), ((), ()))

    def copies(n, width):
        there = pl.ds(pl.multiple_of(owner(me, n) * share, LANES), width)
        sides = (
            (nm_tile.at[n, :, :width], nm_ref.at[:, there]),
            (nb_tile.at[n, :width, :], nb_ref.at[there, :]),
            (up_tile.at[n, :, :width], up_ref.at[:, there]),
        )
        return [
            pltpu.make_async_copy(source, target, sems.at[n, which])
            for which, (source, target) in enumerate(sides)
        ]

    for n in range(count):

        def compute(width):
            there = pl.ds(pl.multiple_of(owner(me, n) * share, LANES), width)
            back = pieces[n][:width, :]
            unit = (back.astype(F32) * scale).astype(BF16)
            nb_tile[n, :width, :] = unit
            nm_tile[n, :, :width] = base_ref[:, there] - 0.05 * lax.dot_general(
                ortho, back, over, preferred_element_type=F32
            )
            up_tile[n, :, :width] = (
                factor * lax.dot_general(ortho, unit, over, preferred_element_type=F32)
            ).astype(BF16)
            for copy in copies(n, width):
                copy.start()

        by_width(owner(me, n), cols, share, 0, share, compute)

    for n in range(count):

        def wait(width):
            for copy in copies(n, width):
                copy.wait()

        by_width(owner(me, n), cols, share, 0, share, wait)


def output_call(owner, blocks, colsq, previous, base, ortho, factor):
    rows, cols = base.shape
    share, rank = blocks[0].shape
    count = len(blocks)
    previous = previous or ()
    vmem, hbm = pl.BlockSpec(memory_space=pltpu.VMEM), pl.BlockSpec(memory_space=pltpu.HBM)
    return pl.pallas_call(
        functools.partial(output_kernel, owner, factor),
        in_specs=[vmem] * (3 + count) + [hbm] * len(previous),
        out_specs=[hbm] * 3,
        out_shape=[
            jax.ShapeDtypeStruct((rows, cols), F32),
            jax.ShapeDtypeStruct((cols, rank), BF16),
            jax.ShapeDtypeStruct((rows, cols), BF16),
        ],
        scratch_shapes=[
            pltpu.VMEM((count, rows, share), F32),
            pltpu.VMEM((count, share, rank), BF16),
            pltpu.VMEM((count, rows, share), BF16),
            pltpu.SemaphoreType.DMA((count, 3)),
        ],
        input_output_aliases={3 + count + n: n for n in range(len(previous))},
        compiler_params=params(16),
        cost_estimate=cost(
            4 * rows * share * rank * count, count * share * (rows * 10 + rank * 4)
        ),
        name="outputs",
    )(base, ortho, colsq, *blocks, *previous)


def ring_order(chips):
    half = chips // 2
    return [2 * q for q in range(half)] + [2 * (chips - 1 - q) + 1 for q in range(half, chips)]


def ring_steps(count):
    order = ring_order(count // 2)
    after = dict(zip(order, order[1:] + order[:1]))
    up = [(2 * c + k, 2 * after[c] + k) for c in order for k in (0, 1)]
    down = [(b, a) for a, b in up]
    first = [p for p in up if p[0] % 2 == 0] + [p for p in down if p[0] % 2 == 1]
    second = [p for p in down if p[0] % 2 == 0] + [p for p in up if p[0] % 2 == 1]
    return first, second


def ring_owner(count, hops, other, me, sign=1):
    chips = count // 2
    half = chips // 2
    core, chip = me & 1, me >> 1
    place = jnp.where((chip & 1) == 0, chip >> 1, chips - 1 - (chip >> 1))
    forward = hops * sign * (2 * core - 1)
    place = lax.rem(place + chips + (-forward if other else forward), chips)
    chip = jnp.where(place < half, 2 * place, 2 * (chips - 1 - place) + 1)
    return 2 * chip + (1 - core if other else core)


def owner_of(ways):
    return lambda me, n: ways[n](me)


def swap_pairs(count):
    return [(n, n ^ 1) for n in range(count)]


def tie(x, *work):
    return lax.optimization_barrier((x, *work))[0] if work else x


def exchange_windows(count):
    chips, steps = count // 2, count // 4
    far, near = list(range(chips, count)), list(range(1, chips))
    windows = [far[:2] + near[:1]]
    windows += [far[w + 1 : w + 2] + near[w : w + 1] for w in range(1, steps)]
    windows += [far[steps + 1 : steps + 2] + near[steps : steps + 2]]
    return windows + [far[steps + 2 :] + near[steps + 2 :]]


def gather_and_exchange(sketch, outgoing, count):
    chips = count // 2
    first, second = ring_steps(count)
    windows = exchange_windows(count)
    columns = {0: outgoing[0]}

    def exchange(window, *after):
        for k in window:
            pairs = [(n, n ^ k) for n in range(count)]
            columns[k] = lax.ppermute(tie(outgoing[k], *after), "fsdp", pairs)

    exchange(windows[0], sketch)
    across = [(0, 1), (1, 0)]
    sketch = sketch + lax.ppermute(sketch, "tp", across)
    turns = [(2 * a + half, 2 * b + half) for half in (0, 1) for a, b in (first, second)[half]]
    hops, held, block = [0], [sketch], sketch
    for step in range(1, chips // 2 + 1):
        work = [columns[k] for k in windows[step - 2]] if step > 1 else []
        block = tie(block, *work)
        exchange(windows[step], block)
        block = lax.ppermute(block, ("fsdp", "tp"), turns)
        held.append(block)
        hops.append(step)
        if 2 * step < chips:
            held.append(lax.ppermute(block, "tp", across))
            hops.append(-step)
    exchange(windows[-1], block)
    held = tie(jnp.stack(held), *[columns[k] for k in windows[-3]])
    other = lax.ppermute(held, "fsdp", swap_pairs(count))
    ways = [(h, far) for far in (False, True) for h in hops]
    return [held, other], ways, [columns[k] for k in range(count)]


def sum_rounds(count):
    rounds, bit = [("tp", [1])], 1
    while bit < count:
        rounds.append(("fsdp", [bit, 2 * bit, 3 * bit] if 2 * bit < count else [bit]))
        bit *= 4
    return rounds


def sum_round(x, axis, distances):
    size = lax.axis_size(axis)
    terms = [x]
    for d in distances:
        terms.append(lax.ppermute(x, axis, [(n, n ^ d) for n in range(size)]))
    if len(terms) == 2:
        return terms[0] + terms[1]
    return (terms[0] + terms[1]) + (terms[2] + terms[3])


def local(momentum, gradient, basis):
    rows, cols = momentum.shape
    rank = basis.shape[1]
    count = lax.axis_size("fsdp")
    tp_count = lax.axis_size("tp")
    chips = count // 2
    share = -(-cols // (count * LANES)) * LANES
    factor = math.sqrt(rows * count * cols * tp_count / rank)
    ring = tp_count == 2 and count in (16, 32) and (count - 1) * share < cols

    base = momentum + gradient.astype(F32)
    base_b = base.astype(BF16)
    sketch = jnp.dot(base_b, basis, preferred_element_type=F32)
    base = pltpu.with_memory_space_constraint(base, pltpu.VMEM)
    if ring:
        outgoing = pack_call(base, share, count)
        pieces, ways, columns = gather_and_exchange(sketch, outgoing, count)
        ways = [functools.partial(ring_owner, count, *way) for way in ways]
        owner = lambda me, n: ways[n](me, 1 - 2 * lax.axis_index("tp"))
    else:
        padded = jnp.pad(base_b, ((0, 0), (0, share * count - cols)))
        columns = jnp.swapaxes(padded.reshape(rows, count, share), 0, 1)
        columns = lax.all_to_all(columns, "fsdp", 0, 0, tiled=True)
        columns = [columns.reshape(count * rows, share)]
        pieces = [lax.all_gather(lax.psum(sketch, "tp"), "fsdp", axis=0)]
        owner = lambda me, n: n
    ortho_t, ortho_here = factor_call(owner, base, pieces)
    part, back = back_call(base, ortho_t, columns)
    write = functools.partial(output_call, base=base, ortho=ortho_here, factor=factor)
    if not ring:
        whole = lax.all_gather(back, "fsdp", axis=0)
        blocks = [whole[n] for n in range(-(-cols // share))]
        colsq = lax.psum(part, ("fsdp", "tp"))
        return tuple(write(lambda me, n: n, blocks, colsq, None))

    turns, swap = ring_steps(count), swap_pairs(count)
    colsq, result = part, None
    for axis, distances in sum_rounds(count):
        colsq = sum_round(colsq, axis, distances)
    arrived, blocks, owners, written = {0: back}, [], [], 0
    waiting = ()
    for n in range(chips):
        block = tie(arrived[n], *waiting)
        for later in (1, 2) if n == 0 else (n + 2,):
            if later < chips:
                arrived[later] = lax.ppermute(block, "fsdp", turns[(later + 1) % 2])
        blocks += [block, lax.ppermute(block, "fsdp", swap)]
        hops = (n + 1) // 2 if n % 2 else -(n // 2)
        owners += [functools.partial(ring_owner, count, hops, far) for far in (False, True)]
        if n == 0:
            waiting = (arrived[2], colsq)
            continue
        if n == 2:
            waiting = ()
            continue
        upto = 2 * n + (2 if n == 1 else 1 if n + 1 == chips else 0)
        upto = min(upto, written + 4) if n + 1 < chips else upto
        result = write(owner_of(owners[written:upto]), blocks[written:upto], colsq, result)
        written, waiting = upto, tuple(result)
    return tuple(write(owner_of(owners[written:]), blocks[written:], colsq, result))


def solution(mesh):
    return jax.shard_map(
        local,
        mesh=mesh,
        in_specs=(P("fsdp", "tp"), P("fsdp", "tp"), P("tp", None)),
        out_specs=(P("fsdp", "tp"), P("tp", None), P("fsdp", "tp")),
        check_vma=False,
    )
```

```python
import functools
import math

import jax
import jax.numpy as jnp
from jax import lax
from jax.experimental import pallas as pl
from jax.experimental.pallas import tpu as pltpu
from jax.sharding import PartitionSpec as P

LANES = 128
SUBLANES = 8
PANEL = 64
MIB = 1024 * 1024
FULL = lax.Precision.HIGHEST
F32 = jnp.float32
BF16 = jnp.bfloat16


def cost(flops, nbytes):
    return pl.CostEstimate(flops=flops, bytes_accessed=nbytes, transcendentals=0)


def params(mib):
    return pltpu.CompilerParams(vmem_limit_bytes=mib * MIB)


def by_width(block, cols, share, start, stop, act):
    last = (cols - 1) // share
    width, short = stop - start, max(0, min(cols - last * share, stop) - start)
    if short == width:
        act(width)
        return

    @pl.when(block < last)
    def _():
        act(width)

    if short:

        @pl.when(block == last)
        def _():
            act(short)


def pack_kernel(base_ref, *out_refs):
    cols = base_ref.shape[1]
    share = out_refs[0].shape[1]
    me = lax.axis_index("fsdp")
    for n, out_ref in enumerate(out_refs):
        owner = me ^ n

        def fill(width):
            start = pl.multiple_of(owner * share, LANES)
            out_ref[:, :width] = base_ref[:, pl.ds(start, width)].astype(BF16)
            if width < share:
                out_ref[:, width:] = jnp.zeros((out_ref.shape[0], share - width), BF16)

        by_width(owner, cols, share, 0, share, fill)


def pack_call(base, share, count):
    rows = base.shape[0]
    vmem = pl.BlockSpec(memory_space=pltpu.VMEM)
    return pl.pallas_call(
        pack_kernel,
        in_specs=[vmem],
        out_specs=[vmem] * count,
        out_shape=[jax.ShapeDtypeStruct((rows, share), BF16)] * count,
        compiler_params=params(16),
        cost_estimate=cost(0, 6 * rows * share * count),
        name="pack",
    )(base)


def spread(x, lane):
    return jnp.broadcast_to(x[:, lane : lane + 1], (x.shape[0], LANES))


def row_of(x, row):
    return jnp.broadcast_to(x[row : row + 1, :], (SUBLANES, LANES))


def eliminate(block):
    sub = lax.broadcasted_iota(jnp.int32, (SUBLANES, LANES), 0)
    groups = PANEL // SUBLANES
    top = [block[SUBLANES * g : SUBLANES * (g + 1)] for g in range(groups)]
    for g in range(groups):
        first = PANEL + SUBLANES * g
        t = top[g]
        cols = [spread(t, first + j) for j in range(SUBLANES)]
        below = [[spread(top[i], first + j) for j in range(SUBLANES)] for i in range(g + 1, groups)]
        pivots = jnp.zeros((SUBLANES, LANES), F32)
        inverse, corner = [], {}
        for j in range(SUBLANES):
            pivot = row_of(cols[j], j)
            pivots = jnp.where(sub == j, pivot, pivots)
            inverse.append(1.0 / pivot)
            factor = jnp.where(sub > j, cols[j] * inverse[j], 0.0)
            t = t - factor * row_of(t, j)
            for k in range(j + 1, SUBLANES):
                corner[j, k] = row_of(cols[k], j)
                cols[k] = cols[k] - factor * corner[j, k]
        lines = [row_of(t, j) for j in range(SUBLANES)]
        for i in range(g + 1, groups):
            entries = below[i - g - 1]
            acc = top[i]
            for j in range(SUBLANES):
                factor = entries[j] * inverse[j]
                acc = acc - factor * lines[j]
                for k in range(j + 1, SUBLANES):
                    entries[k] = entries[k] - factor * corner[j, k]
            top[i] = acc
        top[g] = t * lax.rsqrt(pivots)
    return jnp.concatenate(top, axis=0)[:, :PANEL]


def dot(a, b, dims):
    return lax.dot_general(a, b, (dims, ((), ())), precision=FULL, preferred_element_type=F32)


def factor_kernel(stacks, owner, base_ref, *refs):
    me = lax.axis_index("fsdp")
    stacked, (ortho_t_ref, here_ref, whole_ref, work_ref, corner_ref) = refs[:stacks], refs[stacks:]
    corner_ref[...] = base_ref[:SUBLANES, :LANES]
    rows, rank = here_ref.shape
    total = whole_ref.shape[0]
    pieces = [stack.at[n] for stack in stacked for n in range(stack.shape[0])]
    for n, piece in enumerate(pieces):
        start = pl.multiple_of(owner(me, n) * rows, SUBLANES)
        whole_ref[pl.ds(start, rows), :] = piece[...]

    work_ref[:, :rank] = jnp.zeros((rank, rank), F32)
    chunk = 4 * rows

    @pl.loop(0, total // chunk)
    def _(n):
        part = whole_ref[pl.ds(pl.multiple_of(n * chunk, SUBLANES), chunk), :]
        work_ref[:, :rank] += dot(part, part, ((0,), (0,)))

    line = lax.broadcasted_iota(jnp.int32, (rank, rank), 0)
    column = lax.broadcasted_iota(jnp.int32, (rank, rank), 1)
    work_ref[:, rank:] = jnp.where(line == column, 1.0, 0.0).astype(F32)
    eye = jnp.where(line == column, 1.0, 0.0).astype(F32)[:PANEL, :PANEL]
    for start in range(0, rank, PANEL):
        stop = start + PANEL
        diagonal = work_ref[start:stop, start:stop]
        small = eliminate(jnp.concatenate([eye, diagonal], axis=1))
        panel = dot(small, work_ref[start:stop, :], ((1,), (0,)))
        work_ref[start:stop, :] = panel
        if stop < rank:
            work_ref[stop:, :] -= dot(panel[:, stop:rank], panel, ((0,), (0,)))
    inverse = work_ref[:, rank:]
    start = pl.multiple_of(me * rows, SUBLANES)
    here_ref[...] = dot(whole_ref[pl.ds(start, rows), :], inverse, ((1,), (1,))).astype(BF16)
    for n in range(0, total, chunk):
        ortho_t_ref[:, n : n + chunk] = dot(
            inverse, whole_ref[n : n + chunk, :], ((1,), (1,))
        ).astype(BF16)


def factor_call(owner, base, stacked):
    _, rows, rank = stacked[0].shape
    total = rows * sum(stack.shape[0] for stack in stacked)
    vmem = pl.BlockSpec(memory_space=pltpu.VMEM)
    return pl.pallas_call(
        functools.partial(factor_kernel, len(stacked), owner),
        in_specs=[vmem] * (1 + len(stacked)),
        out_specs=[vmem, vmem],
        out_shape=[
            jax.ShapeDtypeStruct((rank, total), BF16),
            jax.ShapeDtypeStruct((rows, rank), BF16),
        ],
        scratch_shapes=[
            pltpu.VMEM((total, rank), F32),
            pltpu.VMEM((rank, 2 * rank), F32),
            pltpu.VMEM((SUBLANES, LANES), F32),
        ],
        compiler_params=params(24),
        cost_estimate=cost(40 * total * rank * rank, total * rank * 6),
        name="factor",
    )(base, *stacked)


def back_kernel(base_ref, ortho_t_ref, *refs):
    *columns, colsq_ref, back_ref, whole_ref, corner_ref = refs
    corner_ref[...] = base_ref[:SUBLANES, :LANES]
    me = lax.axis_index("fsdp") if len(columns) > 1 else 0
    rows = columns[0].shape[0]
    for n, piece in enumerate(columns):
        whole_ref[pl.ds(pl.multiple_of((me ^ n) * rows, 16), rows), :] = piece[...]
    back_t = jnp.dot(ortho_t_ref[...], whole_ref[...], preferred_element_type=F32)
    back = back_t.T.astype(BF16)
    back_ref[...] = back
    wide = back.astype(F32)
    colsq_ref[...] = jnp.sum(wide * wide, axis=0, keepdims=True)


def back_call(base, ortho_t, columns):
    rank, total = ortho_t.shape
    share = columns[0].shape[1]
    vmem = pl.BlockSpec(memory_space=pltpu.VMEM)
    return pl.pallas_call(
        back_kernel,
        in_specs=[vmem] * (2 + len(columns)),
        out_specs=[vmem] * 2,
        out_shape=[
            jax.ShapeDtypeStruct((1, rank), F32),
            jax.ShapeDtypeStruct((share, rank), BF16),
        ],
        scratch_shapes=[pltpu.VMEM((total, share), BF16), pltpu.VMEM((SUBLANES, LANES), F32)],
        compiler_params=params(24),
        cost_estimate=cost(2 * rank * total * share, total * share * 2),
        name="back",
    )(base, ortho_t, *columns)


def output_kernel(owner, factor, base_ref, ortho_ref, colsq_ref, *refs):
    me = lax.axis_index("fsdp")
    *pieces, nm_ref, nb_ref, up_ref, nm_tile, nb_tile, up_tile, sems = refs
    count, share, cols = nm_tile.shape[0], nm_tile.shape[2], nm_ref.shape[1]
    scale = lax.rsqrt(colsq_ref[...] + 1e-06)
    ortho = ortho_ref[...]
    over = (((1,), (1,)), ((), ()))

    def copies(n, width):
        there = pl.ds(pl.multiple_of(owner(me, n) * share, LANES), width)
        sides = (
            (nm_tile.at[n, :, :width], nm_ref.at[:, there]),
            (nb_tile.at[n, :width, :], nb_ref.at[there, :]),
            (up_tile.at[n, :, :width], up_ref.at[:, there]),
        )
        return [
            pltpu.make_async_copy(source, target, sems.at[n, which])
            for which, (source, target) in enumerate(sides)
        ]

    for n in range(count):

        def compute(width):
            there = pl.ds(pl.multiple_of(owner(me, n) * share, LANES), width)
            back = pieces[n][:width, :]
            unit = (back.astype(F32) * scale).astype(BF16)
            nb_tile[n, :width, :] = unit
            nm_tile[n, :, :width] = base_ref[:, there] - 0.05 * lax.dot_general(
                ortho, back, over, preferred_element_type=F32
            )
            up_tile[n, :, :width] = (
                factor * lax.dot_general(ortho, unit, over, preferred_element_type=F32)
            ).astype(BF16)
            for copy in copies(n, width):
                copy.start()

        by_width(owner(me, n), cols, share, 0, share, compute)

    for n in range(count):

        def wait(width):
            for copy in copies(n, width):
                copy.wait()

        by_width(owner(me, n), cols, share, 0, share, wait)


def output_call(owner, blocks, colsq, previous, base, ortho, factor):
    rows, cols = base.shape
    share, rank = blocks[0].shape
    count = len(blocks)
    previous = previous or ()
    vmem, hbm = pl.BlockSpec(memory_space=pltpu.VMEM), pl.BlockSpec(memory_space=pltpu.HBM)
    return pl.pallas_call(
        functools.partial(output_kernel, owner, factor),
        in_specs=[vmem] * (3 + count) + [hbm] * len(previous),
        out_specs=[hbm] * 3,
        out_shape=[
            jax.ShapeDtypeStruct((rows, cols), F32),
            jax.ShapeDtypeStruct((cols, rank), BF16),
            jax.ShapeDtypeStruct((rows, cols), BF16),
        ],
        scratch_shapes=[
            pltpu.VMEM((count, rows, share), F32),
            pltpu.VMEM((count, share, rank), BF16),
            pltpu.VMEM((count, rows, share), BF16),
            pltpu.SemaphoreType.DMA((count, 3)),
        ],
        input_output_aliases={3 + count + n: n for n in range(len(previous))},
        compiler_params=params(16),
        cost_estimate=cost(
            4 * rows * share * rank * count, count * share * (rows * 10 + rank * 4)
        ),
        name="outputs",
    )(base, ortho, colsq, *blocks, *previous)


def ring_order(chips):
    half = chips // 2
    return [2 * q for q in range(half)] + [2 * (chips - 1 - q) + 1 for q in range(half, chips)]


def ring_steps(count):
    order = ring_order(count // 2)
    after = dict(zip(order, order[1:] + order[:1]))
    up = [(2 * c + k, 2 * after[c] + k) for c in order for k in (0, 1)]
    down = [(b, a) for a, b in up]
    first = [p for p in up if p[0] % 2 == 0] + [p for p in down if p[0] % 2 == 1]
    second = [p for p in down if p[0] % 2 == 0] + [p for p in up if p[0] % 2 == 1]
    return first, second


def ring_owner(count, hops, other, me, sign=1):
    chips = count // 2
    half = chips // 2
    core, chip = me & 1, me >> 1
    place = jnp.where((chip & 1) == 0, chip >> 1, chips - 1 - (chip >> 1))
    forward = hops * sign * (2 * core - 1)
    place = lax.rem(place + chips + (-forward if other else forward), chips)
    chip = jnp.where(place < half, 2 * place, 2 * (chips - 1 - place) + 1)
    return 2 * chip + (1 - core if other else core)


def owner_of(ways):
    return lambda me, n: ways[n](me)


def swap_pairs(count):
    return [(n, n ^ 1) for n in range(count)]


def tie(x, *work):
    return lax.optimization_barrier((x, *work))[0] if work else x


def exchange_windows(count):
    chips, steps = count // 2, count // 4
    far, near = list(range(chips, count)), list(range(1, chips))
    windows = [far[:2], [far[2]] + near[:2]]
    windows += [[far[w + 1], near[w]] for w in range(2, steps)]
    windows[-1].insert(1, far[steps + 1])
    return windows + [near[steps:], far[steps + 2 :]]


def gather_and_exchange(sketch, outgoing, count):
    chips = count // 2
    first, second = ring_steps(count)
    windows = exchange_windows(count)
    columns = {0: outgoing[0]}

    def exchange(window, *after):
        for k in window:
            pairs = [(n, n ^ k) for n in range(count)]
            columns[k] = lax.ppermute(tie(outgoing[k], *after), "fsdp", pairs)

    exchange(windows[0], sketch)
    across = [(0, 1), (1, 0)]
    sketch = sketch + lax.ppermute(sketch, "tp", across)
    turns = [(2 * a + half, 2 * b + half) for half in (0, 1) for a, b in (first, second)[half]]
    hops, held, block = [0], [sketch], sketch
    for step in range(1, chips // 2 + 1):
        work = [columns[k] for k in windows[step - 2]] if step > 1 else []
        block = tie(block, *work)
        exchange(windows[step], block)
        block = lax.ppermute(block, ("fsdp", "tp"), turns)
        held.append(block)
        hops.append(step)
        if 2 * step < chips:
            held.append(lax.ppermute(block, "tp", across))
            hops.append(-step)
    exchange(windows[-1], block)
    held = tie(jnp.stack(held), *[columns[k] for k in windows[-3]])
    other = lax.ppermute(held, "fsdp", swap_pairs(count))
    ways = [(h, far) for far in (False, True) for h in hops]
    return [held, other], ways, [columns[k] for k in range(count)]


def sum_rounds(count):
    rounds, bit = [("tp", [1])], 1
    while bit < count:
        rounds.append(("fsdp", [bit, 2 * bit, 3 * bit] if 2 * bit < count else [bit]))
        bit *= 4
    return rounds


def sum_round(x, axis, distances):
    size = lax.axis_size(axis)
    terms = [x]
    for d in distances:
        terms.append(lax.ppermute(x, axis, [(n, n ^ d) for n in range(size)]))
    if len(terms) == 2:
        return terms[0] + terms[1]
    return (terms[0] + terms[1]) + (terms[2] + terms[3])


def local(momentum, gradient, basis):
    rows, cols = momentum.shape
    rank = basis.shape[1]
    count = lax.axis_size("fsdp")
    tp_count = lax.axis_size("tp")
    chips = count // 2
    share = -(-cols // (count * LANES)) * LANES
    factor = math.sqrt(rows * count * cols * tp_count / rank)
    ring = tp_count == 2 and count in (16, 32) and (count - 1) * share < cols

    base = momentum + gradient.astype(F32)
    base_b = base.astype(BF16)
    sketch = jnp.dot(base_b, basis, preferred_element_type=F32)
    base = pltpu.with_memory_space_constraint(base, pltpu.VMEM)
    if ring:
        outgoing = pack_call(base, share, count)
        pieces, ways, columns = gather_and_exchange(sketch, outgoing, count)
        ways = [functools.partial(ring_owner, count, *way) for way in ways]
        owner = lambda me, n: ways[n](me, 1 - 2 * lax.axis_index("tp"))
    else:
        padded = jnp.pad(base_b, ((0, 0), (0, share * count - cols)))
        columns = jnp.swapaxes(padded.reshape(rows, count, share), 0, 1)
        columns = lax.all_to_all(columns, "fsdp", 0, 0, tiled=True)
        columns = [columns.reshape(count * rows, share)]
        pieces = [lax.all_gather(lax.psum(sketch, "tp"), "fsdp", axis=0)]
        owner = lambda me, n: n
    ortho_t, ortho_here = factor_call(owner, base, pieces)
    part, back = back_call(base, ortho_t, columns)
    write = functools.partial(output_call, base=base, ortho=ortho_here, factor=factor)
    if not ring:
        whole = lax.all_gather(back, "fsdp", axis=0)
        blocks = [whole[n] for n in range(-(-cols // share))]
        colsq = lax.psum(part, ("fsdp", "tp"))
        return tuple(write(lambda me, n: n, blocks, colsq, None))

    turns, swap = ring_steps(count), swap_pairs(count)
    colsq, result = part, None
    for axis, distances in sum_rounds(count):
        colsq = sum_round(colsq, axis, distances)
    arrived, blocks, owners, written = {0: back}, [], [], 0
    waiting = ()
    for n in range(chips):
        block = tie(arrived[n], *waiting)
        for later in (1, 2) if n == 0 else (n + 2,):
            if later < chips:
                arrived[later] = lax.ppermute(block, "fsdp", turns[(later + 1) % 2])
        blocks += [block, lax.ppermute(block, "fsdp", swap)]
        hops = (n + 1) // 2 if n % 2 else -(n // 2)
        owners += [functools.partial(ring_owner, count, hops, far) for far in (False, True)]
        if n == 0:
            waiting = (arrived[2], colsq)
            continue
        if n == 2:
            waiting = ()
            continue
        upto = 2 * n + (2 if n == 1 else 1 if n + 1 == chips else 0)
        upto = min(upto, written + 4) if n + 1 < chips else upto
        result = write(owner_of(owners[written:upto]), blocks[written:upto], colsq, result)
        written, waiting = upto, tuple(result)
    return tuple(write(owner_of(owners[written:]), blocks[written:], colsq, result))


def solution(mesh):
    return jax.shard_map(
        local,
        mesh=mesh,
        in_specs=(P("fsdp", "tp"), P("fsdp", "tp"), P("tp", None)),
        out_specs=(P("fsdp", "tp"), P("tp", None), P("fsdp", "tp")),
        check_vma=False,
    )
```

```python
import functools
import math

import jax
import jax.numpy as jnp
from jax import lax
from jax.experimental import pallas as pl
from jax.experimental.pallas import tpu as pltpu
from jax.sharding import PartitionSpec as P

LANES = 128
SUBLANES = 8
PANEL = 64
MIB = 1024 * 1024
FULL = lax.Precision.HIGHEST
F32 = jnp.float32
BF16 = jnp.bfloat16


def cost(flops, nbytes):
    return pl.CostEstimate(flops=flops, bytes_accessed=nbytes, transcendentals=0)


def params(mib):
    return pltpu.CompilerParams(vmem_limit_bytes=mib * MIB)


def by_width(block, cols, share, start, stop, act):
    last = (cols - 1) // share
    width, short = stop - start, max(0, min(cols - last * share, stop) - start)
    if short == width:
        act(width)
        return

    @pl.when(block < last)
    def _():
        act(width)

    if short:

        @pl.when(block == last)
        def _():
            act(short)


def pack_kernel(base_ref, *out_refs):
    cols = base_ref.shape[1]
    share = out_refs[0].shape[1]
    me = lax.axis_index("fsdp")
    for n, out_ref in enumerate(out_refs):
        owner = me ^ n

        def fill(width):
            start = pl.multiple_of(owner * share, LANES)
            out_ref[:, :width] = base_ref[:, pl.ds(start, width)].astype(BF16)
            if width < share:
                out_ref[:, width:] = jnp.zeros((out_ref.shape[0], share - width), BF16)

        by_width(owner, cols, share, 0, share, fill)


def pack_call(base, share, count):
    rows = base.shape[0]
    vmem = pl.BlockSpec(memory_space=pltpu.VMEM)
    return pl.pallas_call(
        pack_kernel,
        in_specs=[vmem],
        out_specs=[vmem] * count,
        out_shape=[jax.ShapeDtypeStruct((rows, share), BF16)] * count,
        compiler_params=params(16),
        cost_estimate=cost(0, 6 * rows * share * count),
        name="pack",
    )(base)


def spread(x, lane):
    return jnp.broadcast_to(x[:, lane : lane + 1], (x.shape[0], LANES))


def row_of(x, row):
    return jnp.broadcast_to(x[row : row + 1, :], (SUBLANES, LANES))


def eliminate(block):
    sub = lax.broadcasted_iota(jnp.int32, (SUBLANES, LANES), 0)
    groups = PANEL // SUBLANES
    top = [block[SUBLANES * g : SUBLANES * (g + 1)] for g in range(groups)]
    for g in range(groups):
        first = PANEL + SUBLANES * g
        t = top[g]
        cols = [spread(t, first + j) for j in range(SUBLANES)]
        below = [[spread(top[i], first + j) for j in range(SUBLANES)] for i in range(g + 1, groups)]
        pivots = jnp.zeros((SUBLANES, LANES), F32)
        inverse, corner = [], {}
        for j in range(SUBLANES):
            pivot = row_of(cols[j], j)
            pivots = jnp.where(sub == j, pivot, pivots)
            inverse.append(1.0 / pivot)
            factor = jnp.where(sub > j, cols[j] * inverse[j], 0.0)
            t = t - factor * row_of(t, j)
            for k in range(j + 1, SUBLANES):
                corner[j, k] = row_of(cols[k], j)
                cols[k] = cols[k] - factor * corner[j, k]
        lines = [row_of(t, j) for j in range(SUBLANES)]
        for i in range(g + 1, groups):
            entries = below[i - g - 1]
            acc = top[i]
            for j in range(SUBLANES):
                factor = entries[j] * inverse[j]
                acc = acc - factor * lines[j]
                for k in range(j + 1, SUBLANES):
                    entries[k] = entries[k] - factor * corner[j, k]
            top[i] = acc
        top[g] = t * lax.rsqrt(pivots)
    return jnp.concatenate(top, axis=0)[:, :PANEL]


def dot(a, b, dims):
    return lax.dot_general(a, b, (dims, ((), ())), precision=FULL, preferred_element_type=F32)


def factor_kernel(stacks, owner, base_ref, *refs):
    me = lax.axis_index("fsdp")
    stacked, (ortho_t_ref, here_ref, whole_ref, work_ref, corner_ref) = refs[:stacks], refs[stacks:]
    corner_ref[...] = base_ref[:SUBLANES, :LANES]
    rows, rank = here_ref.shape
    total = whole_ref.shape[0]
    pieces = [stack.at[n] for stack in stacked for n in range(stack.shape[0])]
    for n, piece in enumerate(pieces):
        start = pl.multiple_of(owner(me, n) * rows, SUBLANES)
        whole_ref[pl.ds(start, rows), :] = piece[...]

    work_ref[:, :rank] = jnp.zeros((rank, rank), F32)
    chunk = 4 * rows

    @pl.loop(0, total // chunk)
    def _(n):
        part = whole_ref[pl.ds(pl.multiple_of(n * chunk, SUBLANES), chunk), :]
        work_ref[:, :rank] += dot(part, part, ((0,), (0,)))

    line = lax.broadcasted_iota(jnp.int32, (rank, rank), 0)
    column = lax.broadcasted_iota(jnp.int32, (rank, rank), 1)
    work_ref[:, rank:] = jnp.where(line == column, 1.0, 0.0).astype(F32)
    eye = jnp.where(line == column, 1.0, 0.0).astype(F32)[:PANEL, :PANEL]
    for start in range(0, rank, PANEL):
        stop = start + PANEL
        diagonal = work_ref[start:stop, start:stop]
        small = eliminate(jnp.concatenate([eye, diagonal], axis=1))
        panel = dot(small, work_ref[start:stop, :], ((1,), (0,)))
        work_ref[start:stop, :] = panel
        if stop < rank:
            work_ref[stop:, :] -= dot(panel[:, stop:rank], panel, ((0,), (0,)))
    inverse = work_ref[:, rank:]
    start = pl.multiple_of(me * rows, SUBLANES)
    here_ref[...] = dot(whole_ref[pl.ds(start, rows), :], inverse, ((1,), (1,))).astype(BF16)
    for n in range(0, total, chunk):
        ortho_t_ref[:, n : n + chunk] = dot(
            inverse, whole_ref[n : n + chunk, :], ((1,), (1,))
        ).astype(BF16)


def factor_call(owner, base, stacked):
    _, rows, rank = stacked[0].shape
    total = rows * sum(stack.shape[0] for stack in stacked)
    vmem = pl.BlockSpec(memory_space=pltpu.VMEM)
    return pl.pallas_call(
        functools.partial(factor_kernel, len(stacked), owner),
        in_specs=[vmem] * (1 + len(stacked)),
        out_specs=[vmem, vmem],
        out_shape=[
            jax.ShapeDtypeStruct((rank, total), BF16),
            jax.ShapeDtypeStruct((rows, rank), BF16),
        ],
        scratch_shapes=[
            pltpu.VMEM((total, rank), F32),
            pltpu.VMEM((rank, 2 * rank), F32),
            pltpu.VMEM((SUBLANES, LANES), F32),
        ],
        compiler_params=params(24),
        cost_estimate=cost(40 * total * rank * rank, total * rank * 6),
        name="factor",
    )(base, *stacked)


def back_kernel(base_ref, ortho_t_ref, *refs):
    *columns, colsq_ref, back_ref, whole_ref, corner_ref = refs
    corner_ref[...] = base_ref[:SUBLANES, :LANES]
    me = lax.axis_index("fsdp") if len(columns) > 1 else 0
    rows = columns[0].shape[0]
    for n, piece in enumerate(columns):
        whole_ref[pl.ds(pl.multiple_of((me ^ n) * rows, 16), rows), :] = piece[...]
    back_t = jnp.dot(ortho_t_ref[...], whole_ref[...], preferred_element_type=F32)
    back = back_t.T.astype(BF16)
    back_ref[...] = back
    wide = back.astype(F32)
    colsq_ref[...] = jnp.sum(wide * wide, axis=0, keepdims=True)


def back_call(base, ortho_t, columns):
    rank, total = ortho_t.shape
    share = columns[0].shape[1]
    vmem = pl.BlockSpec(memory_space=pltpu.VMEM)
    return pl.pallas_call(
        back_kernel,
        in_specs=[vmem] * (2 + len(columns)),
        out_specs=[vmem] * 2,
        out_shape=[
            jax.ShapeDtypeStruct((1, rank), F32),
            jax.ShapeDtypeStruct((share, rank), BF16),
        ],
        scratch_shapes=[pltpu.VMEM((total, share), BF16), pltpu.VMEM((SUBLANES, LANES), F32)],
        compiler_params=params(24),
        cost_estimate=cost(2 * rank * total * share, total * share * 2),
        name="back",
    )(base, ortho_t, *columns)


def output_kernel(owner, factor, base_ref, ortho_ref, colsq_ref, *refs):
    me = lax.axis_index("fsdp")
    *pieces, nm_ref, nb_ref, up_ref, nm_tile, nb_tile, up_tile, sems = refs
    count, share, cols = nm_tile.shape[0], nm_tile.shape[2], nm_ref.shape[1]
    scale = lax.rsqrt(colsq_ref[...] + 1e-06)
    ortho = ortho_ref[...]
    over = (((1,), (1,)), ((), ()))

    def copies(n, width):
        there = pl.ds(pl.multiple_of(owner(me, n) * share, LANES), width)
        sides = (
            (nm_tile.at[n, :, :width], nm_ref.at[:, there]),
            (nb_tile.at[n, :width, :], nb_ref.at[there, :]),
            (up_tile.at[n, :, :width], up_ref.at[:, there]),
        )
        return [
            pltpu.make_async_copy(source, target, sems.at[n, which])
            for which, (source, target) in enumerate(sides)
        ]

    for n in range(count):

        def compute(width):
            there = pl.ds(pl.multiple_of(owner(me, n) * share, LANES), width)
            back = pieces[n][:width, :]
            unit = (back.astype(F32) * scale).astype(BF16)
            nb_tile[n, :width, :] = unit
            nm_tile[n, :, :width] = base_ref[:, there] - 0.05 * lax.dot_general(
                ortho, back, over, preferred_element_type=F32
            )
            up_tile[n, :, :width] = (
                factor * lax.dot_general(ortho, unit, over, preferred_element_type=F32)
            ).astype(BF16)
            for copy in copies(n, width):
                copy.start()

        by_width(owner(me, n), cols, share, 0, share, compute)

    for n in range(count):

        def wait(width):
            for copy in copies(n, width):
                copy.wait()

        by_width(owner(me, n), cols, share, 0, share, wait)


def output_call(owner, blocks, colsq, previous, base, ortho, factor):
    rows, cols = base.shape
    share, rank = blocks[0].shape
    count = len(blocks)
    previous = previous or ()
    vmem, hbm = pl.BlockSpec(memory_space=pltpu.VMEM), pl.BlockSpec(memory_space=pltpu.HBM)
    return pl.pallas_call(
        functools.partial(output_kernel, owner, factor),
        in_specs=[vmem] * (3 + count) + [hbm] * len(previous),
        out_specs=[hbm] * 3,
        out_shape=[
            jax.ShapeDtypeStruct((rows, cols), F32),
            jax.ShapeDtypeStruct((cols, rank), BF16),
            jax.ShapeDtypeStruct((rows, cols), BF16),
        ],
        scratch_shapes=[
            pltpu.VMEM((count, rows, share), F32),
            pltpu.VMEM((count, share, rank), BF16),
            pltpu.VMEM((count, rows, share), BF16),
            pltpu.SemaphoreType.DMA((count, 3)),
        ],
        input_output_aliases={3 + count + n: n for n in range(len(previous))},
        compiler_params=params(16),
        cost_estimate=cost(
            4 * rows * share * rank * count, count * share * (rows * 10 + rank * 4)
        ),
        name="outputs",
    )(base, ortho, colsq, *blocks, *previous)


def ring_order(chips):
    half = chips // 2
    return [2 * q for q in range(half)] + [2 * (chips - 1 - q) + 1 for q in range(half, chips)]


def ring_steps(count):
    order = ring_order(count // 2)
    after = dict(zip(order, order[1:] + order[:1]))
    up = [(2 * c + k, 2 * after[c] + k) for c in order for k in (0, 1)]
    down = [(b, a) for a, b in up]
    first = [p for p in up if p[0] % 2 == 0] + [p for p in down if p[0] % 2 == 1]
    second = [p for p in down if p[0] % 2 == 0] + [p for p in up if p[0] % 2 == 1]
    return first, second


def ring_owner(count, hops, other, me, sign=1):
    chips = count // 2
    half = chips // 2
    core, chip = me & 1, me >> 1
    place = jnp.where((chip & 1) == 0, chip >> 1, chips - 1 - (chip >> 1))
    forward = hops * sign * (2 * core - 1)
    place = lax.rem(place + chips + (-forward if other else forward), chips)
    chip = jnp.where(place < half, 2 * place, 2 * (chips - 1 - place) + 1)
    return 2 * chip + (1 - core if other else core)


def owner_of(ways):
    return lambda me, n: ways[n](me)


def swap_pairs(count):
    return [(n, n ^ 1) for n in range(count)]


def tie(x, *work):
    return lax.optimization_barrier((x, *work))[0] if work else x


def exchange_windows(count):
    chips, steps = count // 2, count // 4
    far, near = list(range(chips, count)), list(range(1, chips))
    each = -(-len(near) // steps)
    cuts = [0] + [w * each - 1 for w in range(1, steps)] + [len(near)]
    windows = [far[w + 1 : w + 2] + near[cuts[w - 1] : cuts[w]] for w in range(1, steps + 1)]
    return [far[:2]] + windows + [far[steps + 2 :]]


def gather_and_exchange(sketch, outgoing, count):
    chips = count // 2
    first, second = ring_steps(count)
    windows = exchange_windows(count)
    columns = {0: outgoing[0]}

    def exchange(window, *after):
        for k in window:
            pairs = [(n, n ^ k) for n in range(count)]
            columns[k] = lax.ppermute(tie(outgoing[k], *after), "fsdp", pairs)

    exchange(windows[0], sketch)
    across = [(0, 1), (1, 0)]
    sketch = sketch + lax.ppermute(sketch, "tp", across)
    turns = [(2 * a + half, 2 * b + half) for half in (0, 1) for a, b in (first, second)[half]]
    hops, held, block = [0], [sketch], sketch
    for step in range(1, chips // 2 + 1):
        work = [columns[k] for k in windows[step - 2]] if step > 1 else []
        block = tie(block, *work)
        exchange(windows[step], block)
        block = lax.ppermute(block, ("fsdp", "tp"), turns)
        held.append(block)
        hops.append(step)
        if 2 * step < chips:
            held.append(lax.ppermute(block, "tp", across))
            hops.append(-step)
    exchange(windows[-1], block)
    held = tie(jnp.stack(held), *[columns[k] for k in windows[-3]])
    other = lax.ppermute(held, "fsdp", swap_pairs(count))
    ways = [(h, far) for far in (False, True) for h in hops]
    return [held, other], ways, [columns[k] for k in range(count)]


def sum_rounds(count):
    rounds, bit = [("tp", [1])], 1
    while bit < count:
        rounds.append(("fsdp", [bit, 2 * bit, 3 * bit] if 2 * bit < count else [bit]))
        bit *= 4
    return rounds


def sum_round(x, axis, distances):
    size = lax.axis_size(axis)
    terms = [x]
    for d in distances:
        terms.append(lax.ppermute(x, axis, [(n, n ^ d) for n in range(size)]))
    if len(terms) == 2:
        return terms[0] + terms[1]
    return (terms[0] + terms[1]) + (terms[2] + terms[3])


def local(momentum, gradient, basis):
    rows, cols = momentum.shape
    rank = basis.shape[1]
    count = lax.axis_size("fsdp")
    tp_count = lax.axis_size("tp")
    chips = count // 2
    share = -(-cols // (count * LANES)) * LANES
    factor = math.sqrt(rows * count * cols * tp_count / rank)
    ring = tp_count == 2 and count in (16, 32) and (count - 1) * share < cols

    base = momentum + gradient.astype(F32)
    base_b = base.astype(BF16)
    sketch = jnp.dot(base_b, basis, preferred_element_type=F32)
    base = pltpu.with_memory_space_constraint(base, pltpu.VMEM)
    if ring:
        outgoing = pack_call(base, share, count)
        pieces, ways, columns = gather_and_exchange(sketch, outgoing, count)
        ways = [functools.partial(ring_owner, count, *way) for way in ways]
        owner = lambda me, n: ways[n](me, 1 - 2 * lax.axis_index("tp"))
    else:
        padded = jnp.pad(base_b, ((0, 0), (0, share * count - cols)))
        columns = jnp.swapaxes(padded.reshape(rows, count, share), 0, 1)
        columns = lax.all_to_all(columns, "fsdp", 0, 0, tiled=True)
        columns = [columns.reshape(count * rows, share)]
        pieces = [lax.all_gather(lax.psum(sketch, "tp"), "fsdp", axis=0)]
        owner = lambda me, n: n
    ortho_t, ortho_here = factor_call(owner, base, pieces)
    part, back = back_call(base, ortho_t, columns)
    write = functools.partial(output_call, base=base, ortho=ortho_here, factor=factor)
    if not ring:
        whole = lax.all_gather(back, "fsdp", axis=0)
        blocks = [whole[n] for n in range(-(-cols // share))]
        colsq = lax.psum(part, ("fsdp", "tp"))
        return tuple(write(lambda me, n: n, blocks, colsq, None))

    turns, swap = ring_steps(count), swap_pairs(count)
    colsq, result = part, None
    for axis, distances in sum_rounds(count):
        colsq = sum_round(colsq, axis, distances)
    arrived, blocks, owners, written = {0: back}, [], [], 0
    waiting = ()
    for n in range(chips):
        block = tie(arrived[n], *waiting)
        for later in (1, 2) if n == 0 else (n + 2,):
            if later < chips:
                arrived[later] = lax.ppermute(block, "fsdp", turns[(later + 1) % 2])
        blocks += [block, lax.ppermute(block, "fsdp", swap)]
        hops = (n + 1) // 2 if n % 2 else -(n // 2)
        owners += [functools.partial(ring_owner, count, hops, far) for far in (False, True)]
        if n == 0:
            waiting = (arrived[2], colsq)
            continue
        if n == 2:
            waiting = ()
            continue
        upto = 2 * n + (2 if n == 1 else 1 if n + 1 == chips else 0)
        upto = min(upto, written + 4) if n + 1 < chips else upto
        result = write(owner_of(owners[written:upto]), blocks[written:upto], colsq, result)
        written, waiting = upto, tuple(result)
    return tuple(write(owner_of(owners[written:]), blocks[written:], colsq, result))


def solution(mesh):
    return jax.shard_map(
        local,
        mesh=mesh,
        in_specs=(P("fsdp", "tp"), P("fsdp", "tp"), P("tp", None)),
        out_specs=(P("fsdp", "tp"), P("tp", None), P("fsdp", "tp")),
        check_vma=False,
    )
```
